32 devices in a mesh: coarse: 4 (over z), member: 8 (over y, x, core).
Axes of the slice: x: 2, y: 2, z: 4, core: 2. Of those that a mesh axis runs over, the one named last changes fastest.
Arguments:
- samples: bfloat16 [40960, 768], P(('coarse', 'member')), may hold values from -6 to 6
- coarse_label: int32 [40960, 1], P(('coarse', 'member')), may hold values from 0 to 3; in each aligned block of 1280 rows (0 to 1279, 1280 to 2559, ...) at most 480 rows name the same one
- fine_label: int32 [40960], P(('coarse', 'member')), may hold values from 0 to 1023
- live_rows: int32 [32], P(('coarse', 'member')), may hold values from 1 to 1280, 30720 in all
- old_centroids: float32 [4, 1024, 768], P('coarse'), may hold values from -0.3 to 0.3
Outputs:
- scores: bfloat16 [40960, 1024], P(('coarse', 'member'))
- new_centroids: float32 [4, 1024, 768], P('coarse', 'member')
The draws below stay inside these ranges and needn't reach their ends.
Inputs may be any that keep to these rules, and one draw needn't show every extreme that they name: `coarse_label`: among the rows of one device no group is named more than 480 times; some group reaches 480 on some devices. `live_rows`: the largest value equals 1280.
All inputs are finite; a program needn't handle non-finite values. No bound on the sum of `live_rows` on one device may be relied on, other than what follows from the above.
Results may differ from the reference program's by a relative error of at most 0.0085.
Values may be sent and summed in bfloat16 or wider, within the bound.
No kernel may reach another device: no remote copies, remote signals or barrier semaphores. Data moves between devices by JAX's collectives and lax.ppermute only.
A program may use at most 64 MiB of HBM per device.

```python
import math
import jax
import jax.numpy as jnp
import numpy as np
from jax import lax

D = 768
K = 1024
ROW_DEV = 1280
CAP = 480
GROUPS = 4
ROWS = 40960
DEVICES = 32


def set_ends(drawn, key, smallest, high):
    longest = drawn.shape.index(max(drawn.shape))
    spots = []
    for shift in (0, 1):
        where = [jax.random.randint(jax.random.fold_in(key, axis), (), 0, length) for axis, length in enumerate(drawn.shape)]
        where[longest] = (where[longest] + shift) % drawn.shape[longest]
        spots.append(tuple(where))
    return drawn.at[spots[0]].set(smallest).at[spots[1]].set(high)


def steps_of(stream_key, shape, cuts, low, top_value):
    def one(axis_at, shards_of):
        heights = jax.random.uniform(jax.random.fold_in(jax.random.fold_in(stream_key, 6), axis_at), (shards_of,), jnp.float32, low / len(cuts), top_value / len(cuts))
        return jnp.repeat(jnp.exp(heights), shape[axis_at] // shards_of).reshape((-1,) + (1,) * (len(shape) - axis_at - 1))

    level = one(*cuts[0])
    for cut in cuts[1:]:
        level = level * one(*cut)
    return level


def cumulative_ranks(amount, lean):
    weights = [(1 << 20) // math.isqrt(standing ** lean) + 1 for standing in range(1, amount + 1)]
    scale = 1 + sum(weights) // (1 << 30)
    return np.cumsum(np.array([max(1, weight // scale) for weight in weights]))


def ranked(own_key, dims, number_of, slope):
    listing = cumulative_ranks(number_of, slope)
    pick = jax.random.randint(jax.random.fold_in(own_key, 1), dims, 0, int(listing[number_of - 1]))
    standing = jnp.searchsorted(jnp.asarray(listing, jnp.int32), pick, side="right")
    return jax.random.permutation(jax.random.fold_in(own_key, 2), number_of)[standing].astype(jnp.int32)


def length_profile(number_of, total, bound, lean):
    portions = [(1 << 20) // math.isqrt(rank ** lean) + 1 for rank in range(2, number_of + 1)]
    surplus, given = total - bound - (number_of - 1), [1] * (number_of - 1)
    while surplus > 0:
        movable = [i for i in range(number_of - 1) if given[i] < bound]
        whole, left = sum([portions[i] for i in movable]), surplus
        for i in movable:
            extra = min(bound - given[i], max(1, left * portions[i] // whole), surplus)
            given[i] = given[i] + extra
            surplus = surplus - extra
    return np.array([bound] + given)


def ragged(key, count, total, bound, slope):
    if count == 2:
        one = jax.random.randint(key, (), max(1, total - bound), min(bound, total - 1) + 1)
        return jnp.stack([one, total - one])
    sizes = jnp.asarray(length_profile(count, total, bound, slope), jnp.int32)
    twos = (count - 1) // 2
    source_of, sink = sizes[1:1 + 2 * twos:2], sizes[2:2 + 2 * twos:2]
    room = jnp.minimum(source_of - 1, bound - sink)
    moved = jax.random.randint(jax.random.fold_in(key, 1), (twos,), 0, 1 << 20) % (room + 1)
    sizes = sizes.at[1:1 + 2 * twos:2].set(source_of - moved).at[2:2 + 2 * twos:2].set(sink + moved)
    return sizes[jax.random.permutation(jax.random.fold_in(key, 2), count)]


def assign_block(own_key, own, number, rows, count, top, limit, lean):
    ranking = jax.random.permutation(own_key, count)
    crowded, common = load_shares(count, rows * top, limit, lean, True), load_shares(count, rows * top, limit, lean, False)
    places = jnp.arange(count)

    def named(sizes, turn):
        used = int((sizes > 0).sum())
        fixed = max(1, used // 4)
        shifted = fixed + (places - fixed + turn * (used - fixed)) % max(1, count - fixed)
        return jnp.zeros((count,), jnp.int32).at[ranking[jnp.where(places < fixed, places, shifted)]].set(jnp.asarray(sizes, jnp.int32))

    sizes = jnp.where(number % 4 == 0, named(crowded, number // 4), named(common, number - number // 4 - 1))
    mixed = jax.random.permutation(jax.random.fold_in(own, 3), count)
    giver, receiver = mixed[0:count // 2 * 2:2], mixed[1:count // 2 * 2:2]
    margin = jnp.minimum(sizes[giver] - 1, limit - sizes[receiver]) // 2
    margin = jnp.where((giver == ranking[0]) | (receiver == ranking[0]) | (sizes[receiver] == 0), 0, jnp.maximum(margin, 0))
    shifted = jax.random.randint(jax.random.fold_in(own, 4), (count // 2,), 0, 1 << 20) % (margin + 1)
    sizes = sizes.at[giver].add(-shifted).at[receiver].add(shifted)
    members = jnp.searchsorted(jnp.cumsum(sizes), jnp.arange(rows * top), side="right").astype(jnp.int32)
    listing = members.reshape(top, rows).T
    listing = listing[jax.random.permutation(jax.random.fold_in(own, 1), rows)]
    turn = jax.random.randint(jax.random.fold_in(own, 2), (rows, 1), 0, top)
    return jnp.take_along_axis(listing, (jnp.arange(top)[None, :] + turn) % top, axis=1)


def load_shares(amount, total, limit, skew, full):
    portions = [(1 << 20) // math.isqrt(standing ** skew) + 1 for standing in range(1, amount + 1)]
    largest = limit if full else min(limit, max(-(-total // amount), total * portions[0] // sum(portions)))
    least = 1 if total - largest >= amount - 1 else 0
    holding, spare = [largest] + [least] * (amount - 1), total - largest - least * (amount - 1)
    while spare > 0:
        candidates = [i for i in range(1, amount) if holding[i] < largest] or [i for i in range(1, amount) if holding[i] < limit]
        whole, remaining = sum([portions[i] for i in candidates]), spare
        for i in candidates:
            extra = min(limit - holding[i], max(1, remaining * portions[i] // whole), spare)
            holding[i] = holding[i] + extra
            spare = spare - extra
    return np.array(holding)


def scatter_about(own_key, dims, scale, most, cuts=(), kind=jnp.bfloat16):
    array = jax.random.normal(own_key, dims, jnp.float32) * scale
    if len(cuts) > 0:
        array = steps_of(own_key, dims, cuts, -0.22, 0.18) * array
    return jnp.clip(array, min=-most, max=most).astype(kind)


def setup_inputs(seed: int = 0) -> dict:
    key_list = jax.random.split(jax.random.key(seed), 6)
    samples = scatter_about(key_list[0], (ROWS, D), 1.0, 6.0, ((0, 32),))
    coarse_label_keys = jax.random.split(jax.random.fold_in(key_list[1], 1), ROWS // ROW_DEV)
    coarse_label_turns = jax.random.permutation(jax.random.fold_in(key_list[1], 3), ROWS // ROW_DEV)
    coarse_label = jax.vmap(lambda own, number: assign_block(jax.random.fold_in(key_list[1], 2), own, number, ROW_DEV, GROUPS, 1, CAP, 2))(coarse_label_keys, coarse_label_turns).reshape((ROWS, 1))
    fine_label = set_ends(ranked(key_list[2], (ROWS,), K, 1), jax.random.fold_in(key_list[2], 3), 0, K - 1).astype(jnp.int32)
    live_rows = ragged(key_list[3], DEVICES, DEVICES * ROW_DEV * 3 // 4, ROW_DEV, 1).astype(jnp.int32)
    old_centroids = scatter_about(key_list[4], (GROUPS, K, D), 0.05, 0.3, ((0, 4),), jnp.float32)
    return dict(samples=samples, coarse_label=coarse_label, fine_label=fine_label, live_rows=live_rows, old_centroids=old_centroids)


prior_weight = 16.0


def reference(samples, coarse_label, fine_label, live_rows, old_centroids):
    position = jnp.arange(ROWS, dtype=jnp.int32)
    device_of = position // ROW_DEV
    is_live = (position % ROW_DEV) < live_rows[device_of]
    group_id = coarse_label[:, 0]
    segment = jnp.where(is_live, group_id * K + fine_label, GROUPS * K)
    totals = jax.ops.segment_sum(samples.astype(jnp.float32), segment, num_segments=GROUPS * K + 1)[:GROUPS * K]
    counts = jax.ops.segment_sum(jnp.ones((ROWS,), jnp.float32), segment, num_segments=GROUPS * K + 1)[:GROUPS * K]
    renewed = (totals.reshape(GROUPS, K, D) + prior_weight * old_centroids) / (counts.reshape(GROUPS, K, 1) + prior_weight)
    centroid_bf = renewed.astype(jnp.bfloat16)
    wide = centroid_bf.astype(jnp.float32)
    half_norm = 0.5 * jnp.sum(wide * wide, axis=2)

    def score_block(pieces):
        block_rows, block_group, block_live = pieces
        every = jnp.einsum("rd,gkd->grk", block_rows.astype(jnp.float32), wide) - half_norm[:, None, :]
        chosen = jnp.take_along_axis(every, block_group[None, :, None], axis=0)[0]
        return jnp.where(block_live[:, None], chosen, 0.0).astype(jnp.bfloat16)

    blocks = ROWS // ROW_DEV
    scores = lax.map(score_block, (samples.reshape(blocks, ROW_DEV, D), group_id.reshape(blocks, ROW_DEV), is_live.reshape(blocks, ROW_DEV)))
    return scores.reshape(ROWS, K), renewed
```

```python
import functools

import jax
import jax.numpy as jnp
from jax import lax
from jax.experimental import pallas as pl
from jax.experimental.pallas import tpu as pltpu
from jax.sharding import PartitionSpec as P

AXES = ("coarse", "member")
STREAMS = 2
TILE = 16
PRIOR = 16.0
PARTS = 3
F32 = jnp.float32
BF16 = jnp.bfloat16


def pad_rows(blocks):
    return max(TILE, -(-blocks // TILE) * TILE)


def orders_of(groups, members):
    inner = [(0, 1 << bit) for bit in range(1, members.bit_length() - 1)]
    outer = [((1 << (bit + 1)) - 1, 0) for bit in range(groups.bit_length() - 1)]
    dims = []
    for place in range(max(len(inner), len(outer))):
        dims += inner[place : place + 1] + outer[place : place + 1]
    count = len(dims)
    turned = {}
    for core in range(2):
        for stream in range(STREAMS):
            shift = (2 * stream + core) * count // 4
            turned[core, stream] = dims[shift:] + dims[:shift]
    return turned


def exchange(array, partner, groups, members):
    pairs = []
    for z in range(groups):
        for m in range(members):
            to_z, to_m = partner(z, m)
            pairs.append((z * members + m, to_z * members + to_m))
    return lax.ppermute(array, AXES, pairs)


def coefficients(group_rel, member_rel, dims, outer_bits):
    out = []
    for group_mask, member_mask in dims:
        if member_mask:
            out.append((member_rel >> (member_mask.bit_length() - 1)) & 1)
        else:
            top = group_mask.bit_length() - 1
            bit = (group_rel >> top) & 1
            if top + 1 < outer_bits:
                bit = bit ^ ((group_rel >> (top + 1)) & 1)
            out.append(bit)
    return out


def block_position(group_rel, member_rel, dims, outer_bits):
    place = 0
    for bit in coefficients(group_rel, member_rel, dims, outer_bits):
        place = place * 2 + (1 - bit)
    return place


def relative_of(place, dims):
    group_rel = member_rel = 0
    for at, (group_mask, member_mask) in enumerate(dims):
        if not (place >> (len(dims) - 1 - at)) & 1:
            group_rel ^= group_mask
            member_rel ^= member_mask
    return group_rel, member_rel


def sums_kernel(base, step, pos_ref, own_ref, other_ref, count_ref, out_ref):
    rows = own_ref.shape[0]
    at = pl.program_id(0)
    start = pl.multiple_of(at * step, step)
    key = lax.broadcasted_iota(jnp.int32, (step, rows), 0) + (base + start)
    first = jnp.where(pos_ref[:, :rows] == key, 1.0, 0.0).astype(BF16)
    second = jnp.where(pos_ref[:, rows:] == key, 1.0, 0.0).astype(BF16)
    total = jnp.dot(first, own_ref[...], preferred_element_type=F32)
    total += jnp.dot(second, other_ref[...], preferred_element_type=F32)
    out_ref[pl.ds(start, step), :] = total.astype(BF16)

    @pl.when(at == pl.num_programs(0) - 1)
    def _():
        tail = count_ref.shape[0]
        out_ref[pl.ds(out_ref.shape[0] - tail, tail), :] = count_ref[...]


def key_sums(pos_row, own, other, count_tile, base, keys, stream, step=1024):
    rows = own.shape[0]
    wide = own.shape[1] // STREAMS
    step = min(step, keys)
    out_rows = keys + count_tile.shape[0]
    return pl.pallas_call(
        functools.partial(sums_kernel, base, step),
        grid=(keys // step,),
        out_shape=jax.ShapeDtypeStruct((out_rows, wide), BF16),
        in_specs=[
            pl.BlockSpec((1, 2 * rows), lambda i: (0, 0)),
            pl.BlockSpec((rows, wide), lambda i: (0, stream)),
            pl.BlockSpec((rows, wide), lambda i: (0, stream)),
            pl.BlockSpec(count_tile.shape, lambda i: (0, 0)),
        ],
        out_specs=pl.BlockSpec((out_rows, wide), lambda i: (0, 0)),
        compiler_params=pltpu.CompilerParams(vmem_limit_bytes=24 << 20),
        cost_estimate=pl.CostEstimate(
            flops=2 * keys * 2 * rows * wide, bytes_accessed=(4 * rows + 2 * keys) * wide, transcendentals=0
        ),
        name="key_sums",
    )(pos_row, own, other, count_tile)


def small_call(kernel, name, outs, *args):
    whole = pl.BlockSpec(memory_space=pltpu.VMEM)
    moved = sum(a.size * a.dtype.itemsize for a in (*args, *outs))
    return pl.pallas_call(
        kernel,
        out_shape=outs,
        in_specs=[whole] * len(args),
        out_specs=[whole] * len(outs),
        compiler_params=pltpu.CompilerParams(vmem_limit_bytes=12 << 20),
        cost_estimate=pl.CostEstimate(flops=moved // 2, bytes_accessed=moved, transcendentals=0),
        name=name,
    )(*args)


def add_tail(keep_ref, got_ref, body, shift):
    kept = keep_ref[body:, :].astype(F32)
    return kept + pltpu.roll(got_ref[body:, :].astype(F32), shift, 0)


def fold_kernel(half, shift, got_ref, keep_ref, send_out, keep_out):
    tail = add_tail(keep_ref, got_ref, 2 * half, shift).astype(BF16)
    send_out[:half, :] = (got_ref[:half, :].astype(F32) + keep_ref[:half, :].astype(F32)).astype(BF16)
    keep_out[:half, :] = (
        got_ref[half : 2 * half, :].astype(F32) + keep_ref[half : 2 * half, :].astype(F32)
    ).astype(BF16)
    send_out[half:, :] = tail
    keep_out[half:, :] = tail


def seed_kernel(share, shift, got_ref, keep_ref, old_ref, send_out, near_out):
    two = 2 * share
    near = got_ref[share:two, :].astype(F32) + keep_ref[share:two, :].astype(F32) + PRIOR * old_ref[...]
    near_out[...] = near
    send_out[:share, :] = (got_ref[:share, :].astype(F32) + keep_ref[:share, :].astype(F32)).astype(BF16)
    send_out[share:two, :] = near.astype(BF16)
    send_out[two:, :] = add_tail(keep_ref, got_ref, two, shift).astype(BF16)


def centroid_kernel(share, base, digits, rows_out, got_ref, sent_ref, near_ref, fresh_out, cents_out):
    two = 2 * share
    wide = got_ref.shape[1]
    last = sent_ref.shape[0] - two - 1
    lane = lax.broadcasted_iota(jnp.int32, (share, wide), 1)
    line = lax.broadcasted_iota(jnp.int32, (share, wide), 0)
    mine = sent_ref[two:, :].astype(F32)
    theirs = got_ref[two:, :].astype(F32)
    total = (
        sent_ref[:share, :].astype(F32) + got_ref[share:two, :].astype(F32),
        near_ref[...] + got_ref[:share, :].astype(F32),
    )
    tile = jnp.zeros((rows_out, wide), F32)
    tile_row = lax.broadcasted_iota(jnp.int32, (rows_out, wide), 0)
    for block in range(2):
        row = mine[last - 1 + block : last + block, :] + theirs[last - block : last - block + 1, :]
        count = jnp.full((share, 1), PRIOR, F32)
        for digit in range(digits):
            hit = jnp.where(lane == line + digit * share, row, 0.0)
            count += jnp.sum(hit, axis=1, keepdims=True) * float(base**digit)
        fresh = total[block] / count
        rounded = fresh.astype(BF16)
        cents_out[block * share : (block + 1) * share, :] = rounded
        if block == 1:
            fresh_out[...] = fresh
        norm = 0.5 * jnp.sum(jnp.square(rounded.astype(F32)), axis=1, keepdims=True)
        spread = jnp.zeros((1, wide), F32)
        for part in range(PARTS):
            term = norm.astype(BF16).astype(F32)
            norm = norm - term
            hit = jnp.where(lane == line + part * share, term, 0.0)
            spread += jnp.sum(hit, axis=0, keepdims=True)
        tile = jnp.where(tile_row == rows_out - 2 + block, spread, tile)
    cents_out[two:, :] = tile.astype(BF16)


def join_kernel(body, shift, got_ref, held_ref, out_ref):
    out_ref[:body, :] = got_ref[:body, :]
    out_ref[body : 2 * body, :] = held_ref[:body, :]
    rows = held_ref.shape[0] - body
    moved = pltpu.roll(got_ref[body:, :].astype(F32), rows - shift, 0)
    out_ref[2 * body :, :] = (held_ref[body:, :].astype(F32) + moved).astype(BF16)


def scores_kernel(groups, share, stream, first, last, where_ref, x_ref, gid_ref, half_ref, *rest):
    pieces = 4
    piece_refs = rest[:pieces]
    rest = rest[pieces:]
    total_ref = None if first else rest[0]
    out_ref, cents, masked = rest[-3:]
    wide = x_ref.shape[1]
    keys = cents.shape[0]
    blocks = where_ref.shape[0] // pieces

    @pl.when(pl.program_id(0) == 0)
    def _():
        for piece in range(pieces):
            for block in range(blocks):
                code = where_ref[piece * blocks + block]
                group = code // (keys // share)
                member = code % (keys // share)
                cents[
                    pl.ds(pl.multiple_of(member * share, share), share),
                    pl.ds(pl.multiple_of(group * wide, 128), wide),
                ] = piece_refs[piece][block * share : (block + 1) * share, :]
        for group in range(groups):
            masked[:, group * wide : (group + 1) * wide] = jnp.where(
                gid_ref[...] == group, x_ref[...], jnp.zeros_like(x_ref)
            )

    step = out_ref.shape[1]
    start = pl.multiple_of(pl.program_id(0) * step, step)
    dots = lax.dot_general(
        masked[...], cents[pl.ds(start, step), :], (((1,), (1,)), ((), ())), preferred_element_type=F32
    )
    if not first:
        dots = dots + total_ref[...]
    if last:
        half = jnp.zeros_like(dots)
        for group in range(groups):
            half = jnp.where(gid_ref[...] == group, half_ref[group : group + 1, :], half)
        dots = dots - half
    out_ref[...] = dots.astype(out_ref.dtype)


def add_scores(samples, gid, half, pieces, where, total, groups, keys, share, stream):
    rows, width = samples.shape
    wide = width // STREAMS
    step = min(256, keys)
    first, last = stream == 0, stream == STREAMS - 1
    whole = pl.BlockSpec(memory_space=pltpu.VMEM)
    return pl.pallas_call(
        functools.partial(scores_kernel, groups, share, stream, first, last),
        grid_spec=pltpu.PrefetchScalarGridSpec(
            num_scalar_prefetch=1,
            grid=(keys // step,),
            in_specs=[
                pl.BlockSpec((rows, wide), lambda i, w: (0, stream)),
                pl.BlockSpec((rows, 1), lambda i, w: (0, 0)),
                pl.BlockSpec((groups, step), lambda i, w: (0, i)),
            ]
            + [whole] * len(pieces)
            + [pl.BlockSpec((rows, step), lambda i, w: (0, i))] * (not first),
            out_specs=pl.BlockSpec((rows, step), lambda i, w: (0, i)),
            scratch_shapes=[
                pltpu.VMEM((keys, groups * wide), BF16),
                pltpu.VMEM((rows, groups * wide), BF16),
            ],
        ),
        out_shape=jax.ShapeDtypeStruct((rows, keys), BF16 if last else F32),
        compiler_params=pltpu.CompilerParams(vmem_limit_bytes=32 << 20),
        cost_estimate=pl.CostEstimate(
            flops=2 * rows * keys * groups * wide, bytes_accessed=2 * (rows + groups * keys) * wide, transcendentals=0
        ),
        name="scores",
    )(where, samples, gid, half, *pieces, *([] if first else [total]))


def per_device(samples, coarse_label, fine_label, live_rows, old_centroids):
    groups = lax.axis_size("coarse")
    members = lax.axis_size("member")
    z = lax.axis_index("coarse")
    me = lax.axis_index("member")
    core = me & 1
    rows, width = samples.shape
    keys = old_centroids.shape[1]
    share = keys // members
    wide = width // STREAMS
    half_keys = groups * keys // 2
    blocks = half_keys // share
    outer_bits = groups.bit_length() - 1
    turned = orders_of(groups, members)
    stages = len(turned[0, 0])
    base = 256 // (groups * members // 2) + 1
    digits = 1
    while base**digits <= 2 * rows:
        digits += 1

    live = jnp.arange(rows, dtype=jnp.int32) < live_rows[0]
    label = jnp.where(live, coarse_label[:, 0] * keys + fine_label, -1)
    sibling = lambda a: exchange(a, lambda gz, m: (gz, m ^ 1), groups, members)
    other_samples = sibling(samples)
    label_all = jnp.concatenate([label, sibling(label)])

    group_of = label_all // keys
    fine = label_all % keys
    owner = fine // share
    mine = (label_all >= 0) & ((owner & 1) == core)

    def of_core(make):
        return jnp.where(core == 0, make(0), make(1))

    def pairing(stage, stream):
        def partner(gz, m):
            group_mask, member_mask = turned[m & 1, stream][stage]
            return gz ^ group_mask, m ^ member_mask

        return partner

    tail = pad_rows(blocks)
    sends, keeps = [], []
    for stream in range(STREAMS):
        place = of_core(
            lambda c: block_position(group_of ^ z, owner ^ me, turned[c, stream], outer_bits)
        )
        pos = jnp.where(mine, place * share + fine % share, -1)
        in_block = (jnp.where(mine, place, -1)[:, None] == jnp.arange(tail)[None, :]).astype(BF16)
        in_lane = ((fine % share)[:, None] == jnp.arange(share)[None, :]).astype(BF16)
        counted = lax.dot_general(
            in_block, in_lane, (((0,), (0,)), ((), ())), preferred_element_type=F32
        ).astype(jnp.int32)
        tile = [(counted // base**digit) % base for digit in range(digits)]
        tile = jnp.concatenate(tile, axis=1).astype(BF16)
        tile = jnp.pad(tile, ((0, 0), (0, wide - digits * share)))
        make = functools.partial(
            key_sums, pos[None, :], samples, other_samples, tile, keys=half_keys // 2, stream=stream
        )
        sends.append(make(base=0))
        keeps.append(make(base=half_keys // 2))

    old_share = lax.dynamic_slice(old_centroids[0], (me * share, 0), (share, width))
    bf = lambda count: jax.ShapeDtypeStruct((count * share + tail, wide), BF16)
    share_f32 = jax.ShapeDtypeStruct((share, wide), F32)
    send, keep, held, fresh, near = list(sends), list(keeps), [None] * 2, [None] * 2, [None] * 2
    count = blocks // 2
    for stage in range(stages - 1):
        for stream in range(STREAMS):
            got = exchange(send[stream], pairing(stage, stream), groups, members)
            if stage < stages - 2:
                send[stream], keep[stream] = small_call(
                    functools.partial(fold_kernel, count // 2 * share, count),
                    "fold",
                    [bf(count // 2)] * 2,
                    got,
                    keep[stream],
                )
            else:
                send[stream], near[stream] = small_call(
                    functools.partial(seed_kernel, share, count),
                    "seed",
                    [bf(2), share_f32],
                    got,
                    keep[stream],
                    old_share[:, stream * wide : (stream + 1) * wide],
                )
        count //= 2
    for stream in range(STREAMS):
        got = exchange(send[stream], pairing(stages - 1, stream), groups, members)
        fresh[stream], held[stream] = small_call(
            functools.partial(centroid_kernel, share, base, digits, tail),
            "centroid",
            [share_f32, bf(2)],
            got,
            send[stream],
            near[stream],
        )
    count = 2
    pieces = [[], []]
    for stage in reversed(range(stages - 1)):
        for stream in range(STREAMS):
            got = exchange(held[stream], pairing(stage, stream), groups, members)
            if stage:
                held[stream] = small_call(
                    functools.partial(join_kernel, count * share, count), "join", [bf(2 * count)], got, held[stream]
                )[0]
            else:
                pieces[stream] = [got, held[stream]]
        count *= 2

    half_blocks = blocks // 2
    norm_rows, where = [], []
    for stream in range(STREAMS):
        pieces[stream] += [sibling(piece) for piece in pieces[stream]]
        codes = []
        for which, piece in enumerate(pieces[stream]):
            part = which % 2
            flip = which // 2
            rows_of = piece[half_blocks * share + tail - half_blocks :].astype(F32)
            norm_rows.append(sum(rows_of[:, p * share : (p + 1) * share] for p in range(PARTS)))
            for block in range(half_blocks):
                rel = [relative_of(part * half_blocks + block, turned[c, stream]) for c in range(2)]
                holder = core ^ flip
                group_rel = jnp.where(holder == 0, rel[0][0], rel[1][0])
                member_rel = jnp.where(holder == 0, rel[0][1], rel[1][1])
                codes.append((z ^ group_rel) * members + (me ^ flip ^ member_rel))
        where.append(jnp.stack(codes).astype(jnp.int32))
    norm_rows = jnp.concatenate(norm_rows)
    where_all = jnp.concatenate(where)
    pick = (where_all[None, :] == jnp.arange(groups * members, dtype=jnp.int32)[:, None]).astype(F32)
    half_norm = jnp.dot(pick, norm_rows, precision=lax.Precision.HIGHEST).reshape(groups, keys)

    gid = jnp.where(live, coarse_label[:, 0], -1)[:, None]
    scores = None
    for stream in range(STREAMS):
        scores = add_scores(
            samples, gid, half_norm, pieces[stream], where[stream], scores, groups, keys, share, stream
        )
    return scores, jnp.concatenate(fresh, axis=1)[None]


def solution(mesh):
    return jax.shard_map(
        per_device,
        mesh=mesh,
        in_specs=(
            P(AXES, None),
            P(AXES, None),
            P(AXES),
            P(AXES),
            P("coarse", None, None),
        ),
        out_specs=(P(AXES, None), P("coarse", "member", None)),
        check_vma=False,
    )
```

```python
import functools

import jax
import jax.numpy as jnp
from jax import lax
from jax.experimental import pallas as pl
from jax.experimental.pallas import tpu as pltpu
from jax.sharding import PartitionSpec as P

AXES = ("coarse", "member")
TILE = 16
PRIOR = 16.0
PARTS = 2
F32 = jnp.float32
BF16 = jnp.bfloat16


def pad_rows(blocks):
    return max(TILE, -(-blocks // TILE) * TILE)


def streams_of(width):
    wide = width * 2 // 3
    return ((0, wide), (wide, width - wide))


def orders_of(groups, members):
    inner = [(0, 1 << bit) for bit in range(1, members.bit_length() - 1)]
    outer = [((1 << (bit + 1)) - 1, 0) for bit in range(groups.bit_length() - 1)]
    found = {}
    for core in range(2):
        cut = core * len(inner) // 2
        turned = inner[cut:] + inner[:cut]
        found[core, 0] = turned + outer
        found[core, 1] = outer[:1] + turned + outer[1:]
    return found


def exchange(array, partner, groups, members):
    pairs = []
    for z in range(groups):
        for m in range(members):
            to_z, to_m = partner(z, m)
            pairs.append((z * members + m, to_z * members + to_m))
    return lax.ppermute(array, AXES, pairs)


def coefficients(group_rel, member_rel, dims, outer_bits):
    out = []
    for group_mask, member_mask in dims:
        if member_mask:
            out.append((member_rel >> (member_mask.bit_length() - 1)) & 1)
        else:
            top = group_mask.bit_length() - 1
            bit = (group_rel >> top) & 1
            if top + 1 < outer_bits:
                bit = bit ^ ((group_rel >> (top + 1)) & 1)
            out.append(bit)
    return out


def block_position(group_rel, member_rel, dims, outer_bits):
    place = 0
    for bit in coefficients(group_rel, member_rel, dims, outer_bits):
        place = place * 2 + (1 - bit)
    return place


def relative_of(place, dims):
    group_rel = member_rel = 0
    for at, (group_mask, member_mask) in enumerate(dims):
        if not (place >> (len(dims) - 1 - at)) & 1:
            group_rel ^= group_mask
            member_rel ^= member_mask
    return group_rel, member_rel


def sums_kernel(base, pos_ref, own_ref, other_ref, *rest):
    out_ref = rest[-1]
    rows = own_ref.shape[0]
    keys = out_ref.shape[0] - (rest[0].shape[0] if len(rest) > 1 else 0)
    key = lax.broadcasted_iota(jnp.int32, (keys, rows), 0) + base
    first = jnp.where(pos_ref[:, :rows] == key, 1.0, 0.0).astype(BF16)
    second = jnp.where(pos_ref[:, rows:] == key, 1.0, 0.0).astype(BF16)
    total = jnp.dot(first, own_ref[...], preferred_element_type=F32)
    total += jnp.dot(second, other_ref[...], preferred_element_type=F32)
    out_ref[:keys, :] = total.astype(BF16)
    if len(rest) > 1:
        out_ref[keys:, :] = rest[0][...]


def key_sums(pos_row, own, other, count_tile, base, keys, start, wide):
    rows = own.shape[0]
    extra = [] if count_tile is None else [count_tile]
    out_rows = keys + sum(e.shape[0] for e in extra)
    return pl.pallas_call(
        functools.partial(sums_kernel, base),
        grid=(1,),
        out_shape=jax.ShapeDtypeStruct((out_rows, wide), BF16),
        in_specs=[
            pl.BlockSpec((1, 2 * rows), lambda i: (0, 0)),
            pl.BlockSpec((rows, wide), lambda i: (0, start // wide)),
            pl.BlockSpec((rows, wide), lambda i: (0, start // wide)),
        ]
        + [pl.BlockSpec(e.shape, lambda i: (0, 0)) for e in extra],
        out_specs=pl.BlockSpec((out_rows, wide), lambda i: (0, 0)),
        compiler_params=pltpu.CompilerParams(vmem_limit_bytes=24 << 20),
        cost_estimate=pl.CostEstimate(
            flops=2 * keys * 2 * rows * wide, bytes_accessed=(4 * rows + 2 * keys) * wide, transcendentals=0
        ),
        name="key_sums",
    )(pos_row, own, other, *extra)


def small_call(kernel, name, outs, *args):
    whole = pl.BlockSpec(memory_space=pltpu.VMEM)
    moved = sum(a.size * a.dtype.itemsize for a in (*args, *outs))
    return pl.pallas_call(
        kernel,
        out_shape=outs,
        in_specs=[whole] * len(args),
        out_specs=[whole] * len(outs),
        compiler_params=pltpu.CompilerParams(vmem_limit_bytes=12 << 20),
        cost_estimate=pl.CostEstimate(flops=moved // 2, bytes_accessed=moved, transcendentals=0),
        name=name,
    )(*args)


def add_pair(got_ref, keep_ref, start, stop):
    return got_ref[start:stop, :].astype(F32) + keep_ref[start:stop, :].astype(F32)


def add_tail(got_ref, keep_ref, body, shift):
    kept = keep_ref[body:, :].astype(F32)
    return (kept + pltpu.roll(got_ref[body:, :].astype(F32), shift, 0)).astype(BF16)


def fold_kernel(half, shift, got_ref, keep_ref, send_out, keep_out):
    send_out[:half, :] = add_pair(got_ref, keep_ref, 0, half).astype(BF16)
    keep_out[:half, :] = add_pair(got_ref, keep_ref, half, 2 * half).astype(BF16)
    if got_ref.shape[0] > 2 * half:
        tail = add_tail(got_ref, keep_ref, 2 * half, shift)
        send_out[half:, :] = tail
        keep_out[half:, :] = tail


def seed_kernel(share, shift, got_ref, keep_ref, old_ref, send_out, near_out):
    two = 2 * share
    near = add_pair(got_ref, keep_ref, share, two) + PRIOR * old_ref[...]
    near_out[...] = near
    send_out[:share, :] = add_pair(got_ref, keep_ref, 0, share).astype(BF16)
    send_out[share:two, :] = near.astype(BF16)
    if got_ref.shape[0] > two:
        send_out[two:, :] = add_tail(got_ref, keep_ref, two, shift)


def summed(share, block, got_ref, sent_ref, near_ref):
    if block == 0:
        return sent_ref[:share, :].astype(F32) + got_ref[share : 2 * share, :].astype(F32)
    return near_ref[...] + got_ref[:share, :].astype(F32)


def square_sums(rounded):
    return jnp.sum(jnp.square(rounded.astype(F32)), axis=1, keepdims=True)


def first_kernel(share, base, digits, got_ref, sent_ref, near_ref, fresh_out, cents_out, scale_out, norm_out):
    two = 2 * share
    wide = got_ref.shape[1]
    last = sent_ref.shape[0] - two - 1
    lane = lax.broadcasted_iota(jnp.int32, (share, wide), 1)
    line = lax.broadcasted_iota(jnp.int32, (share, wide), 0)
    mine = sent_ref[two:, :].astype(F32)
    theirs = got_ref[two:, :].astype(F32)
    for block in range(2):
        row = mine[last - 1 + block : last + block, :] + theirs[last - block : last - block + 1, :]
        count = jnp.full((share, 1), PRIOR, F32)
        for digit in range(digits):
            hit = jnp.where(lane == line + digit * share, row, 0.0)
            count += jnp.sum(hit, axis=1, keepdims=True) * float(base**digit)
        scale_out[block * share : (block + 1) * share, :] = count
        fresh = summed(share, block, got_ref, sent_ref, near_ref) / count
        rounded = fresh.astype(BF16)
        cents_out[block * share : (block + 1) * share, :] = rounded
        norm_out[block * share : (block + 1) * share, :] = square_sums(rounded)
        if block == 1:
            fresh_out[...] = fresh


def last_kernel(share, tail, got_ref, sent_ref, near_ref, scale_ref, norm_ref, fresh_out, cents_out):
    two = 2 * share
    wide = got_ref.shape[1]
    lane = lax.broadcasted_iota(jnp.int32, (share, wide), 1)
    line = lax.broadcasted_iota(jnp.int32, (share, wide), 0)
    tile = jnp.zeros((tail, wide), F32)
    tile_row = lax.broadcasted_iota(jnp.int32, (tail, wide), 0)
    for block in range(2):
        part = slice(block * share, (block + 1) * share)
        fresh = summed(share, block, got_ref, sent_ref, near_ref) / scale_ref[part, :]
        rounded = fresh.astype(BF16)
        cents_out[part, :] = rounded
        if block == 1:
            fresh_out[...] = fresh
        norm = 0.5 * (norm_ref[part, :] + square_sums(rounded))
        spread = jnp.zeros((1, wide), F32)
        for term_at in range(PARTS):
            term = norm.astype(BF16).astype(F32)
            norm = norm - term
            hit = jnp.where(lane == line + term_at * share, term, 0.0)
            spread += jnp.sum(hit, axis=0, keepdims=True)
        tile = jnp.where(tile_row == tail - 2 + block, spread, tile)
    cents_out[two:, :] = tile.astype(BF16)


def join_kernel(body, shift, got_ref, held_ref, out_ref):
    out_ref[:body, :] = got_ref[:body, :]
    out_ref[body : 2 * body, :] = held_ref[:body, :]
    if held_ref.shape[0] > body:
        rows = held_ref.shape[0] - body
        moved = pltpu.roll(got_ref[body:, :].astype(F32), rows - shift, 0)
        out_ref[2 * body :, :] = (held_ref[body:, :].astype(F32) + moved).astype(BF16)


def scores_kernel(groups, share, last, where_ref, x_ref, gid_ref, *rest):
    pieces = 4
    piece_refs, rest = rest[:pieces], rest[pieces:]
    if last:
        total_ref, half_ref, out_ref, cents, masked, half = rest
    else:
        out_ref, cents, masked = rest
    wide = x_ref.shape[1]
    keys = cents.shape[0]
    members = keys // share
    blocks = where_ref.shape[0] // pieces
    lanes = 128

    @pl.when(pl.program_id(0) == 0)
    def _():
        if last and share < lanes:
            half[...] = half_ref[...]
        for piece in range(pieces):
            ref = piece_refs[piece]
            for block in range(blocks):
                code = where_ref[piece * blocks + block]
                group = code // members
                member = code % members
                cents[
                    pl.ds(pl.multiple_of(member * share, share), share),
                    pl.ds(pl.multiple_of(group * wide, lanes), wide),
                ] = ref[block * share : (block + 1) * share, :]
            if last and share >= lanes:
                tail = ref[blocks * share :, :].astype(F32)
                for block in range(blocks):
                    code = where_ref[piece * blocks + block]
                    at = tail.shape[0] - blocks + block
                    row = sum(tail[at : at + 1, p * share : (p + 1) * share] for p in range(PARTS))
                    for cut in range(share // lanes):
                        half[pl.ds(code * (share // lanes) + cut, 1), :] = row[:, cut * lanes : (cut + 1) * lanes]
        for group in range(groups):
            masked[:, group * wide : (group + 1) * wide] = jnp.where(
                gid_ref[...] == group, x_ref[...], jnp.zeros_like(x_ref)
            )

    step = out_ref.shape[1]
    at = pl.program_id(0)
    start = pl.multiple_of(at * step, step)
    dots = lax.dot_general(
        masked[...], cents[pl.ds(start, step), :], (((1,), (1,)), ((), ())), preferred_element_type=F32
    )
    if not last:
        out_ref[...] = dots
        return
    gid = gid_ref[...]
    for cut in range(step // lanes):
        columns = slice(cut * lanes, (cut + 1) * lanes)
        offset = jnp.zeros((out_ref.shape[0], lanes), F32)
        for group in range(groups):
            row = half[pl.ds(group * (keys // lanes) + at * (step // lanes) + cut, 1), :]
            offset = jnp.where(gid == group, row, offset)
        out_ref[:, columns] = (dots[:, columns] + total_ref[:, columns] - offset).astype(BF16)


def add_scores(samples, gid, pieces, where, total, half, groups, keys, share, start, wide):
    rows = samples.shape[0]
    step = min(256, keys)
    last = total is not None
    whole = pl.BlockSpec(memory_space=pltpu.VMEM)
    return pl.pallas_call(
        functools.partial(scores_kernel, groups, share, last),
        grid_spec=pltpu.PrefetchScalarGridSpec(
            num_scalar_prefetch=1,
            grid=(keys // step,),
            in_specs=[
                pl.BlockSpec((rows, wide), lambda i, w: (0, start // wide)),
                pl.BlockSpec((rows, 1), lambda i, w: (0, 0)),
            ]
            + [whole] * len(pieces)
            + [pl.BlockSpec((rows, step), lambda i, w: (0, i)), whole] * last,
            out_specs=pl.BlockSpec((rows, step), lambda i, w: (0, i)),
            scratch_shapes=[
                pltpu.VMEM((keys, groups * wide), BF16),
                pltpu.VMEM((rows, groups * wide), BF16),
            ]
            + [pltpu.VMEM((groups * keys // 128, 128), F32)] * last,
        ),
        out_shape=jax.ShapeDtypeStruct((rows, keys), BF16 if last else F32),
        compiler_params=pltpu.CompilerParams(vmem_limit_bytes=26 << 20),
        cost_estimate=pl.CostEstimate(
            flops=2 * rows * keys * groups * wide, bytes_accessed=2 * (rows + groups * keys) * wide, transcendentals=0
        ),
        name="scores",
    )(where, samples, gid, *pieces, *([total, half] if last else []))


def per_device(samples, coarse_label, fine_label, live_rows, old_centroids):
    groups = lax.axis_size("coarse")
    members = lax.axis_size("member")
    z = lax.axis_index("coarse")
    me = lax.axis_index("member")
    core = me & 1
    rows, width = samples.shape
    keys = old_centroids.shape[1]
    share = keys // members
    columns = streams_of(width)
    streams = range(len(columns))
    half_keys = groups * keys // 2
    blocks = half_keys // share
    outer_bits = groups.bit_length() - 1
    turned = orders_of(groups, members)
    stages = len(turned[0, 0])
    base = 256 // (groups * members // 2) + 1
    digits = 1
    while base**digits <= 2 * rows:
        digits += 1

    live = jnp.arange(rows, dtype=jnp.int32) < live_rows[0]
    label = jnp.where(live, coarse_label[:, 0] * keys + fine_label, -1)
    sibling = lambda a: exchange(a, lambda gz, m: (gz, m ^ 1), groups, members)
    other_samples = sibling(samples)
    label_all = jnp.concatenate([label, sibling(label)])

    group_of = label_all // keys
    fine = label_all % keys
    owner = fine // share
    mine = (label_all >= 0) & ((owner & 1) == core)

    def of_core(make):
        return jnp.where(core == 0, make(0), make(1))

    def pairing(stage, stream):
        def partner(gz, m):
            group_mask, member_mask = turned[m & 1, stream][stage]
            return gz ^ group_mask, m ^ member_mask

        return partner

    tail = pad_rows(blocks)
    sends, keeps = [], []
    for stream, (start, wide) in enumerate(columns):
        place = of_core(
            lambda c: block_position(group_of ^ z, owner ^ me, turned[c, stream], outer_bits)
        )
        pos = jnp.where(mine, place * share + fine % share, -1)
        tile = None
        if stream == 0:
            in_block = (jnp.where(mine, place, -1)[:, None] == jnp.arange(tail)[None, :]).astype(BF16)
            in_lane = ((fine % share)[:, None] == jnp.arange(share)[None, :]).astype(BF16)
            counted = lax.dot_general(
                in_block, in_lane, (((0,), (0,)), ((), ())), preferred_element_type=F32
            ).astype(jnp.int32)
            tile = [(counted // base**digit) % base for digit in range(digits)]
            tile = jnp.concatenate(tile, axis=1).astype(BF16)
            tile = jnp.pad(tile, ((0, 0), (0, wide - digits * share)))
        make = functools.partial(
            key_sums, pos[None, :], samples, other_samples, tile, keys=half_keys // 2, start=start, wide=wide
        )
        sends.append(make(base=0))
        keeps.append(make(base=half_keys // 2))

    old_share = lax.dynamic_slice(old_centroids[0], (me * share, 0), (share, width))

    def bf(count, stream, tailed):
        rows_out = count * share + (tail if stream == tailed else 0)
        return jax.ShapeDtypeStruct((rows_out, columns[stream][1]), BF16)

    share_f32 = [jax.ShapeDtypeStruct((share, wide), F32) for _, wide in columns]
    send, keep, held, fresh, near = list(sends), list(keeps), [None] * 2, [None] * 2, [None] * 2
    count = blocks // 2
    for stage in range(stages - 1):
        for stream, (start, wide) in enumerate(columns):
            got = exchange(send[stream], pairing(stage, stream), groups, members)
            if stage < stages - 2:
                send[stream], keep[stream] = small_call(
                    functools.partial(fold_kernel, count // 2 * share, count),
                    "fold",
                    [bf(count // 2, stream, 0)] * 2,
                    got,
                    keep[stream],
                )
            else:
                send[stream], near[stream] = small_call(
                    functools.partial(seed_kernel, share, count),
                    "seed",
                    [bf(2, stream, 0), share_f32[stream]],
                    got,
                    keep[stream],
                    old_share[:, start : start + wide],
                )
        count //= 2
    column = jax.ShapeDtypeStruct((2 * share, 1), F32)
    for stream in streams:
        got = exchange(send[stream], pairing(stages - 1, stream), groups, members)
        if stream == 0:
            fresh[0], held[0], scale, norm = small_call(
                functools.partial(first_kernel, share, base, digits),
                "first_centroids",
                [share_f32[0], bf(2, 0, 1), column, column],
                got,
                send[0],
                near[0],
            )
        else:
            fresh[1], held[1] = small_call(
                functools.partial(last_kernel, share, tail),
                "last_centroids",
                [share_f32[1], bf(2, 1, 1)],
                got,
                send[1],
                near[1],
                scale,
                norm,
            )
    count = 2
    pieces = [[], []]
    for stage in reversed(range(stages - 1)):
        for stream in streams:
            got = exchange(held[stream], pairing(stage, stream), groups, members)
            if stage:
                held[stream] = small_call(
                    functools.partial(join_kernel, count * share, count),
                    "join",
                    [bf(2 * count, stream, 1)],
                    got,
                    held[stream],
                )[0]
            else:
                pieces[stream] = [got, held[stream]]
        count *= 2

    half_blocks = blocks // 2
    where = []
    for stream in streams:
        pieces[stream] += [sibling(piece) for piece in pieces[stream]]
        codes = []
        for which in range(len(pieces[stream])):
            part = which % 2
            flip = which // 2
            for block in range(half_blocks):
                rel = [relative_of(part * half_blocks + block, turned[c, stream]) for c in range(2)]
                holder = core ^ flip
                group_rel = jnp.where(holder == 0, rel[0][0], rel[1][0])
                member_rel = jnp.where(holder == 0, rel[0][1], rel[1][1])
                codes.append((z ^ group_rel) * members + (me ^ flip ^ member_rel))
        where.append(jnp.stack(codes).astype(jnp.int32))
    half = jnp.zeros((groups * keys // 128, 128), F32)
    if share < 128:
        norm_rows = []
        for piece in pieces[1]:
            rows_of = piece[half_blocks * share + tail - half_blocks :].astype(F32)
            norm_rows.append(sum(rows_of[:, p * share : (p + 1) * share] for p in range(PARTS)))
        pick = (where[1][None, :] == jnp.arange(groups * members, dtype=jnp.int32)[:, None]).astype(F32)
        half = jnp.dot(pick, jnp.concatenate(norm_rows), precision=lax.Precision.HIGHEST).reshape(half.shape)

    gid = jnp.where(live, coarse_label[:, 0], -1)[:, None]
    scores = None
    for stream, (start, wide) in enumerate(columns):
        scores = add_scores(
            samples, gid, pieces[stream], where[stream], scores, half, groups, keys, share, start, wide
        )
    return scores, jnp.concatenate(fresh, axis=1)[None]


def solution(mesh):
    return jax.shard_map(
        per_device,
        mesh=mesh,
        in_specs=(
            P(AXES, None),
            P(AXES, None),
            P(AXES),
            P(AXES),
            P("coarse", None, None),
        ),
        out_specs=(P(AXES, None), P("coarse", "member", None)),
        check_vma=False,
    )
```

```python
import functools

import jax
import jax.numpy as jnp
from jax import lax
from jax.experimental import pallas as pl
from jax.experimental.pallas import tpu as pltpu
from jax.sharding import PartitionSpec as P

AXES = ("coarse", "member")
TILE = 16
PRIOR = 16.0
PARTS = 2
F32 = jnp.float32
BF16 = jnp.bfloat16


def pad_rows(blocks):
    return max(TILE, -(-blocks // TILE) * TILE)


def streams_of(width):
    wide = width * 2 // 3
    return ((0, wide), (wide, width - wide))


def orders_of(groups, members):
    inner = [(0, 1 << bit) for bit in range(1, members.bit_length() - 1)]
    outer = [((1 << (bit + 1)) - 1, 0) for bit in range(groups.bit_length() - 1)]
    found = {}
    for core in range(2):
        cut = core * len(inner) // 2
        turned = inner[cut:] + inner[:cut]
        found[core, 0] = turned + outer
        found[core, 1] = outer[:1] + turned + outer[1:]
    return found


def exchange(array, partner, groups, members):
    pairs = []
    for z in range(groups):
        for m in range(members):
            to_z, to_m = partner(z, m)
            pairs.append((z * members + m, to_z * members + to_m))
    return lax.ppermute(array, AXES, pairs)


def coefficients(group_rel, member_rel, dims, outer_bits):
    out = []
    for group_mask, member_mask in dims:
        if member_mask:
            out.append((member_rel >> (member_mask.bit_length() - 1)) & 1)
        else:
            top = group_mask.bit_length() - 1
            bit = (group_rel >> top) & 1
            if top + 1 < outer_bits:
                bit = bit ^ ((group_rel >> (top + 1)) & 1)
            out.append(bit)
    return out


def block_position(group_rel, member_rel, dims, outer_bits):
    place = 0
    for bit in coefficients(group_rel, member_rel, dims, outer_bits):
        place = place * 2 + (1 - bit)
    return place


def relative_of(place, dims):
    group_rel = member_rel = 0
    for at, (group_mask, member_mask) in enumerate(dims):
        if not (place >> (len(dims) - 1 - at)) & 1:
            group_rel ^= group_mask
            member_rel ^= member_mask
    return group_rel, member_rel


def token_shape():
    return jax.ShapeDtypeStruct((8, 128), F32)


def hand_on(kernel, inputs):
    def run(*refs):
        kernel(*refs[:inputs], *refs[inputs + 1 : -1])
        refs[-1][...] = refs[inputs][...]

    return run


def sums_kernel(base, pos_ref, own_ref, other_ref, *rest):
    out_ref = rest[-1]
    rows = own_ref.shape[0]
    keys = out_ref.shape[0] - (rest[0].shape[0] if len(rest) > 1 else 0)
    key = lax.broadcasted_iota(jnp.int32, (keys, rows), 0) + base
    first = jnp.where(pos_ref[:, :rows] == key, 1.0, 0.0).astype(BF16)
    second = jnp.where(pos_ref[:, rows:] == key, 1.0, 0.0).astype(BF16)
    total = jnp.dot(first, own_ref[...], preferred_element_type=F32)
    total += jnp.dot(second, other_ref[...], preferred_element_type=F32)
    out_ref[:keys, :] = total.astype(BF16)
    if len(rest) > 1:
        out_ref[keys:, :] = rest[0][...]


def key_sums(token, pos_row, own, other, count_tile, base, keys, start, wide):
    rows = own.shape[0]
    extra = [] if count_tile is None else [count_tile]
    out_rows = keys + sum(e.shape[0] for e in extra)
    whole = lambda shape: pl.BlockSpec(shape, lambda i: (0, 0))
    return pl.pallas_call(
        hand_on(functools.partial(sums_kernel, base), 3 + len(extra)),
        grid=(1,),
        out_shape=[jax.ShapeDtypeStruct((out_rows, wide), BF16), token_shape()],
        in_specs=[
            whole((1, 2 * rows)),
            pl.BlockSpec((rows, wide), lambda i: (0, start // wide)),
            pl.BlockSpec((rows, wide), lambda i: (0, start // wide)),
        ]
        + [whole(e.shape) for e in extra]
        + [whole(token.shape)],
        out_specs=[whole((out_rows, wide)), whole(token.shape)],
        compiler_params=pltpu.CompilerParams(vmem_limit_bytes=24 << 20),
        cost_estimate=pl.CostEstimate(
            flops=2 * keys * 2 * rows * wide, bytes_accessed=(4 * rows + 2 * keys) * wide, transcendentals=0
        ),
        name="key_sums",
    )(pos_row, own, other, *extra, token)


def small_call(kernel, name, outs, token, *args):
    whole = pl.BlockSpec(memory_space=pltpu.VMEM)
    moved = sum(a.size * a.dtype.itemsize for a in (*args, *outs))
    return pl.pallas_call(
        hand_on(kernel, len(args)),
        out_shape=[*outs, token_shape()],
        in_specs=[whole] * (len(args) + 1),
        out_specs=[whole] * (len(outs) + 1),
        compiler_params=pltpu.CompilerParams(vmem_limit_bytes=12 << 20),
        cost_estimate=pl.CostEstimate(flops=moved // 2, bytes_accessed=moved, transcendentals=0),
        name=name,
    )(*args, token)


def add_pair(got_ref, keep_ref, start, stop):
    return got_ref[start:stop, :].astype(F32) + keep_ref[start:stop, :].astype(F32)


def add_tail(got_ref, keep_ref, body, shift):
    kept = keep_ref[body:, :].astype(F32)
    return (kept + pltpu.roll(got_ref[body:, :].astype(F32), shift, 0)).astype(BF16)


def fold_kernel(half, shift, got_ref, keep_ref, send_out, keep_out):
    send_out[:half, :] = add_pair(got_ref, keep_ref, 0, half).astype(BF16)
    keep_out[:half, :] = add_pair(got_ref, keep_ref, half, 2 * half).astype(BF16)
    if got_ref.shape[0] > 2 * half:
        tail = add_tail(got_ref, keep_ref, 2 * half, shift)
        send_out[half:, :] = tail
        keep_out[half:, :] = tail


def seed_kernel(share, shift, got_ref, keep_ref, old_ref, send_out, near_out):
    two = 2 * share
    near = add_pair(got_ref, keep_ref, share, two) + PRIOR * old_ref[...]
    near_out[...] = near
    send_out[:share, :] = add_pair(got_ref, keep_ref, 0, share).astype(BF16)
    send_out[share:two, :] = near.astype(BF16)
    if got_ref.shape[0] > two:
        send_out[two:, :] = add_tail(got_ref, keep_ref, two, shift)


def summed(share, block, got_ref, sent_ref, near_ref):
    if block == 0:
        return sent_ref[:share, :].astype(F32) + got_ref[share : 2 * share, :].astype(F32)
    return near_ref[...] + got_ref[:share, :].astype(F32)


def square_sums(rounded):
    return jnp.sum(jnp.square(rounded.astype(F32)), axis=1, keepdims=True)


def first_kernel(share, base, digits, got_ref, sent_ref, near_ref, fresh_out, cents_out, scale_out, norm_out):
    two = 2 * share
    wide = got_ref.shape[1]
    last = sent_ref.shape[0] - two - 1
    lane = lax.broadcasted_iota(jnp.int32, (share, wide), 1)
    line = lax.broadcasted_iota(jnp.int32, (share, wide), 0)
    mine = sent_ref[two:, :].astype(F32)
    theirs = got_ref[two:, :].astype(F32)
    for block in range(2):
        row = mine[last - 1 + block : last + block, :] + theirs[last - block : last - block + 1, :]
        count = jnp.full((share, 1), PRIOR, F32)
        for digit in range(digits):
            hit = jnp.where(lane == line + digit * share, row, 0.0)
            count += jnp.sum(hit, axis=1, keepdims=True) * float(base**digit)
        scale_out[block * share : (block + 1) * share, :] = count
        fresh = summed(share, block, got_ref, sent_ref, near_ref) / count
        rounded = fresh.astype(BF16)
        cents_out[block * share : (block + 1) * share, :] = rounded
        norm_out[block * share : (block + 1) * share, :] = square_sums(rounded)
        if block == 1:
            fresh_out[...] = fresh


def last_kernel(share, tail, got_ref, sent_ref, near_ref, scale_ref, norm_ref, fresh_out, cents_out):
    two = 2 * share
    wide = got_ref.shape[1]
    lane = lax.broadcasted_iota(jnp.int32, (share, wide), 1)
    line = lax.broadcasted_iota(jnp.int32, (share, wide), 0)
    tile = jnp.zeros((tail, wide), F32)
    tile_row = lax.broadcasted_iota(jnp.int32, (tail, wide), 0)
    for block in range(2):
        part = slice(block * share, (block + 1) * share)
        fresh = summed(share, block, got_ref, sent_ref, near_ref) / scale_ref[part, :]
        rounded = fresh.astype(BF16)
        cents_out[part, :] = rounded
        if block == 1:
            fresh_out[...] = fresh
        norm = 0.5 * (norm_ref[part, :] + square_sums(rounded))
        spread = jnp.zeros((1, wide), F32)
        for term_at in range(PARTS):
            term = norm.astype(BF16).astype(F32)
            norm = norm - term
            hit = jnp.where(lane == line + term_at * share, term, 0.0)
            spread += jnp.sum(hit, axis=0, keepdims=True)
        tile = jnp.where(tile_row == tail - 2 + block, spread, tile)
    cents_out[two:, :] = tile.astype(BF16)


def join_kernel(body, shift, got_ref, held_ref, out_ref):
    out_ref[:body, :] = got_ref[:body, :]
    out_ref[body : 2 * body, :] = held_ref[:body, :]
    if held_ref.shape[0] > body:
        rows = held_ref.shape[0] - body
        moved = pltpu.roll(got_ref[body:, :].astype(F32), rows - shift, 0)
        out_ref[2 * body :, :] = (held_ref[body:, :].astype(F32) + moved).astype(BF16)


def mask_kernel(groups, columns, gid_ref, x_ref, *outs):
    gid = gid_ref[...]
    for (start, wide), out in zip(columns, outs):
        x = x_ref[:, start : start + wide]
        for group in range(groups):
            out[:, group * wide : (group + 1) * wide] = jnp.where(gid == group, x, jnp.zeros_like(x))
    pick = outs[-1]
    lane = lax.broadcasted_iota(jnp.int32, pick.shape, 1)
    hit = (lane % groups == gid) & (lane < PARTS * groups)
    pick[...] = jnp.where(hit, -1.0, 0.0).astype(BF16)


def product(a, b):
    return lax.dot_general(a, b, (((1,), (1,)), ((), ())), preferred_element_type=F32)


def part_kernel(groups, share, group_ref, masked_ref, own_ref, other_ref, *rest):
    out_ref, cents = rest[-2:]
    wide = own_ref.shape[1]
    blocks = own_ref.shape[0] // share

    @pl.when(pl.program_id(0) == 0)
    def _():
        for piece, ref in enumerate((own_ref, other_ref)):
            for block in range(blocks):
                group = group_ref[piece * blocks + block]
                slot = (piece * blocks + block) // groups
                cents[
                    slot * share : (slot + 1) * share, pl.ds(pl.multiple_of(group * wide, 128), wide)
                ] = ref[block * share : (block + 1) * share, :]

    step = out_ref.shape[1]
    start = pl.multiple_of(pl.program_id(0) * step, step)
    out_ref[...] = product(masked_ref[...], cents[pl.ds(start, step), :])


def part_scores(token, masked, group_of, pieces, before, groups, keys, share):
    rows = masked.shape[0]
    wide = pieces[0].shape[1]
    half = pieces[0].shape[0] * len(pieces) // groups
    step = min(256, half)
    steps = half // step
    at = 0 if before is None else steps
    whole = pl.BlockSpec(memory_space=pltpu.VMEM)
    extra = [] if before is None else [before]

    def kernel(group_ref, *refs):
        count = 3 + len(extra)
        part_kernel(groups, share, group_ref, *refs[:3], refs[count + 1], refs[-1])
        refs[count + 2][...] = refs[count][...]

    return pl.pallas_call(
        kernel,
        grid_spec=pltpu.PrefetchScalarGridSpec(
            num_scalar_prefetch=1,
            grid=(steps,),
            in_specs=[whole] * 3 + [pl.BlockSpec(memory_space=pl.ANY)] * len(extra) + [whole],
            out_specs=[pl.BlockSpec((rows, step), lambda i, w: (0, i + at)), whole],
            scratch_shapes=[pltpu.VMEM((half, groups * wide), BF16)],
        ),
        out_shape=[jax.ShapeDtypeStruct((rows, keys), F32), token_shape()],
        input_output_aliases={} if before is None else {4: 0},
        compiler_params=pltpu.CompilerParams(vmem_limit_bytes=16 << 20),
        cost_estimate=pl.CostEstimate(
            flops=2 * rows * half * groups * wide,
            bytes_accessed=2 * (rows + half) * groups * wide + 4 * rows * half,
            transcendentals=0,
        ),
        name="part_scores",
    )(group_of, masked, *pieces, *extra, token)


def final_kernel(groups, share, code_ref, slot_ref, masked_ref, pick_ref, half_ref, *rest):
    pieces = 4
    piece_refs, total_refs = rest[:pieces], rest[pieces : pieces + 2]
    out_ref, cents, half = rest[-3:]
    keys = cents.shape[0]
    wide = cents.shape[1] // groups
    members = keys // share
    blocks = code_ref.shape[0] // pieces
    lanes = 128

    @pl.when(pl.program_id(0) == 0)
    def _():
        half[...] = half_ref[...]
        for piece, ref in enumerate(piece_refs):
            for block in range(blocks):
                code = code_ref[piece * blocks + block]
                group = code // members
                row_at = pl.multiple_of((code % members) * share, share)
                cents[pl.ds(row_at, share), pl.ds(pl.multiple_of(group * wide, lanes), wide)] = ref[
                    block * share : (block + 1) * share, :
                ]
                if share >= lanes:
                    tail = ref[blocks * share :, :].astype(F32)
                    at = tail.shape[0] - blocks + block
                    lines = pl.ds(pl.multiple_of(row_at, lanes), share)
                    line = lax.broadcasted_iota(jnp.int32, (half.shape[0], share), 0)
                    filled = half[:, lines]
                    for term in range(PARTS):
                        row = tail[at : at + 1, term * share : (term + 1) * share]
                        filled = jnp.where(line == group + term * groups, row, filled)
                    half[:, lines] = filled

    step = out_ref.shape[1]
    start = pl.multiple_of(pl.program_id(0) * step, step)
    dots = product(masked_ref[...], cents[pl.ds(start, step), :])
    offsets = half[:, pl.ds(start, step)].astype(BF16)
    dots += jnp.dot(pick_ref[...], offsets, preferred_element_type=F32)
    cut = step // 2
    out_ref[:, :cut] = (dots[:, :cut] + total_refs[0][...]).astype(BF16)
    out_ref[:, cut:] = (dots[:, cut:] + total_refs[1][...]).astype(BF16)


def final_scores(masked, pick, codes, slots, pieces, total, half, groups, keys, share):
    rows = masked.shape[0]
    wide = pieces[0].shape[1]
    step = min(256, keys)
    cut = step // 2
    whole = pl.BlockSpec(memory_space=pltpu.VMEM)
    return pl.pallas_call(
        functools.partial(final_kernel, groups, share),
        grid_spec=pltpu.PrefetchScalarGridSpec(
            num_scalar_prefetch=2,
            grid=(keys // step,),
            in_specs=[whole] * (3 + len(pieces))
            + [
                pl.BlockSpec((rows, cut), lambda i, c, s: (0, s[2 * i])),
                pl.BlockSpec((rows, cut), lambda i, c, s: (0, s[2 * i + 1])),
            ],
            out_specs=pl.BlockSpec((rows, step), lambda i, c, s: (0, i)),
            scratch_shapes=[pltpu.VMEM((keys, groups * wide), BF16), pltpu.VMEM(half.shape, F32)],
        ),
        out_shape=jax.ShapeDtypeStruct((rows, keys), BF16),
        compiler_params=pltpu.CompilerParams(vmem_limit_bytes=16 << 20),
        cost_estimate=pl.CostEstimate(
            flops=2 * rows * keys * groups * wide,
            bytes_accessed=2 * (rows + keys) * groups * wide + 6 * rows * keys,
            transcendentals=0,
        ),
        name="final_scores",
    )(codes, slots, masked, pick, half, *pieces, total, total)


def per_device(samples, coarse_label, fine_label, live_rows, old_centroids):
    groups = lax.axis_size("coarse")
    members = lax.axis_size("member")
    z = lax.axis_index("coarse")
    me = lax.axis_index("member")
    core = me & 1
    rows, width = samples.shape
    keys = old_centroids.shape[1]
    share = keys // members
    columns = streams_of(width)
    streams = range(len(columns))
    half_keys = groups * keys // 2
    blocks = half_keys // share
    outer_bits = groups.bit_length() - 1
    turned = orders_of(groups, members)
    stages = len(turned[0, 0])
    base = 256 // (groups * members // 2) + 1
    digits = 1
    while base**digits <= 2 * rows:
        digits += 1

    live = jnp.arange(rows, dtype=jnp.int32) < live_rows[0]
    label = jnp.where(live, coarse_label[:, 0] * keys + fine_label, -1)
    sibling = lambda a: exchange(a, lambda gz, m: (gz, m ^ 1), groups, members)
    other_samples = sibling(samples)
    label_all = jnp.concatenate([label, sibling(label)])

    group_of = label_all // keys
    fine = label_all % keys
    owner = fine // share
    mine = (label_all >= 0) & ((owner & 1) == core)

    def of_core(make):
        return jnp.where(core == 0, make(0), make(1))

    def pairing(stage, stream):
        def partner(gz, m):
            group_mask, member_mask = turned[m & 1, stream][stage]
            return gz ^ group_mask, m ^ member_mask

        return partner

    tail = pad_rows(blocks)
    token = jnp.zeros((8, 128), F32)
    rows_of, tiles = [], []
    for stream, (start, wide) in enumerate(columns):
        place = of_core(
            lambda c: block_position(group_of ^ z, owner ^ me, turned[c, stream], outer_bits)
        )
        rows_of.append(jnp.where(mine, place * share + fine % share, -1)[None, :])
        tile = None
        if stream == 0:
            in_block = (jnp.where(mine, place, -1)[:, None] == jnp.arange(tail)[None, :]).astype(BF16)
            in_lane = ((fine % share)[:, None] == jnp.arange(share)[None, :]).astype(BF16)
            counted = lax.dot_general(
                in_block, in_lane, (((0,), (0,)), ((), ())), preferred_element_type=F32
            ).astype(jnp.int32)
            tile = [(counted // base**digit) % base for digit in range(digits)]
            tile = jnp.concatenate(tile, axis=1).astype(BF16)
            tile = jnp.pad(tile, ((0, 0), (0, wide - digits * share)))
        tiles.append(tile)

    half_keys //= 2
    send, keep = [None] * 2, [None] * 2
    for part, found in enumerate((send, keep)):
        for stream, (start, wide) in enumerate(columns):
            found[stream], token = key_sums(
                token, rows_of[stream], samples, other_samples, tiles[stream], part * half_keys, half_keys, start, wide
            )

    gid = jnp.where(live, coarse_label[:, 0], -1)[:, None]
    *masked, pick, token = small_call(
        functools.partial(mask_kernel, groups, columns),
        "mask",
        [jax.ShapeDtypeStruct((rows, groups * wide), BF16) for _, wide in columns]
        + [jax.ShapeDtypeStruct((rows, TILE), BF16)],
        token,
        gid,
        samples,
    )

    old_share = lax.dynamic_slice(old_centroids[0], (me * share, 0), (share, width))

    def bf(count, stream, tailed):
        rows_out = count * share + (tail if stream == tailed else 0)
        return jax.ShapeDtypeStruct((rows_out, columns[stream][1]), BF16)

    share_f32 = [jax.ShapeDtypeStruct((share, wide), F32) for _, wide in columns]
    held, fresh, near = [None] * 2, [None] * 2, [None] * 2
    count = blocks // 2
    for stage in range(stages - 1):
        for stream, (start, wide) in enumerate(columns):
            got = exchange(send[stream], pairing(stage, stream), groups, members)
            if stage < stages - 2:
                send[stream], keep[stream], token = small_call(
                    functools.partial(fold_kernel, count // 2 * share, count),
                    "fold",
                    [bf(count // 2, stream, 0)] * 2,
                    token,
                    got,
                    keep[stream],
                )
            else:
                send[stream], near[stream], token = small_call(
                    functools.partial(seed_kernel, share, count),
                    "seed",
                    [bf(2, stream, 0), share_f32[stream]],
                    token,
                    got,
                    keep[stream],
                    old_share[:, start : start + wide],
                )
        count //= 2
    column = jax.ShapeDtypeStruct((2 * share, 1), F32)
    for stream in streams:
        got = exchange(send[stream], pairing(stages - 1, stream), groups, members)
        if stream == 0:
            fresh[0], held[0], scale, norm, token = small_call(
                functools.partial(first_kernel, share, base, digits),
                "first_centroids",
                [share_f32[0], bf(2, 0, 1), column, column],
                token,
                got,
                send[0],
                near[0],
            )
        else:
            fresh[1], held[1], token = small_call(
                functools.partial(last_kernel, share, tail),
                "last_centroids",
                [share_f32[1], bf(2, 1, 1)],
                token,
                got,
                send[1],
                near[1],
                scale,
                norm,
            )
    count = 2
    arrived = [None] * 2
    for stage in reversed(range(stages - 1)):
        for stream in streams:
            got = exchange(held[stream], pairing(stage, stream), groups, members)
            if stage:
                held[stream], token = small_call(
                    functools.partial(join_kernel, count * share, count),
                    "join",
                    [bf(2 * count, stream, 1)],
                    token,
                    got,
                    held[stream],
                )
            else:
                arrived[stream] = got
        count *= 2

    half_blocks = blocks // 2

    def codes_of(stream, part, flip):
        codes = []
        for block in range(half_blocks):
            rel = [relative_of(part * half_blocks + block, turned[c, stream]) for c in range(2)]
            holder = core ^ flip
            group_rel = jnp.where(holder == 0, rel[0][0], rel[1][0])
            member_rel = jnp.where(holder == 0, rel[0][1], rel[1][1])
            codes.append((z ^ group_rel) * members + (me ^ flip ^ member_rel))
        return jnp.stack(codes).astype(jnp.int32)

    total = None
    for part, piece in ((1, held[0]), (0, arrived[0])):
        group_codes = jnp.concatenate([codes_of(0, part, flip) for flip in range(2)]) // members
        total, token = part_scores(
            token, masked[0], group_codes, [piece, sibling(piece)], total, groups, keys, share
        )

    every = jnp.arange(members, dtype=jnp.int32)
    flip_of = (every ^ me) & 1
    spot = jnp.where(
        (core ^ flip_of) == 0,
        *(block_position(jnp.zeros_like(every), every ^ me, turned[c, 0], outer_bits) // groups for c in range(2)),
    )
    quarter = half_blocks // groups
    slots = jnp.where(spot >= quarter, spot - quarter, spot + 2 * quarter) + flip_of * quarter
    flat = [piece for got in (arrived[1], held[1]) for piece in (got, sibling(got))]
    codes = jnp.concatenate([codes_of(1, part, flip) for part in range(2) for flip in range(2)])
    half = jnp.zeros((TILE, keys), F32)
    if share < 128:
        norm_rows = []
        for piece in flat:
            norm_rows.append(piece[half_blocks * share + tail - half_blocks :].astype(F32))
        norm_rows = jnp.concatenate(norm_rows)
        spread = (codes[None, :] == jnp.arange(groups * members, dtype=jnp.int32)[:, None]).astype(F32)
        for term in range(PARTS):
            found = jnp.dot(
                spread, norm_rows[:, term * share : (term + 1) * share], precision=lax.Precision.HIGHEST
            )
            half = half.at[term * groups : (term + 1) * groups].set(found.reshape(groups, keys))
        lane = jnp.arange(keys, dtype=jnp.int32)
        source = jnp.repeat(slots, share) * share + lane % share
        move = (lane[:, None] == source[None, :]).astype(F32)
        total = jnp.dot(total, move, precision=lax.Precision.HIGHEST)
        slots = jnp.arange(keys // 128, dtype=jnp.int32)
    scores = final_scores(masked[1], pick, codes, slots, flat, total, half, groups, keys, share)
    return scores, jnp.concatenate(fresh, axis=1)[None]


def solution(mesh):
    return jax.shard_map(
        per_device,
        mesh=mesh,
        in_specs=(
            P(AXES, None),
            P(AXES, None),
            P(AXES),
            P(AXES),
            P("coarse", None, None),
        ),
        out_specs=(P(AXES, None), P("coarse", "member", None)),
        check_vma=False,
    )
```

```python
import functools

import jax
import jax.numpy as jnp
from jax import lax
from jax.experimental import pallas as pl
from jax.experimental.pallas import tpu as pltpu
from jax.sharding import PartitionSpec as P

AXES = ("coarse", "member")
TILE = 16
PRIOR = 16.0
PARTS = 2
F32 = jnp.float32
BF16 = jnp.bfloat16


def pad_rows(blocks):
    return max(TILE, -(-blocks // TILE) * TILE)


def streams_of(width):
    wide = width // 2
    return ((0, wide), (wide, wide))


def orders_of(groups, members):
    inner = [(0, 1 << bit) for bit in range(1, members.bit_length() - 1)]
    outer = [((1 << (bit + 1)) - 1, 0) for bit in range(groups.bit_length() - 1)]
    cut = len(inner) // 2
    other = inner[cut:] + inner[:cut]
    found = {}
    found[0, 0] = inner + outer
    found[1, 0] = other[:cut] + outer[:1] + other[cut:] + outer[1:]
    found[0, 1] = outer[:1] + inner + outer[1:]
    found[1, 1] = inner + outer
    return found


def exchange(array, partner, groups, members):
    pairs = []
    for z in range(groups):
        for m in range(members):
            to_z, to_m = partner(z, m)
            pairs.append((z * members + m, to_z * members + to_m))
    return lax.ppermute(array, AXES, pairs)


def coefficients(group_rel, member_rel, dims, outer_bits):
    out = []
    for group_mask, member_mask in dims:
        if member_mask:
            out.append((member_rel >> (member_mask.bit_length() - 1)) & 1)
        else:
            top = group_mask.bit_length() - 1
            bit = (group_rel >> top) & 1
            if top + 1 < outer_bits:
                bit = bit ^ ((group_rel >> (top + 1)) & 1)
            out.append(bit)
    return out


def block_position(group_rel, member_rel, dims, outer_bits):
    place = 0
    for bit in coefficients(group_rel, member_rel, dims, outer_bits):
        place = place * 2 + (1 - bit)
    return place


def relative_of(place, dims):
    group_rel = member_rel = 0
    for at, (group_mask, member_mask) in enumerate(dims):
        if not (place >> (len(dims) - 1 - at)) & 1:
            group_rel ^= group_mask
            member_rel ^= member_mask
    return group_rel, member_rel


def token_shape():
    return jax.ShapeDtypeStruct((8, 128), F32)


def hand_on(kernel, inputs):
    def run(*refs):
        kernel(*refs[:inputs], *refs[inputs + 1 : -1])
        refs[-1][...] = refs[inputs][...]

    return run


def sums_kernel(base, pos_ref, own_ref, other_ref, *rest):
    out_ref = rest[-1]
    rows = own_ref.shape[0]
    keys = out_ref.shape[0] - (rest[0].shape[0] if len(rest) > 1 else 0)
    key = lax.broadcasted_iota(jnp.int32, (keys, rows), 0) + base
    first = jnp.where(pos_ref[:, :rows] == key, 1.0, 0.0).astype(BF16)
    second = jnp.where(pos_ref[:, rows:] == key, 1.0, 0.0).astype(BF16)
    total = jnp.dot(first, own_ref[...], preferred_element_type=F32)
    total += jnp.dot(second, other_ref[...], preferred_element_type=F32)
    out_ref[:keys, :] = total.astype(BF16)
    if len(rest) > 1:
        out_ref[keys:, :] = rest[0][...]


def key_sums(token, pos_row, own, other, count_tile, base, keys, start, wide):
    rows = own.shape[0]
    extra = [] if count_tile is None else [count_tile]
    out_rows = keys + sum(e.shape[0] for e in extra)
    whole = lambda shape: pl.BlockSpec(shape, lambda i: (0, 0))
    return pl.pallas_call(
        hand_on(functools.partial(sums_kernel, base), 3 + len(extra)),
        grid=(1,),
        out_shape=[jax.ShapeDtypeStruct((out_rows, wide), BF16), token_shape()],
        in_specs=[
            whole((1, 2 * rows)),
            pl.BlockSpec((rows, wide), lambda i: (0, start // wide)),
            pl.BlockSpec((rows, wide), lambda i: (0, start // wide)),
        ]
        + [whole(e.shape) for e in extra]
        + [whole(token.shape)],
        out_specs=[whole((out_rows, wide)), whole(token.shape)],
        compiler_params=pltpu.CompilerParams(vmem_limit_bytes=16 << 20),
        cost_estimate=pl.CostEstimate(
            flops=2 * keys * 2 * rows * wide, bytes_accessed=(4 * rows + 2 * keys) * wide, transcendentals=0
        ),
        name="key_sums",
    )(pos_row, own, other, *extra, token)


def small_call(kernel, name, outs, token, *args):
    whole = pl.BlockSpec(memory_space=pltpu.VMEM)
    moved = sum(a.size * a.dtype.itemsize for a in (*args, *outs))
    return pl.pallas_call(
        hand_on(kernel, len(args)),
        out_shape=[*outs, token_shape()],
        in_specs=[whole] * (len(args) + 1),
        out_specs=[whole] * (len(outs) + 1),
        compiler_params=pltpu.CompilerParams(vmem_limit_bytes=12 << 20),
        cost_estimate=pl.CostEstimate(flops=moved // 2, bytes_accessed=moved, transcendentals=0),
        name=name,
    )(*args, token)


def add_pair(got_ref, keep_ref, start, stop):
    return got_ref[start:stop, :].astype(F32) + keep_ref[start:stop, :].astype(F32)


def add_tail(got_ref, keep_ref, body, shift):
    kept = keep_ref[body:, :].astype(F32)
    return (kept + pltpu.roll(got_ref[body:, :].astype(F32), shift, 0)).astype(BF16)


def fold_kernel(half, shift, got_ref, keep_ref, send_out, keep_out):
    send_out[:half, :] = add_pair(got_ref, keep_ref, 0, half).astype(BF16)
    keep_out[:half, :] = add_pair(got_ref, keep_ref, half, 2 * half).astype(BF16)
    if got_ref.shape[0] > 2 * half:
        tail = add_tail(got_ref, keep_ref, 2 * half, shift)
        send_out[half:, :] = tail
        keep_out[half:, :] = tail


def seed_kernel(share, shift, got_ref, keep_ref, old_ref, send_out, near_out):
    two = 2 * share
    near = add_pair(got_ref, keep_ref, share, two) + PRIOR * old_ref[...]
    near_out[...] = near
    send_out[:share, :] = add_pair(got_ref, keep_ref, 0, share).astype(BF16)
    send_out[share:two, :] = near.astype(BF16)
    if got_ref.shape[0] > two:
        send_out[two:, :] = add_tail(got_ref, keep_ref, two, shift)


def summed(share, block, got_ref, sent_ref, near_ref):
    if block == 0:
        return sent_ref[:share, :].astype(F32) + got_ref[share : 2 * share, :].astype(F32)
    return near_ref[...] + got_ref[:share, :].astype(F32)


def square_sums(rounded):
    return jnp.sum(jnp.square(rounded.astype(F32)), axis=1, keepdims=True)


def first_kernel(share, base, digits, got_ref, sent_ref, near_ref, fresh_out, cents_out, scale_out, norm_out):
    two = 2 * share
    wide = got_ref.shape[1]
    last = sent_ref.shape[0] - two - 1
    lane = lax.broadcasted_iota(jnp.int32, (share, wide), 1)
    line = lax.broadcasted_iota(jnp.int32, (share, wide), 0)
    mine = sent_ref[two:, :].astype(F32)
    theirs = got_ref[two:, :].astype(F32)
    for block in range(2):
        row = mine[last - 1 + block : last + block, :] + theirs[last - block : last - block + 1, :]
        count = jnp.full((share, 1), PRIOR, F32)
        for digit in range(digits):
            hit = jnp.where(lane == line + digit * share, row, 0.0)
            count += jnp.sum(hit, axis=1, keepdims=True) * float(base**digit)
        scale_out[block * share : (block + 1) * share, :] = count
        fresh = summed(share, block, got_ref, sent_ref, near_ref) / count
        rounded = fresh.astype(BF16)
        cents_out[block * share : (block + 1) * share, :] = rounded
        norm_out[block * share : (block + 1) * share, :] = square_sums(rounded)
        if block == 1:
            fresh_out[...] = fresh


def last_kernel(share, tail, got_ref, sent_ref, near_ref, scale_ref, norm_ref, fresh_out, cents_out):
    two = 2 * share
    wide = got_ref.shape[1]
    lane = lax.broadcasted_iota(jnp.int32, (share, wide), 1)
    line = lax.broadcasted_iota(jnp.int32, (share, wide), 0)
    tile = jnp.zeros((tail, wide), F32)
    tile_row = lax.broadcasted_iota(jnp.int32, (tail, wide), 0)
    for block in range(2):
        part = slice(block * share, (block + 1) * share)
        fresh = summed(share, block, got_ref, sent_ref, near_ref) / scale_ref[part, :]
        rounded = fresh.astype(BF16)
        cents_out[part, :] = rounded
        if block == 1:
            fresh_out[...] = fresh
        norm = 0.5 * (norm_ref[part, :] + square_sums(rounded))
        spread = jnp.zeros((1, wide), F32)
        for term_at in range(PARTS):
            term = norm.astype(BF16).astype(F32)
            norm = norm - term
            hit = jnp.where(lane == line + term_at * share, term, 0.0)
            spread += jnp.sum(hit, axis=0, keepdims=True)
        tile = jnp.where(tile_row == tail - 2 + block, spread, tile)
    cents_out[two:, :] = tile.astype(BF16)


def join_kernel(body, shift, got_ref, held_ref, out_ref):
    out_ref[:body, :] = got_ref[:body, :]
    out_ref[body : 2 * body, :] = held_ref[:body, :]
    if held_ref.shape[0] > body:
        rows = held_ref.shape[0] - body
        moved = pltpu.roll(got_ref[body:, :].astype(F32), rows - shift, 0)
        out_ref[2 * body :, :] = (held_ref[body:, :].astype(F32) + moved).astype(BF16)


def pass_kernel(in_ref, out_ref):
    out_ref[...] = in_ref[...]


def mask_kernel(groups, columns, gid_ref, x_ref, *outs):
    gid = gid_ref[...]
    for (start, wide), out in zip(columns, outs):
        x = x_ref[:, start : start + wide]
        for group in range(groups):
            out[:, group * wide : (group + 1) * wide] = jnp.where(gid == group, x, jnp.zeros_like(x))
    pick = outs[-1]
    lane = lax.broadcasted_iota(jnp.int32, pick.shape, 1)
    hit = (lane % groups == gid) & (lane < PARTS * groups)
    pick[...] = jnp.where(hit, -1.0, 0.0).astype(BF16)


def product(a, b):
    return lax.dot_general(a, b, (((1,), (1,)), ((), ())), preferred_element_type=F32)


def part_kernel(groups, share, code_ref, masked_ref, own_ref, other_ref, *rest):
    out_ref, cents = rest[-2:]
    wide = own_ref.shape[1]
    blocks = own_ref.shape[0] // share

    @pl.when(pl.program_id(0) == 0)
    def _():
        for piece, ref in enumerate((own_ref, other_ref)):
            for block in range(blocks):
                code = code_ref[piece * blocks + block]
                slot = pl.multiple_of(code // groups * share, share)
                cents[pl.ds(slot, share), pl.ds(pl.multiple_of(code % groups * wide, 128), wide)] = ref[block * share : (block + 1) * share, :]

    step = out_ref.shape[1]
    start = pl.multiple_of(pl.program_id(0) * step, step)
    out_ref[...] = product(masked_ref[...], cents[pl.ds(start, step), :])


def part_scores(token, masked, codes, pieces, before, groups, keys, share):
    rows = masked.shape[0]
    wide = pieces[0].shape[1]
    half = pieces[0].shape[0] * len(pieces) // groups
    step = min(256, half)
    steps = half // step
    at = 0 if before is None else steps
    whole = pl.BlockSpec(memory_space=pltpu.VMEM)
    extra = [] if before is None else [before]

    def kernel(code_ref, *refs):
        count = 3 + len(extra)
        part_kernel(groups, share, code_ref, *refs[:3], refs[count + 1], refs[-1])
        refs[count + 2][...] = refs[count][...]

    return pl.pallas_call(
        kernel,
        grid_spec=pltpu.PrefetchScalarGridSpec(
            num_scalar_prefetch=1,
            grid=(steps,),
            in_specs=[whole] * 3 + [pl.BlockSpec(memory_space=pl.ANY)] * len(extra) + [whole],
            out_specs=[pl.BlockSpec((rows, step), lambda i, w: (0, i + at)), whole],
            scratch_shapes=[pltpu.VMEM((half, groups * wide), BF16)],
        ),
        out_shape=[jax.ShapeDtypeStruct((rows, keys), F32), token_shape()],
        input_output_aliases={} if before is None else {4: 0},
        compiler_params=pltpu.CompilerParams(vmem_limit_bytes=16 << 20),
        cost_estimate=pl.CostEstimate(flops=1, bytes_accessed=1, transcendentals=0),
        name="part_scores",
    )(codes, masked, *pieces, *extra, token)


def final_kernel(groups, share, code_ref, slot_ref, masked_ref, pick_ref, half_ref, *rest):
    pieces = 4
    piece_refs, total_refs = rest[:pieces], rest[pieces : pieces + 2]
    out_ref, cents, half = rest[-3:]
    keys = cents.shape[0]
    wide = cents.shape[1] // groups
    members = keys // share
    blocks = code_ref.shape[0] // pieces
    lanes = 128

    @pl.when(pl.program_id(0) == 0)
    def _():
        half[...] = half_ref[...]
        for piece, ref in enumerate(piece_refs):
            for block in range(blocks):
                code = code_ref[piece * blocks + block]
                group = code // members
                row_at = pl.multiple_of((code % members) * share, share)
                cents[pl.ds(row_at, share), pl.ds(pl.multiple_of(group * wide, lanes), wide)] = ref[
                    block * share : (block + 1) * share, :
                ]
                if share >= lanes:
                    tail = ref[blocks * share :, :].astype(F32)
                    at = tail.shape[0] - blocks + block
                    lines = pl.ds(pl.multiple_of(row_at, lanes), share)
                    line = lax.broadcasted_iota(jnp.int32, (half.shape[0], share), 0)
                    filled = half[:, lines]
                    for term in range(PARTS):
                        row = tail[at : at + 1, term * share : (term + 1) * share]
                        filled = jnp.where(line == group + term * groups, row, filled)
                    half[:, lines] = filled

    step = out_ref.shape[1]
    start = pl.multiple_of(pl.program_id(0) * step, step)
    dots = product(masked_ref[...], cents[pl.ds(start, step), :])
    offsets = half[:, pl.ds(start, step)].astype(BF16)
    dots += jnp.dot(pick_ref[...], offsets, preferred_element_type=F32)
    cut = step // 2
    out_ref[:, :cut] = (dots[:, :cut] + total_refs[0][...]).astype(BF16)
    out_ref[:, cut:] = (dots[:, cut:] + total_refs[1][...]).astype(BF16)


def final_scores(masked, pick, codes, slots, pieces, total, half, groups, keys, share):
    rows = masked.shape[0]
    wide = pieces[0].shape[1]
    step = min(256, keys)
    cut = step // 2
    whole = pl.BlockSpec(memory_space=pltpu.VMEM)
    return pl.pallas_call(
        functools.partial(final_kernel, groups, share),
        grid_spec=pltpu.PrefetchScalarGridSpec(
            num_scalar_prefetch=2,
            grid=(keys // step,),
            in_specs=[whole] * (3 + len(pieces))
            + [
                pl.BlockSpec((rows, cut), lambda i, c, s: (0, s[2 * i])),
                pl.BlockSpec((rows, cut), lambda i, c, s: (0, s[2 * i + 1])),
            ],
            out_specs=pl.BlockSpec((rows, step), lambda i, c, s: (0, i)),
            scratch_shapes=[pltpu.VMEM((keys, groups * wide), BF16), pltpu.VMEM(half.shape, F32)],
        ),
        out_shape=jax.ShapeDtypeStruct((rows, keys), BF16),
        compiler_params=pltpu.CompilerParams(vmem_limit_bytes=16 << 20),
        cost_estimate=pl.CostEstimate(flops=1, bytes_accessed=1, transcendentals=0),
        name="final_scores",
    )(codes, slots, masked, pick, half, *pieces, total, total)


def per_device(samples, coarse_label, fine_label, live_rows, old_centroids):
    groups = lax.axis_size("coarse")
    members = lax.axis_size("member")
    z = lax.axis_index("coarse")
    me = lax.axis_index("member")
    core = me & 1
    rows, width = samples.shape
    keys = old_centroids.shape[1]
    share = keys // members
    columns = streams_of(width)
    streams = range(len(columns))
    half_keys = groups * keys // 2
    blocks = half_keys // share
    outer_bits = groups.bit_length() - 1
    turned = orders_of(groups, members)
    stages = len(turned[0, 0])
    base = 256 // (groups * members // 2) + 1
    digits = 1
    while base**digits <= 2 * rows:
        digits += 1

    live = jnp.arange(rows, dtype=jnp.int32) < live_rows[0]
    label = jnp.where(live, coarse_label[:, 0] * keys + fine_label, -1)
    sibling = lambda a: exchange(a, lambda gz, m: (gz, m ^ 1), groups, members)
    other_samples = sibling(samples)
    label_all = jnp.concatenate([label, sibling(label)])

    group_of = label_all // keys
    fine = label_all % keys
    owner = fine // share
    mine = (label_all >= 0) & ((owner & 1) == core)

    def of_core(make):
        return jnp.where(core == 0, make(0), make(1))

    def pairing(stage, stream):
        def partner(gz, m):
            group_mask, member_mask = turned[m & 1, stream][stage]
            return gz ^ group_mask, m ^ member_mask

        return partner

    tail = pad_rows(blocks)
    token = start_token = jnp.zeros((8, 128), F32)
    rows_of, tiles = [], []
    for stream, (start, wide) in enumerate(columns):
        place = of_core(
            lambda c: block_position(group_of ^ z, owner ^ me, turned[c, stream], outer_bits)
        )
        rows_of.append(jnp.where(mine, place * share + fine % share, -1)[None, :])
        tile = None
        if stream == 0:
            in_block = (jnp.where(mine, place, -1)[:, None] == jnp.arange(tail)[None, :]).astype(BF16)
            in_lane = ((fine % share)[:, None] == jnp.arange(share)[None, :]).astype(BF16)
            counted = lax.dot_general(
                in_block, in_lane, (((0,), (0,)), ((), ())), preferred_element_type=F32
            ).astype(jnp.int32)
            tile = [(counted // base**digit) % base for digit in range(digits)]
            tile = jnp.concatenate(tile, axis=1).astype(BF16)
            tile = jnp.pad(tile, ((0, 0), (0, wide - digits * share)))
        tiles.append(tile)

    half_keys //= 2
    send, keep = [None] * 2, [None] * 2
    for part, found in enumerate((send, keep)):
        for stream, (start, wide) in enumerate(columns):
            found[stream], token = key_sums(
                token, rows_of[stream], samples, other_samples, tiles[stream], part * half_keys, half_keys, start, wide
            )

    tokens = [start_token] * 2
    pick_token = lambda stream: tokens[1 - stream]
    old_share = lax.dynamic_slice(old_centroids[0], (me * share, 0), (share, width))

    def bf(count, stream, tailed):
        rows_out = count * share + (tail if stream == tailed else 0)
        return jax.ShapeDtypeStruct((rows_out, columns[stream][1]), BF16)

    share_f32 = [jax.ShapeDtypeStruct((share, wide), F32) for _, wide in columns]
    held, fresh, near = [None] * 2, [None] * 2, [None] * 2
    count = blocks // 2
    for stage in range(stages - 1):
        for stream, (start, wide) in enumerate(columns):
            got = exchange(send[stream], pairing(stage, stream), groups, members)
            if stage < stages - 2:
                send[stream], keep[stream], tokens[stream] = small_call(
                    functools.partial(fold_kernel, count // 2 * share, count),
                    "fold",
                    [bf(count // 2, stream, 0)] * 2,
                    pick_token(stream),
                    got,
                    keep[stream],
                )
            else:
                send[stream], near[stream], tokens[stream] = small_call(
                    functools.partial(seed_kernel, share, count),
                    "seed",
                    [bf(2, stream, 0), share_f32[stream]],
                    pick_token(stream),
                    got,
                    keep[stream],
                    old_share[:, start : start + wide],
                )
        count //= 2
    column = jax.ShapeDtypeStruct((2 * share, 1), F32)
    for stream in streams:
        got = exchange(send[stream], pairing(stages - 1, stream), groups, members)
        if stream == 0:
            fresh[0], held[0], scale, norm, tokens[stream] = small_call(
                functools.partial(first_kernel, share, base, digits),
                "first_centroids",
                [share_f32[0], bf(2, 0, 1), column, column],
                pick_token(stream),
                got,
                send[0],
                near[0],
            )
        else:
            fresh[1], held[1], tokens[stream] = small_call(
                functools.partial(last_kernel, share, tail),
                "last_centroids",
                [share_f32[1], bf(2, 1, 1)],
                pick_token(stream),
                got,
                send[1],
                near[1],
                scale,
                norm,
            )
    count = 2
    arrived = [None] * 2
    for stage in reversed(range(stages - 1)):
        for stream in streams:
            got = exchange(held[stream], pairing(stage, stream), groups, members)
            if stage:
                held[stream], tokens[stream] = small_call(
                    functools.partial(join_kernel, count * share, count),
                    "join",
                    [bf(2 * count, stream, 1)],
                    pick_token(stream),
                    got,
                    held[stream],
                )
            else:
                arrived[stream] = got
        count *= 2

    half_blocks = blocks // 2

    def codes_of(stream, part, flip):
        codes = []
        for block in range(half_blocks):
            rel = [relative_of(part * half_blocks + block, turned[c, stream]) for c in range(2)]
            holder = core ^ flip
            group_rel = jnp.where(holder == 0, rel[0][0], rel[1][0])
            member_rel = jnp.where(holder == 0, rel[0][1], rel[1][1])
            codes.append((z ^ group_rel) * members + (me ^ flip ^ member_rel))
        return jnp.stack(codes).astype(jnp.int32)

    gid = jnp.where(live, coarse_label[:, 0], -1)[:, None]
    *masked, pick, token = small_call(
        functools.partial(mask_kernel, groups, columns),
        "mask",
        [jax.ShapeDtypeStruct((rows, groups * wide), BF16) for _, wide in columns]
        + [jax.ShapeDtypeStruct((rows, TILE), BF16)],
        token,
        gid,
        samples,
    )

    quarter = half_blocks // groups
    inner_of = [[dim for dim in turned[c, 0] if dim[1]] for c in range(2)]
    total = None
    for part, piece in ((1, held[0]), (0, arrived[0])):
        part_codes = []
        for flip in range(2):
            for block in range(half_blocks):
                code = []
                for c in range(2):
                    group_rel, member_rel = relative_of(part * half_blocks + block, turned[c, 0])
                    spot = block_position(0, member_rel, inner_of[c], outer_bits) % quarter
                    code.append((spot + flip * quarter) * groups + (z ^ group_rel))
                part_codes.append(jnp.where(core ^ flip == 0, *code))
        total, token = part_scores(
            token, masked[0], jnp.stack(part_codes).astype(jnp.int32), [piece, sibling(piece)], total, groups, keys, share
        )

    last, token = small_call(
        pass_kernel, "pass", [jax.ShapeDtypeStruct(arrived[1].shape, BF16)], token, arrived[1]
    )
    every = jnp.arange(members, dtype=jnp.int32)
    flip_of = (every ^ me) & 1
    spot = jnp.where(
        (core ^ flip_of) == 0,
        *(block_position(0, every ^ me, inner_of[c], outer_bits) for c in range(2)),
    )
    slots = jnp.where(spot >= quarter, spot - quarter, spot + 2 * quarter) + flip_of * quarter
    flat = [piece for got in (last, held[1]) for piece in (got, sibling(got))]
    codes = jnp.concatenate([codes_of(1, part, flip) for part in range(2) for flip in range(2)])
    half = jnp.zeros((TILE, keys), F32)
    if share < 128:
        norm_rows = []
        for piece in flat:
            norm_rows.append(piece[half_blocks * share + tail - half_blocks :].astype(F32))
        norm_rows = jnp.concatenate(norm_rows)
        spread = (codes[None, :] == jnp.arange(groups * members, dtype=jnp.int32)[:, None]).astype(F32)
        for term in range(PARTS):
            found = jnp.dot(
                spread, norm_rows[:, term * share : (term + 1) * share], precision=lax.Precision.HIGHEST
            )
            half = half.at[term * groups : (term + 1) * groups].set(found.reshape(groups, keys))
        lane = jnp.arange(keys, dtype=jnp.int32)
        source = jnp.repeat(slots, share) * share + lane % share
        move = (lane[:, None] == source[None, :]).astype(F32)
        total = jnp.dot(total, move, precision=lax.Precision.HIGHEST)
        slots = jnp.arange(keys // 128, dtype=jnp.int32)
    scores = final_scores(masked[1], pick, codes, slots, flat, total, half, groups, keys, share)
    return scores, jnp.concatenate(fresh, axis=1)[None]


def solution(mesh):
    return jax.shard_map(
        per_device,
        mesh=mesh,
        in_specs=(
            P(AXES, None),
            P(AXES, None),
            P(AXES),
            P(AXES),
            P("coarse", None, None),
        ),
        out_specs=(P(AXES, None), P("coarse", "member", None)),
        check_vma=False,
    )
```

```python
import functools

import jax
import jax.numpy as jnp
from jax import lax
from jax.experimental import pallas as pl
from jax.experimental.pallas import tpu as pltpu
from jax.sharding import PartitionSpec as P

AXES = ("coarse", "member")
TILE = 16
PRIOR = 16.0
PARTS = 2
F32 = jnp.float32
BF16 = jnp.bfloat16


def pad_rows(blocks):
    return max(TILE, -(-blocks // TILE) * TILE)


def streams_of(width):
    wide = width // 2
    return ((0, wide), (wide, wide))


def orders_of(groups, members):
    inner = [(0, 1 << bit) for bit in range(1, members.bit_length() - 1)]
    outer = [((1 << (bit + 1)) - 1, 0) for bit in range(groups.bit_length() - 1)]
    cut = len(inner) // 2
    other = inner[cut:] + inner[:cut]
    found = {}
    found[0, 0] = inner + outer
    found[1, 0] = other[:cut] + outer[:1] + other[cut:] + outer[1:]
    found[0, 1] = outer[:1] + inner + outer[1:]
    found[1, 1] = inner + outer
    return found


def exchange(array, partner, groups, members):
    pairs = []
    for z in range(groups):
        for m in range(members):
            to_z, to_m = partner(z, m)
            pairs.append((z * members + m, to_z * members + to_m))
    return lax.ppermute(array, AXES, pairs)


def coefficients(group_rel, member_rel, dims, outer_bits):
    out = []
    for group_mask, member_mask in dims:
        if member_mask:
            out.append((member_rel >> (member_mask.bit_length() - 1)) & 1)
        else:
            top = group_mask.bit_length() - 1
            bit = (group_rel >> top) & 1
            if top + 1 < outer_bits:
                bit = bit ^ ((group_rel >> (top + 1)) & 1)
            out.append(bit)
    return out


def block_position(group_rel, member_rel, dims, outer_bits):
    place = 0
    for bit in coefficients(group_rel, member_rel, dims, outer_bits):
        place = place * 2 + (1 - bit)
    return place


def relative_of(place, dims):
    group_rel = member_rel = 0
    for at, (group_mask, member_mask) in enumerate(dims):
        if not (place >> (len(dims) - 1 - at)) & 1:
            group_rel ^= group_mask
            member_rel ^= member_mask
    return group_rel, member_rel


def token_shape():
    return jax.ShapeDtypeStruct((8, 128), F32)


def hand_on(kernel, inputs):
    def run(*refs):
        kernel(*refs[:inputs], *refs[inputs + 1 : -1])
        refs[-1][...] = refs[inputs][...]

    return run


def sums_kernel(base, pos_ref, own_ref, other_ref, *rest):
    out_ref = rest[-1]
    rows = own_ref.shape[0]
    keys = out_ref.shape[0] - (rest[0].shape[0] if len(rest) > 1 else 0)
    key = lax.broadcasted_iota(jnp.int32, (keys, rows), 0) + base
    first = jnp.where(pos_ref[:, :rows] == key, 1.0, 0.0).astype(BF16)
    second = jnp.where(pos_ref[:, rows:] == key, 1.0, 0.0).astype(BF16)
    total = jnp.dot(first, own_ref[...], preferred_element_type=F32)
    total += jnp.dot(second, other_ref[...], preferred_element_type=F32)
    out_ref[:keys, :] = total.astype(BF16)
    if len(rest) > 1:
        out_ref[keys:, :] = rest[0][...]


def key_sums(token, pos_row, own, other, count_tile, base, keys, start, wide):
    rows = own.shape[0]
    extra = [] if count_tile is None else [count_tile]
    out_rows = keys + sum(e.shape[0] for e in extra)
    whole = lambda shape: pl.BlockSpec(shape, lambda i: (0, 0))
    return pl.pallas_call(
        hand_on(functools.partial(sums_kernel, base), 3 + len(extra)),
        grid=(1,),
        out_shape=[jax.ShapeDtypeStruct((out_rows, wide), BF16), token_shape()],
        in_specs=[
            whole((1, 2 * rows)),
            pl.BlockSpec((rows, wide), lambda i: (0, start // wide)),
            pl.BlockSpec((rows, wide), lambda i: (0, start // wide)),
        ]
        + [whole(e.shape) for e in extra]
        + [whole(token.shape)],
        out_specs=[whole((out_rows, wide)), whole(token.shape)],
        compiler_params=pltpu.CompilerParams(vmem_limit_bytes=16 << 20),
        cost_estimate=pl.CostEstimate(
            flops=2 * keys * 2 * rows * wide, bytes_accessed=(4 * rows + 2 * keys) * wide, transcendentals=0
        ),
        name="key_sums",
    )(pos_row, own, other, *extra, token)


def small_call(kernel, name, outs, token, *args, scalars=0, limit=4):
    whole = pl.BlockSpec(memory_space=pltpu.VMEM)
    moved = sum(a.size * a.dtype.itemsize for a in (*args, *outs))
    return pl.pallas_call(
        hand_on(kernel, len(args)),
        out_shape=[*outs, token_shape()],
        in_specs=[pl.BlockSpec(memory_space=pltpu.SMEM)] * scalars + [whole] * (len(args) + 1 - scalars),
        out_specs=[whole if limit < 16 else pl.BlockSpec()] * len(outs) + [whole],
        compiler_params=pltpu.CompilerParams(vmem_limit_bytes=limit << 20),
        cost_estimate=pl.CostEstimate(flops=moved // 2, bytes_accessed=moved, transcendentals=0),
        name=name,
    )(*args, token)


def add_pair(got_ref, keep_ref, start, stop):
    return got_ref[start:stop, :].astype(F32) + keep_ref[start:stop, :].astype(F32)


def add_tail(got_ref, keep_ref, body, shift):
    kept = keep_ref[body:, :].astype(F32)
    return (kept + pltpu.roll(got_ref[body:, :].astype(F32), shift, 0)).astype(BF16)


def fold_kernel(half, shift, got_ref, keep_ref, send_out, keep_out):
    send_out[:half, :] = add_pair(got_ref, keep_ref, 0, half).astype(BF16)
    keep_out[:half, :] = add_pair(got_ref, keep_ref, half, 2 * half).astype(BF16)
    if got_ref.shape[0] > 2 * half:
        tail = add_tail(got_ref, keep_ref, 2 * half, shift)
        send_out[half:, :] = tail
        keep_out[half:, :] = tail


def seed_kernel(share, shift, got_ref, keep_ref, old_ref, send_out, near_out):
    two = 2 * share
    near = add_pair(got_ref, keep_ref, share, two) + PRIOR * old_ref[...]
    near_out[...] = near
    send_out[:share, :] = add_pair(got_ref, keep_ref, 0, share).astype(BF16)
    send_out[share:two, :] = near.astype(BF16)
    if got_ref.shape[0] > two:
        send_out[two:, :] = add_tail(got_ref, keep_ref, two, shift)


def summed(share, block, got_ref, sent_ref, near_ref):
    if block == 0:
        return sent_ref[:share, :].astype(F32) + got_ref[share : 2 * share, :].astype(F32)
    return near_ref[...] + got_ref[:share, :].astype(F32)


def square_sums(rounded):
    return jnp.sum(jnp.square(rounded.astype(F32)), axis=1, keepdims=True)


def first_kernel(share, base, digits, got_ref, sent_ref, near_ref, fresh_out, cents_out, scale_out, norm_out):
    two = 2 * share
    wide = got_ref.shape[1]
    last = sent_ref.shape[0] - two - 1
    lane = lax.broadcasted_iota(jnp.int32, (share, wide), 1)
    line = lax.broadcasted_iota(jnp.int32, (share, wide), 0)
    mine = sent_ref[two:, :].astype(F32)
    theirs = got_ref[two:, :].astype(F32)
    for block in range(2):
        row = mine[last - 1 + block : last + block, :] + theirs[last - block : last - block + 1, :]
        count = jnp.full((share, 1), PRIOR, F32)
        for digit in range(digits):
            hit = jnp.where(lane == line + digit * share, row, 0.0)
            count += jnp.sum(hit, axis=1, keepdims=True) * float(base**digit)
        scale_out[block * share : (block + 1) * share, :] = count
        fresh = summed(share, block, got_ref, sent_ref, near_ref) / count
        rounded = fresh.astype(BF16)
        cents_out[block * share : (block + 1) * share, :] = rounded
        norm_out[block * share : (block + 1) * share, :] = square_sums(rounded)
        if block == 1:
            fresh_out[...] = fresh


def last_kernel(share, tail, got_ref, sent_ref, near_ref, scale_ref, norm_ref, first_ref, fresh_out, cents_out):
    two = 2 * share
    wide = got_ref.shape[1]
    lane = lax.broadcasted_iota(jnp.int32, (share, wide), 1)
    line = lax.broadcasted_iota(jnp.int32, (share, wide), 0)
    tile = jnp.zeros((tail, wide), F32)
    tile_row = lax.broadcasted_iota(jnp.int32, (tail, wide), 0)
    for block in range(2):
        part = slice(block * share, (block + 1) * share)
        fresh = summed(share, block, got_ref, sent_ref, near_ref) / scale_ref[part, :]
        rounded = fresh.astype(BF16)
        cents_out[part, :] = rounded
        if block == 1:
            before = first_ref.shape[1]
            fresh_out[:, :before] = first_ref[...]
            fresh_out[:, before:] = fresh
        norm = 0.5 * (norm_ref[part, :] + square_sums(rounded))
        spread = jnp.zeros((1, wide), F32)
        for term_at in range(PARTS):
            term = norm.astype(BF16).astype(F32)
            norm = norm - term
            hit = jnp.where(lane == line + term_at * share, term, 0.0)
            spread += jnp.sum(hit, axis=0, keepdims=True)
        tile = jnp.where(tile_row == tail - 2 + block, spread, tile)
    cents_out[two:, :] = tile.astype(BF16)


def join_kernel(body, shift, got_ref, held_ref, out_ref):
    out_ref[:body, :] = got_ref[:body, :]
    out_ref[body : 2 * body, :] = held_ref[:body, :]
    if held_ref.shape[0] > body:
        rows = held_ref.shape[0] - body
        moved = pltpu.roll(got_ref[body:, :].astype(F32), rows - shift, 0)
        out_ref[2 * body :, :] = (held_ref[body:, :].astype(F32) + moved).astype(BF16)


def behind(array, token):
    def kernel(in_ref, token_ref, out_ref):
        del in_ref, token_ref, out_ref

    return pl.pallas_call(
        kernel,
        out_shape=jax.ShapeDtypeStruct(array.shape, array.dtype),
        in_specs=[pl.BlockSpec(memory_space=pl.ANY)] * 2,
        out_specs=pl.BlockSpec(memory_space=pl.ANY),
        input_output_aliases={0: 0},
        compiler_params=pltpu.CompilerParams(vmem_limit_bytes=1 << 20),
        cost_estimate=pl.CostEstimate(flops=1, bytes_accessed=1, transcendentals=0),
        name="behind",
    )(array, token)


def mask_kernel(groups, start, wide, live_ref, label_ref, x_ref, out_ref, *pick_out):
    row = lax.broadcasted_iota(jnp.int32, label_ref.shape, 0)
    gid = jnp.where(row < live_ref[0], label_ref[...], -1)
    x = x_ref[:, start : start + wide]
    for group in range(groups):
        out_ref[:, group * wide : (group + 1) * wide] = jnp.where(gid == group, x, jnp.zeros_like(x))
    for pick_ref in pick_out:
        lane = lax.broadcasted_iota(jnp.int32, pick_ref.shape, 1)
        hit = (lane % groups == gid) & (lane < PARTS * groups)
        pick_ref[...] = jnp.where(hit, -1.0, 0.0).astype(BF16)


def product(a, b):
    return lax.dot_general(a, b, (((1,), (1,)), ((), ())), preferred_element_type=F32)


def part_kernel(groups, share, code_ref, masked_ref, own_ref, other_ref, *rest):
    out_ref, cents = rest[-2:]
    wide = own_ref.shape[1]
    blocks = own_ref.shape[0] // share

    @pl.when(pl.program_id(0) == 0)
    def _():
        for piece, ref in enumerate((own_ref, other_ref)):
            for block in range(blocks):
                code = code_ref[piece * blocks + block]
                slot = pl.multiple_of(code // groups * share, share)
                cents[pl.ds(slot, share), pl.ds(pl.multiple_of(code % groups * wide, 128), wide)] = ref[block * share : (block + 1) * share, :]

    step = out_ref.shape[1]
    start = pl.multiple_of(pl.program_id(0) * step, step)
    out_ref[...] = product(masked_ref[...], cents[pl.ds(start, step), :])


def part_scores(token, masked, codes, pieces, before, groups, keys, share):
    rows = masked.shape[0]
    wide = pieces[0].shape[1]
    half = pieces[0].shape[0] * len(pieces) // groups
    step = min(256, half)
    steps = half // step
    at = 0 if before is None else steps
    whole = pl.BlockSpec(memory_space=pltpu.VMEM)
    extra = [] if before is None else [before]

    def kernel(code_ref, *refs):
        count = 3 + len(extra)
        part_kernel(groups, share, code_ref, *refs[:3], refs[count + 1], refs[-1])
        refs[count + 2][...] = refs[count][...]

    return pl.pallas_call(
        kernel,
        grid_spec=pltpu.PrefetchScalarGridSpec(
            num_scalar_prefetch=1,
            grid=(steps,),
            in_specs=[whole] * 3 + [pl.BlockSpec(memory_space=pl.ANY)] * len(extra) + [whole],
            out_specs=[pl.BlockSpec((rows, step), lambda i, w: (0, i + at)), whole],
            scratch_shapes=[pltpu.VMEM((half, groups * wide), BF16)],
        ),
        out_shape=[jax.ShapeDtypeStruct((rows, keys), F32), token_shape()],
        input_output_aliases={} if before is None else {4: 0},
        compiler_params=pltpu.CompilerParams(vmem_limit_bytes=46 << 20),
        cost_estimate=pl.CostEstimate(flops=1, bytes_accessed=1, transcendentals=0),
        name="part_scores",
    )(codes, masked, *pieces, *extra, token)


def final_kernel(groups, share, code_ref, slot_ref, masked_ref, pick_ref, half_ref, *rest):
    pieces = 4
    piece_refs, total_refs = rest[:pieces], rest[pieces : pieces + 2]
    out_ref, cents, half, rows_of, sem = rest[-5:]
    load = pltpu.make_async_copy(masked_ref, rows_of, sem)
    keys = cents.shape[0]
    wide = cents.shape[1] // groups
    members = keys // share
    blocks = code_ref.shape[0] // pieces
    lanes = 128

    @pl.when(pl.program_id(0) == 0)
    def _():
        load.start()
        half[...] = half_ref[...]
        for piece, ref in enumerate(piece_refs):
            for block in range(blocks):
                code = code_ref[piece * blocks + block]
                group = code // members
                row_at = pl.multiple_of((code % members) * share, share)
                cents[pl.ds(row_at, share), pl.ds(pl.multiple_of(group * wide, lanes), wide)] = ref[
                    block * share : (block + 1) * share, :
                ]
                if share >= lanes:
                    tail = ref[blocks * share :, :].astype(F32)
                    at = tail.shape[0] - blocks + block
                    lines = pl.ds(pl.multiple_of(row_at, lanes), share)
                    line = lax.broadcasted_iota(jnp.int32, (half.shape[0], share), 0)
                    filled = half[:, lines]
                    for term in range(PARTS):
                        row = tail[at : at + 1, term * share : (term + 1) * share]
                        filled = jnp.where(line == group + term * groups, row, filled)
                    half[:, lines] = filled
        load.wait()

    step = out_ref.shape[1]
    start = pl.multiple_of(pl.program_id(0) * step, step)
    dots = product(rows_of[...], cents[pl.ds(start, step), :])
    offsets = half[:, pl.ds(start, step)].astype(BF16)
    dots += jnp.dot(pick_ref[...], offsets, preferred_element_type=F32)
    cut = step // 2
    out_ref[:, :cut] = (dots[:, :cut] + total_refs[0][...]).astype(BF16)
    out_ref[:, cut:] = (dots[:, cut:] + total_refs[1][...]).astype(BF16)


def final_scores(masked, pick, codes, slots, pieces, total, half, groups, keys, share):
    rows = masked.shape[0]
    wide = pieces[0].shape[1]
    step = min(256, keys)
    cut = step // 2
    whole = pl.BlockSpec(memory_space=pltpu.VMEM)
    return pl.pallas_call(
        functools.partial(final_kernel, groups, share),
        grid_spec=pltpu.PrefetchScalarGridSpec(
            num_scalar_prefetch=2,
            grid=(keys // step,),
            in_specs=[pl.BlockSpec(memory_space=pl.ANY)]
            + [whole] * (2 + len(pieces))
            + [
                pl.BlockSpec((rows, cut), lambda i, c, s: (0, s[2 * i])),
                pl.BlockSpec((rows, cut), lambda i, c, s: (0, s[2 * i + 1])),
            ],
            out_specs=pl.BlockSpec((rows, step), lambda i, c, s: (0, i)),
            scratch_shapes=[
                pltpu.VMEM((keys, groups * wide), BF16),
                pltpu.VMEM(half.shape, F32),
                pltpu.VMEM(masked.shape, BF16),
                pltpu.SemaphoreType.DMA,
            ],
        ),
        out_shape=jax.ShapeDtypeStruct((rows, keys), BF16),
        compiler_params=pltpu.CompilerParams(vmem_limit_bytes=50 << 20),
        cost_estimate=pl.CostEstimate(flops=1, bytes_accessed=1, transcendentals=0),
        name="final_scores",
    )(codes, slots, masked, pick, half, *pieces, total, total)


def per_device(samples, coarse_label, fine_label, live_rows, old_centroids):
    groups = lax.axis_size("coarse")
    members = lax.axis_size("member")
    z = lax.axis_index("coarse")
    me = lax.axis_index("member")
    core = me & 1
    rows, width = samples.shape
    keys = old_centroids.shape[1]
    share = keys // members
    columns = streams_of(width)
    streams = range(len(columns))
    half_keys = groups * keys // 2
    blocks = half_keys // share
    outer_bits = groups.bit_length() - 1
    turned = orders_of(groups, members)
    stages = len(turned[0, 0])
    base = 256 // (groups * members // 2) + 1
    digits = 1
    while base**digits <= 2 * rows:
        digits += 1

    live = jnp.arange(rows, dtype=jnp.int32) < live_rows[0]
    label = jnp.where(live, coarse_label[:, 0] * keys + fine_label, -1)
    sibling = lambda a: exchange(a, lambda gz, m: (gz, m ^ 1), groups, members)
    other_samples = sibling(samples)
    label_all = jnp.concatenate([label, sibling(label)])

    group_of = label_all // keys
    fine = label_all % keys
    owner = fine // share
    mine = (label_all >= 0) & ((owner & 1) == core)

    def of_core(make):
        return jnp.where(core == 0, make(0), make(1))

    def pairing(stage, stream):
        def partner(gz, m):
            group_mask, member_mask = turned[m & 1, stream][stage]
            return gz ^ group_mask, m ^ member_mask

        return partner

    tail = pad_rows(blocks)
    token = start_token = jnp.zeros((8, 128), F32)
    rows_of, tiles = [], []
    for stream, (start, wide) in enumerate(columns):
        place = of_core(
            lambda c: block_position(group_of ^ z, owner ^ me, turned[c, stream], outer_bits)
        )
        rows_of.append(jnp.where(mine, place * share + fine % share, -1)[None, :])
        tile = None
        if stream == 0:
            in_block = (jnp.where(mine, place, -1)[:, None] == jnp.arange(tail)[None, :]).astype(BF16)
            in_lane = ((fine % share)[:, None] == jnp.arange(share)[None, :]).astype(BF16)
            counted = lax.dot_general(
                in_block, in_lane, (((0,), (0,)), ((), ())), preferred_element_type=F32
            ).astype(jnp.int32)
            tile = [(counted // base**digit) % base for digit in range(digits)]
            tile = jnp.concatenate(tile, axis=1).astype(BF16)
            tile = jnp.pad(tile, ((0, 0), (0, wide - digits * share)))
        tiles.append(tile)

    half_keys //= 2
    send, keep = [None] * 2, [None] * 2
    for part, found in enumerate((send, keep)):
        for stream, (start, wide) in enumerate(columns):
            found[stream], token = key_sums(
                token, rows_of[stream], samples, other_samples, tiles[stream], part * half_keys, half_keys, start, wide
            )

    tokens = [start_token] * 2
    pick_token = lambda stream: tokens[1 - stream]
    old_share = lax.dynamic_slice(old_centroids[0], (me * share, 0), (share, width))

    def bf(count, stream, tailed):
        rows_out = count * share + (tail if stream == tailed else 0)
        return jax.ShapeDtypeStruct((rows_out, columns[stream][1]), BF16)

    share_f32 = [jax.ShapeDtypeStruct((share, wide), F32) for _, wide in columns]
    held, fresh, near = [None] * 2, [None] * 2, [None] * 2
    count = blocks // 2
    for stage in range(stages - 1):
        for stream, (start, wide) in enumerate(columns):
            got = exchange(send[stream], pairing(stage, stream), groups, members)
            if stage < stages - 2:
                send[stream], keep[stream], tokens[stream] = small_call(
                    functools.partial(fold_kernel, count // 2 * share, count),
                    "fold",
                    [bf(count // 2, stream, 0)] * 2,
                    pick_token(stream),
                    got,
                    keep[stream],
                )
            else:
                send[stream], near[stream], tokens[stream] = small_call(
                    functools.partial(seed_kernel, share, count),
                    "seed",
                    [bf(2, stream, 0), share_f32[stream]],
                    pick_token(stream),
                    got,
                    keep[stream],
                    old_share[:, start : start + wide],
                )
        count //= 2
    column = jax.ShapeDtypeStruct((2 * share, 1), F32)
    for stream in streams:
        got = exchange(send[stream], pairing(stages - 1, stream), groups, members)
        if stream == 0:
            fresh[0], held[0], scale, norm, tokens[stream] = small_call(
                functools.partial(first_kernel, share, base, digits),
                "first_centroids",
                [share_f32[0], bf(2, 0, 1), column, column],
                pick_token(stream),
                got,
                send[0],
                near[0],
            )
        else:
            fresh[1], held[1], tokens[stream] = small_call(
                functools.partial(last_kernel, share, tail),
                "last_centroids",
                [jax.ShapeDtypeStruct((share, width), F32), bf(2, 1, 1)],
                pick_token(stream),
                got,
                send[1],
                near[1],
                scale,
                norm,
                fresh[0],
            )
    half_blocks = blocks // 2
    quarter = half_blocks // groups
    inner_of = [[dim for dim in turned[c, 0] if dim[1]] for c in range(2)]

    def mask_rows(token, stream, more):
        start, wide = columns[stream]
        return small_call(
            functools.partial(mask_kernel, groups, start, wide),
            "mask",
            [jax.ShapeDtypeStruct((rows, groups * wide), BF16), *more],
            token,
            live_rows,
            coarse_label,
            samples,
            scalars=1,
            limit=52 if stream else 4,
        )

    def part_codes(part):
        codes = []
        for flip in range(2):
            for block in range(half_blocks):
                code = []
                for c in range(2):
                    group_rel, member_rel = relative_of(part * half_blocks + block, turned[c, 0])
                    spot = block_position(0, member_rel, inner_of[c], outer_bits) % quarter
                    code.append((spot + flip * quarter) * groups + (z ^ group_rel))
                codes.append(jnp.where(core ^ flip == 0, *code))
        return jnp.stack(codes).astype(jnp.int32)

    count = 2
    arrived = [None] * 2
    for stage in reversed(range(stages - 1)):
        for stream in streams:
            got = exchange(held[stream], pairing(stage, stream), groups, members)
            if stage:
                held[stream], tokens[stream] = small_call(
                    functools.partial(join_kernel, count * share, count),
                    "join",
                    [bf(2 * count, stream, 1)],
                    pick_token(stream),
                    got,
                    held[stream],
                )
            else:
                arrived[stream] = got
            if (stage, stream) == (1, 0):
                masked, tokens[0] = mask_rows(tokens[0], 0, [])
                total, tokens[0] = part_scores(
                    tokens[0], masked, part_codes(1), [held[0], sibling(held[0])], None, groups, keys, share
                )
        count *= 2

    def codes_of(stream, part, flip):
        codes = []
        for block in range(half_blocks):
            rel = [relative_of(part * half_blocks + block, turned[c, stream]) for c in range(2)]
            holder = core ^ flip
            group_rel = jnp.where(holder == 0, rel[0][0], rel[1][0])
            member_rel = jnp.where(holder == 0, rel[0][1], rel[1][1])
            codes.append((z ^ group_rel) * members + (me ^ flip ^ member_rel))
        return jnp.stack(codes).astype(jnp.int32)

    total, token = part_scores(
        tokens[1], masked, part_codes(0), [arrived[0], sibling(arrived[0])], total, groups, keys, share
    )
    masked, pick, token = mask_rows(token, 1, [jax.ShapeDtypeStruct((rows, TILE), BF16)])
    last = behind(arrived[1], token)
    every = jnp.arange(members, dtype=jnp.int32)
    flip_of = (every ^ me) & 1
    spot = jnp.where(
        (core ^ flip_of) == 0,
        *(block_position(0, every ^ me, inner_of[c], outer_bits) for c in range(2)),
    )
    slots = jnp.where(spot >= quarter, spot - quarter, spot + 2 * quarter) + flip_of * quarter
    flat = [piece for got in (last, held[1]) for piece in (got, sibling(got))]
    codes = jnp.concatenate([codes_of(1, part, flip) for part in range(2) for flip in range(2)])
    half = jnp.zeros((TILE, keys), F32)
    if share < 128:
        norm_rows = []
        for piece in flat:
            norm_rows.append(piece[half_blocks * share + tail - half_blocks :].astype(F32))
        norm_rows = jnp.concatenate(norm_rows)
        spread = (codes[None, :] == jnp.arange(groups * members, dtype=jnp.int32)[:, None]).astype(F32)
        for term in range(PARTS):
            found = jnp.dot(
                spread, norm_rows[:, term * share : (term + 1) * share], precision=lax.Precision.HIGHEST
            )
            half = half.at[term * groups : (term + 1) * groups].set(found.reshape(groups, keys))
        lane = jnp.arange(keys, dtype=jnp.int32)
        source = jnp.repeat(slots, share) * share + lane % share
        move = (lane[:, None] == source[None, :]).astype(F32)
        total = jnp.dot(total, move, precision=lax.Precision.HIGHEST)
        slots = jnp.arange(keys // 128, dtype=jnp.int32)
    scores = final_scores(masked, pick, codes, slots, flat, total, half, groups, keys, share)
    return scores, fresh[1][None]


def solution(mesh):
    return jax.shard_map(
        per_device,
        mesh=mesh,
        in_specs=(
            P(AXES, None),
            P(AXES, None),
            P(AXES),
            P(AXES),
            P("coarse", None, None),
        ),
        out_specs=(P(AXES, None), P("coarse", "member", None)),
        check_vma=False,
    )
```

```python
import functools

import jax
import jax.numpy as jnp
from jax import lax
from jax.experimental import pallas as pl
from jax.experimental.pallas import tpu as pltpu
from jax.sharding import PartitionSpec as P

AXES = ("coarse", "member")
TILE = 16
PRIOR = 16.0
PARTS = 2
F32 = jnp.float32
BF16 = jnp.bfloat16


def pad_rows(blocks):
    return max(TILE, -(-blocks // TILE) * TILE)


def streams_of(width):
    wide = width // 2
    return ((0, wide), (wide, wide))


def orders_of(groups, members):
    inner = [(0, 1 << bit) for bit in range(1, members.bit_length() - 1)]
    outer = [((1 << (bit + 1)) - 1, 0) for bit in range(groups.bit_length() - 1)]
    cut = len(inner) // 2
    other = inner[cut:] + inner[:cut]
    found = {}
    found[0, 0] = inner + outer
    found[1, 0] = other[:cut] + outer[:1] + other[cut:] + outer[1:]
    found[0, 1] = found[1, 0]
    found[1, 1] = inner[:cut] + outer[:1] + inner[cut:] + outer[1:]
    return found


def exchange(array, partner, groups, members):
    pairs = []
    for z in range(groups):
        for m in range(members):
            to_z, to_m = partner(z, m)
            pairs.append((z * members + m, to_z * members + to_m))
    return lax.ppermute(array, AXES, pairs)


def coefficients(group_rel, member_rel, dims, outer_bits):
    out = []
    for group_mask, member_mask in dims:
        if member_mask:
            out.append((member_rel >> (member_mask.bit_length() - 1)) & 1)
        else:
            top = group_mask.bit_length() - 1
            bit = (group_rel >> top) & 1
            if top + 1 < outer_bits:
                bit = bit ^ ((group_rel >> (top + 1)) & 1)
            out.append(bit)
    return out


def block_position(group_rel, member_rel, dims, outer_bits):
    place = 0
    for bit in coefficients(group_rel, member_rel, dims, outer_bits):
        place = place * 2 + (1 - bit)
    return place


def relative_of(place, dims):
    group_rel = member_rel = 0
    for at, (group_mask, member_mask) in enumerate(dims):
        if not (place >> (len(dims) - 1 - at)) & 1:
            group_rel ^= group_mask
            member_rel ^= member_mask
    return group_rel, member_rel


def token_shape():
    return jax.ShapeDtypeStruct((8, 128), F32)


def hand_on(kernel, inputs):
    def run(*refs):
        kernel(*refs[:inputs], *refs[inputs + 1 : -1])
        refs[-1][...] = refs[inputs][...]

    return run


def sums_kernel(base, pos_ref, own_ref, other_ref, *rest):
    out_ref = rest[-1]
    rows = own_ref.shape[0]
    keys = out_ref.shape[0] - (rest[0].shape[0] if len(rest) > 1 else 0)
    key = lax.broadcasted_iota(jnp.int32, (keys, rows), 0) + base
    first = jnp.where(pos_ref[:, :rows] == key, 1.0, 0.0).astype(BF16)
    second = jnp.where(pos_ref[:, rows:] == key, 1.0, 0.0).astype(BF16)
    total = jnp.dot(first, own_ref[...], preferred_element_type=F32)
    total += jnp.dot(second, other_ref[...], preferred_element_type=F32)
    out_ref[:keys, :] = total.astype(BF16)
    if len(rest) > 1:
        out_ref[keys:, :] = rest[0][...]


def key_sums(token, pos_row, own, other, count_tile, base, keys, start, wide):
    rows = own.shape[0]
    extra = [] if count_tile is None else [count_tile]
    out_rows = keys + sum(e.shape[0] for e in extra)
    whole = lambda shape: pl.BlockSpec(shape, lambda i: (0, 0))
    return pl.pallas_call(
        hand_on(functools.partial(sums_kernel, base), 3 + len(extra)),
        grid=(1,),
        out_shape=[jax.ShapeDtypeStruct((out_rows, wide), BF16), token_shape()],
        in_specs=[
            whole((1, 2 * rows)),
            pl.BlockSpec((rows, wide), lambda i: (0, start // wide)),
            pl.BlockSpec((rows, wide), lambda i: (0, start // wide)),
        ]
        + [whole(e.shape) for e in extra]
        + [whole(token.shape)],
        out_specs=[whole((out_rows, wide)), whole(token.shape)],
        compiler_params=pltpu.CompilerParams(vmem_limit_bytes=16 << 20),
        cost_estimate=pl.CostEstimate(
            flops=2 * keys * 2 * rows * wide, bytes_accessed=(4 * rows + 2 * keys) * wide, transcendentals=0
        ),
        name="key_sums",
    )(pos_row, own, other, *extra, token)


def small_call(kernel, name, outs, token, *args, scalars=0, limit=4):
    whole = pl.BlockSpec(memory_space=pltpu.VMEM)
    moved = sum(a.size * a.dtype.itemsize for a in (*args, *outs))
    return pl.pallas_call(
        hand_on(kernel, len(args)),
        out_shape=[*outs, token_shape()],
        in_specs=[pl.BlockSpec(memory_space=pltpu.SMEM)] * scalars + [whole] * (len(args) + 1 - scalars),
        out_specs=[whole if limit < 16 else pl.BlockSpec()] * len(outs) + [whole],
        compiler_params=pltpu.CompilerParams(vmem_limit_bytes=limit << 20),
        cost_estimate=pl.CostEstimate(flops=moved // 2, bytes_accessed=moved, transcendentals=0),
        name=name,
    )(*args, token)


def add_pair(got_ref, keep_ref, start, stop):
    return got_ref[start:stop, :].astype(F32) + keep_ref[start:stop, :].astype(F32)


def add_tail(got_ref, keep_ref, body, shift):
    kept = keep_ref[body:, :].astype(F32)
    return (kept + pltpu.roll(got_ref[body:, :].astype(F32), shift, 0)).astype(BF16)


def fold_kernel(half, shift, got_ref, keep_ref, send_out, keep_out):
    send_out[:half, :] = add_pair(got_ref, keep_ref, 0, half).astype(BF16)
    keep_out[:half, :] = add_pair(got_ref, keep_ref, half, 2 * half).astype(BF16)
    if got_ref.shape[0] > 2 * half:
        tail = add_tail(got_ref, keep_ref, 2 * half, shift)
        send_out[half:, :] = tail
        keep_out[half:, :] = tail


def seed_kernel(share, shift, got_ref, keep_ref, old_ref, send_out, near_out):
    two = 2 * share
    near = add_pair(got_ref, keep_ref, share, two) + PRIOR * old_ref[...]
    near_out[...] = near
    send_out[:share, :] = add_pair(got_ref, keep_ref, 0, share).astype(BF16)
    send_out[share:two, :] = near.astype(BF16)
    if got_ref.shape[0] > two:
        send_out[two:, :] = add_tail(got_ref, keep_ref, two, shift)


def summed(share, block, got_ref, sent_ref, near_ref):
    if block == 0:
        return sent_ref[:share, :].astype(F32) + got_ref[share : 2 * share, :].astype(F32)
    return near_ref[...] + got_ref[:share, :].astype(F32)


def square_sums(rounded):
    return jnp.sum(jnp.square(rounded.astype(F32)), axis=1, keepdims=True)


def first_kernel(share, base, digits, got_ref, sent_ref, near_ref, fresh_out, cents_out, scale_out, norm_out):
    two = 2 * share
    wide = got_ref.shape[1]
    last = sent_ref.shape[0] - two - 1
    lane = lax.broadcasted_iota(jnp.int32, (share, wide), 1)
    line = lax.broadcasted_iota(jnp.int32, (share, wide), 0)
    mine = sent_ref[two:, :].astype(F32)
    theirs = got_ref[two:, :].astype(F32)
    for block in range(2):
        row = mine[last - 1 + block : last + block, :] + theirs[last - block : last - block + 1, :]
        count = jnp.full((share, 1), PRIOR, F32)
        for digit in range(digits):
            hit = jnp.where(lane == line + digit * share, row, 0.0)
            count += jnp.sum(hit, axis=1, keepdims=True) * float(base**digit)
        scale_out[block * share : (block + 1) * share, :] = count
        fresh = summed(share, block, got_ref, sent_ref, near_ref) / count
        rounded = fresh.astype(BF16)
        cents_out[block * share : (block + 1) * share, :] = rounded
        norm_out[block * share : (block + 1) * share, :] = square_sums(rounded)
        if block == 1:
            fresh_out[...] = fresh


def last_kernel(share, tail, got_ref, sent_ref, near_ref, scale_ref, norm_ref, first_ref, fresh_out, cents_out):
    two = 2 * share
    wide = got_ref.shape[1]
    lane = lax.broadcasted_iota(jnp.int32, (share, wide), 1)
    line = lax.broadcasted_iota(jnp.int32, (share, wide), 0)
    tile = jnp.zeros((tail, wide), F32)
    tile_row = lax.broadcasted_iota(jnp.int32, (tail, wide), 0)
    for block in range(2):
        part = slice(block * share, (block + 1) * share)
        fresh = summed(share, block, got_ref, sent_ref, near_ref) / scale_ref[part, :]
        rounded = fresh.astype(BF16)
        cents_out[part, :] = rounded
        if block == 1:
            before = first_ref.shape[1]
            fresh_out[:, :before] = first_ref[...]
            fresh_out[:, before:] = fresh
        norm = 0.5 * (norm_ref[part, :] + square_sums(rounded))
        spread = jnp.zeros((1, wide), F32)
        for term_at in range(PARTS):
            term = norm.astype(BF16).astype(F32)
            norm = norm - term
            hit = jnp.where(lane == line + term_at * share, term, 0.0)
            spread += jnp.sum(hit, axis=0, keepdims=True)
        tile = jnp.where(tile_row == tail - 2 + block, spread, tile)
    cents_out[two:, :] = tile.astype(BF16)


def join_kernel(body, shift, got_ref, held_ref, out_ref):
    out_ref[:body, :] = got_ref[:body, :]
    out_ref[body : 2 * body, :] = held_ref[:body, :]
    if held_ref.shape[0] > body:
        rows = held_ref.shape[0] - body
        moved = pltpu.roll(got_ref[body:, :].astype(F32), rows - shift, 0)
        out_ref[2 * body :, :] = (held_ref[body:, :].astype(F32) + moved).astype(BF16)


def behind(array, token):
    def kernel(in_ref, token_ref, out_ref):
        del in_ref, token_ref, out_ref

    return pl.pallas_call(
        kernel,
        out_shape=jax.ShapeDtypeStruct(array.shape, array.dtype),
        in_specs=[pl.BlockSpec(memory_space=pl.ANY)] * 2,
        out_specs=pl.BlockSpec(memory_space=pl.ANY),
        input_output_aliases={0: 0},
        compiler_params=pltpu.CompilerParams(vmem_limit_bytes=1 << 20),
        cost_estimate=pl.CostEstimate(flops=1, bytes_accessed=1, transcendentals=0),
        name="behind",
    )(array, token)


def mask_kernel(groups, columns, live_ref, label_ref, x_ref, *outs):
    row = lax.broadcasted_iota(jnp.int32, label_ref.shape, 0)
    gid = jnp.where(row < live_ref[0], label_ref[...], -1)
    for (start, wide), out_ref in zip(columns, outs):
        x = x_ref[:, start : start + wide]
        for group in range(groups):
            out_ref[:, group * wide : (group + 1) * wide] = jnp.where(gid == group, x, jnp.zeros_like(x))
    pick_ref = outs[len(columns)]
    lane = lax.broadcasted_iota(jnp.int32, pick_ref.shape, 1)
    hit = (lane % groups == gid) & (lane < PARTS * groups)
    pick_ref[...] = jnp.where(hit, -1.0, 0.0).astype(BF16)


def product(a, b):
    return lax.dot_general(a, b, (((1,), (1,)), ((), ())), preferred_element_type=F32)


def part_kernel(groups, share, code_ref, masked_ref, own_ref, other_ref, *rest):
    out_ref, cents, rows_of, sem = rest
    load = pltpu.make_async_copy(masked_ref, rows_of, sem)
    wide = own_ref.shape[1]
    blocks = own_ref.shape[0] // share

    @pl.when(pl.program_id(0) == 0)
    def _():
        load.start()
        for piece, ref in enumerate((own_ref, other_ref)):
            for block in range(blocks):
                code = code_ref[piece * blocks + block]
                slot = pl.multiple_of(code // groups * share, share)
                cents[pl.ds(slot, share), pl.ds(pl.multiple_of(code % groups * wide, 128), wide)] = ref[block * share : (block + 1) * share, :]
        load.wait()

    step = out_ref.shape[1]
    start = pl.multiple_of(pl.program_id(0) * step, step)
    out_ref[...] = product(rows_of[...], cents[pl.ds(start, step), :])


def part_scores(token, masked, codes, pieces, before, groups, keys, share):
    rows = masked.shape[0]
    wide = pieces[0].shape[1]
    half = pieces[0].shape[0] * len(pieces) // groups
    step = min(256, half)
    steps = half // step
    at = 0 if before is None else steps
    whole = pl.BlockSpec(memory_space=pltpu.VMEM)
    extra = [] if before is None else [before]
    anywhere = pl.BlockSpec(memory_space=pl.ANY)

    def kernel(code_ref, *refs):
        count = 3 + len(extra)
        part_kernel(groups, share, code_ref, *refs[:3], refs[count + 1], *refs[-3:])
        refs[count + 2][...] = refs[count][...]

    return pl.pallas_call(
        kernel,
        grid_spec=pltpu.PrefetchScalarGridSpec(
            num_scalar_prefetch=1,
            grid=(steps,),
            in_specs=[anywhere] + [whole] * 2 + [anywhere] * len(extra) + [whole],
            out_specs=[pl.BlockSpec((rows, step), lambda i, w: (0, i + at)), whole],
            scratch_shapes=[
                pltpu.VMEM((half, groups * wide), BF16),
                pltpu.VMEM(masked.shape, BF16),
                pltpu.SemaphoreType.DMA,
            ],
        ),
        out_shape=[jax.ShapeDtypeStruct((rows, keys), F32), token_shape()],
        input_output_aliases={} if before is None else {4: 0},
        compiler_params=pltpu.CompilerParams(vmem_limit_bytes=51 << 20),
        cost_estimate=pl.CostEstimate(flops=1, bytes_accessed=1, transcendentals=0),
        name="part_scores",
    )(codes, masked, *pieces, *extra, token)


def final_kernel(groups, share, code_ref, slot_ref, masked_ref, pick_ref, half_ref, *rest):
    pieces = 4
    piece_refs, total_refs = rest[:pieces], rest[pieces : pieces + 2]
    out_ref, cents, half, rows_of, sem = rest[-5:]
    load = pltpu.make_async_copy(masked_ref, rows_of, sem)
    keys = cents.shape[0]
    wide = cents.shape[1] // groups
    members = keys // share
    blocks = code_ref.shape[0] // pieces
    lanes = 128

    @pl.when(pl.program_id(0) == 0)
    def _():
        load.start()
        half[...] = half_ref[...]
        for piece, ref in enumerate(piece_refs):
            for block in range(blocks):
                code = code_ref[piece * blocks + block]
                group = code // members
                row_at = pl.multiple_of((code % members) * share, share)
                cents[pl.ds(row_at, share), pl.ds(pl.multiple_of(group * wide, lanes), wide)] = ref[
                    block * share : (block + 1) * share, :
                ]
                if share >= lanes:
                    tail = ref[blocks * share :, :].astype(F32)
                    at = tail.shape[0] - blocks + block
                    lines = pl.ds(pl.multiple_of(row_at, lanes), share)
                    line = lax.broadcasted_iota(jnp.int32, (half.shape[0], share), 0)
                    filled = half[:, lines]
                    for term in range(PARTS):
                        row = tail[at : at + 1, term * share : (term + 1) * share]
                        filled = jnp.where(line == group + term * groups, row, filled)
                    half[:, lines] = filled
        load.wait()

    step = out_ref.shape[1]
    start = pl.multiple_of(pl.program_id(0) * step, step)
    dots = product(rows_of[...], cents[pl.ds(start, step), :])
    offsets = half[:, pl.ds(start, step)].astype(BF16)
    dots += jnp.dot(pick_ref[...], offsets, preferred_element_type=F32)
    cut = step // 2
    out_ref[:, :cut] = (dots[:, :cut] + total_refs[0][...]).astype(BF16)
    out_ref[:, cut:] = (dots[:, cut:] + total_refs[1][...]).astype(BF16)


def final_scores(masked, pick, codes, slots, pieces, total, half, groups, keys, share):
    rows = masked.shape[0]
    wide = pieces[0].shape[1]
    step = min(256, keys)
    cut = step // 2
    whole = pl.BlockSpec(memory_space=pltpu.VMEM)
    return pl.pallas_call(
        functools.partial(final_kernel, groups, share),
        grid_spec=pltpu.PrefetchScalarGridSpec(
            num_scalar_prefetch=2,
            grid=(keys // step,),
            in_specs=[pl.BlockSpec(memory_space=pl.ANY)]
            + [whole] * (2 + len(pieces))
            + [
                pl.BlockSpec((rows, cut), lambda i, c, s: (0, s[2 * i])),
                pl.BlockSpec((rows, cut), lambda i, c, s: (0, s[2 * i + 1])),
            ],
            out_specs=pl.BlockSpec((rows, step), lambda i, c, s: (0, i)),
            scratch_shapes=[
                pltpu.VMEM((keys, groups * wide), BF16),
                pltpu.VMEM(half.shape, F32),
                pltpu.VMEM(masked.shape, BF16),
                pltpu.SemaphoreType.DMA,
            ],
        ),
        out_shape=jax.ShapeDtypeStruct((rows, keys), BF16),
        compiler_params=pltpu.CompilerParams(vmem_limit_bytes=50 << 20),
        cost_estimate=pl.CostEstimate(flops=1, bytes_accessed=1, transcendentals=0),
        name="final_scores",
    )(codes, slots, masked, pick, half, *pieces, total, total)


def per_device(samples, coarse_label, fine_label, live_rows, old_centroids):
    groups = lax.axis_size("coarse")
    members = lax.axis_size("member")
    z = lax.axis_index("coarse")
    me = lax.axis_index("member")
    core = me & 1
    rows, width = samples.shape
    keys = old_centroids.shape[1]
    share = keys // members
    columns = streams_of(width)
    streams = range(len(columns))
    half_keys = groups * keys // 2
    blocks = half_keys // share
    outer_bits = groups.bit_length() - 1
    turned = orders_of(groups, members)
    stages = len(turned[0, 0])
    base = 256 // (groups * members // 2) + 1
    digits = 1
    while base**digits <= 2 * rows:
        digits += 1

    live = jnp.arange(rows, dtype=jnp.int32) < live_rows[0]
    label = jnp.where(live, coarse_label[:, 0] * keys + fine_label, -1)
    sibling = lambda a: exchange(a, lambda gz, m: (gz, m ^ 1), groups, members)
    other_samples = sibling(samples)
    label_all = jnp.concatenate([label, sibling(label)])

    group_of = label_all // keys
    fine = label_all % keys
    owner = fine // share
    mine = (label_all >= 0) & ((owner & 1) == core)

    def of_core(make):
        return jnp.where(core == 0, make(0), make(1))

    def pairing(stage, stream):
        def partner(gz, m):
            group_mask, member_mask = turned[m & 1, stream][stage]
            return gz ^ group_mask, m ^ member_mask

        return partner

    tail = pad_rows(blocks)
    token = start_token = jnp.zeros((8, 128), F32)
    rows_of, tiles = [], []
    for stream, (start, wide) in enumerate(columns):
        place = of_core(
            lambda c: block_position(group_of ^ z, owner ^ me, turned[c, stream], outer_bits)
        )
        rows_of.append(jnp.where(mine, place * share + fine % share, -1)[None, :])
        tile = None
        if stream == 0:
            in_block = (jnp.where(mine, place, -1)[:, None] == jnp.arange(tail)[None, :]).astype(BF16)
            in_lane = ((fine % share)[:, None] == jnp.arange(share)[None, :]).astype(BF16)
            counted = lax.dot_general(
                in_block, in_lane, (((0,), (0,)), ((), ())), preferred_element_type=F32
            ).astype(jnp.int32)
            tile = [(counted // base**digit) % base for digit in range(digits)]
            tile = jnp.concatenate(tile, axis=1).astype(BF16)
            tile = jnp.pad(tile, ((0, 0), (0, wide - digits * share)))
        tiles.append(tile)

    half_keys //= 2
    send, keep = [None] * 2, [None] * 2
    for part, found in enumerate((send, keep)):
        for stream, (start, wide) in enumerate(columns):
            found[stream], token = key_sums(
                token, rows_of[stream], samples, other_samples, tiles[stream], part * half_keys, half_keys, start, wide
            )

    tokens = [start_token] * 2
    own_turn = (2, 3, 4)

    def step_token(step, stream):
        return tokens[stream if stream == 0 and step in own_turn else 1 - stream]

    old_share = lax.dynamic_slice(old_centroids[0], (me * share, 0), (share, width))

    def bf(count, stream, tailed):
        rows_out = count * share + (tail if stream == tailed else 0)
        return jax.ShapeDtypeStruct((rows_out, columns[stream][1]), BF16)

    share_f32 = [jax.ShapeDtypeStruct((share, wide), F32) for _, wide in columns]
    held, fresh, near = [None] * 2, [None] * 2, [None] * 2
    count = blocks // 2
    for stage in range(stages - 1):
        for stream, (start, wide) in enumerate(columns):
            got = exchange(send[stream], pairing(stage, stream), groups, members)
            if stage < stages - 2:
                send[stream], keep[stream], tokens[stream] = small_call(
                    functools.partial(fold_kernel, count // 2 * share, count),
                    "fold",
                    [bf(count // 2, stream, 0)] * 2,
                    step_token(stage, stream),
                    got,
                    keep[stream],
                )
            else:
                send[stream], near[stream], tokens[stream] = small_call(
                    functools.partial(seed_kernel, share, count),
                    "seed",
                    [bf(2, stream, 0), share_f32[stream]],
                    step_token(stage, stream),
                    got,
                    keep[stream],
                    old_share[:, start : start + wide],
                )
        count //= 2
    column = jax.ShapeDtypeStruct((2 * share, 1), F32)
    for stream in streams:
        got = exchange(send[stream], pairing(stages - 1, stream), groups, members)
        if stream == 0:
            fresh[0], held[0], scale, norm, tokens[stream] = small_call(
                functools.partial(first_kernel, share, base, digits),
                "first_centroids",
                [share_f32[0], bf(2, 0, 1), column, column],
                step_token(stages - 1, stream),
                got,
                send[0],
                near[0],
            )
        else:
            fresh[1], held[1], tokens[stream] = small_call(
                functools.partial(last_kernel, share, tail),
                "last_centroids",
                [jax.ShapeDtypeStruct((share, width), F32), bf(2, 1, 1)],
                step_token(stages - 1, stream),
                got,
                send[1],
                near[1],
                scale,
                norm,
                fresh[0],
            )
    half_blocks = blocks // 2
    quarter = half_blocks // groups
    inner_of = [[dim for dim in turned[c, 0] if dim[1]] for c in range(2)]

    def part_codes(part):
        codes = []
        for flip in range(2):
            for block in range(half_blocks):
                code = []
                for c in range(2):
                    group_rel, member_rel = relative_of(part * half_blocks + block, turned[c, 0])
                    spot = block_position(0, member_rel, inner_of[c], outer_bits) % quarter
                    code.append((spot + flip * quarter) * groups + (z ^ group_rel))
                codes.append(jnp.where(core ^ flip == 0, *code))
        return jnp.stack(codes).astype(jnp.int32)

    count = 2
    arrived = [None] * 2
    for stage in reversed(range(stages - 1)):
        for stream in streams:
            got = exchange(held[stream], pairing(stage, stream), groups, members)
            if stage:
                held[stream], tokens[stream] = small_call(
                    functools.partial(join_kernel, count * share, count),
                    "join",
                    [bf(2 * count, stream, 1)],
                    step_token(2 * stages - 2 - stage, stream),
                    got,
                    held[stream],
                )
            else:
                arrived[stream] = got
            if (stage, stream) == (stages - 2, 0):
                *masked, pick, tokens[0] = small_call(
                    functools.partial(mask_kernel, groups, columns),
                    "mask",
                    [jax.ShapeDtypeStruct((rows, groups * wide), BF16) for _, wide in columns]
                    + [jax.ShapeDtypeStruct((rows, TILE), BF16)],
                    tokens[0],
                    live_rows,
                    coarse_label,
                    samples,
                    scalars=1,
                    limit=48,
                )
            if (stage, stream) == (1, 0):
                total, tokens[0] = part_scores(
                    tokens[0], masked[0], part_codes(1), [held[0], sibling(held[0])], None, groups, keys, share
                )
        count *= 2

    def codes_of(stream, part, flip):
        codes = []
        for block in range(half_blocks):
            rel = [relative_of(part * half_blocks + block, turned[c, stream]) for c in range(2)]
            holder = core ^ flip
            group_rel = jnp.where(holder == 0, rel[0][0], rel[1][0])
            member_rel = jnp.where(holder == 0, rel[0][1], rel[1][1])
            codes.append((z ^ group_rel) * members + (me ^ flip ^ member_rel))
        return jnp.stack(codes).astype(jnp.int32)

    total, token = part_scores(
        tokens[1], masked[0], part_codes(0), [arrived[0], sibling(arrived[0])], total, groups, keys, share
    )
    last = behind(arrived[1], token)
    every = jnp.arange(members, dtype=jnp.int32)
    flip_of = (every ^ me) & 1
    spot = jnp.where(
        (core ^ flip_of) == 0,
        *(block_position(0, every ^ me, inner_of[c], outer_bits) for c in range(2)),
    )
    slots = jnp.where(spot >= quarter, spot - quarter, spot + 2 * quarter) + flip_of * quarter
    flat = [piece for got in (last, held[1]) for piece in (got, sibling(got))]
    codes = jnp.concatenate([codes_of(1, part, flip) for part in range(2) for flip in range(2)])
    half = jnp.zeros((TILE, keys), F32)
    if share < 128:
        norm_rows = []
        for piece in flat:
            norm_rows.append(piece[half_blocks * share + tail - half_blocks :].astype(F32))
        norm_rows = jnp.concatenate(norm_rows)
        spread = (codes[None, :] == jnp.arange(groups * members, dtype=jnp.int32)[:, None]).astype(F32)
        for term in range(PARTS):
            found = jnp.dot(
                spread, norm_rows[:, term * share : (term + 1) * share], precision=lax.Precision.HIGHEST
            )
            half = half.at[term * groups : (term + 1) * groups].set(found.reshape(groups, keys))
        lane = jnp.arange(keys, dtype=jnp.int32)
        source = jnp.repeat(slots, share) * share + lane % share
        move = (lane[:, None] == source[None, :]).astype(F32)
        total = jnp.dot(total, move, precision=lax.Precision.HIGHEST)
        slots = jnp.arange(keys // 128, dtype=jnp.int32)
    scores = final_scores(masked[1], pick, codes, slots, flat, total, half, groups, keys, share)
    return scores, fresh[1][None]


def solution(mesh):
    return jax.shard_map(
        per_device,
        mesh=mesh,
        in_specs=(
            P(AXES, None),
            P(AXES, None),
            P(AXES),
            P(AXES),
            P("coarse", None, None),
        ),
        out_specs=(P(AXES, None), P("coarse", "member", None)),
        check_vma=False,
    )
```

```python
import functools

import jax
import jax.numpy as jnp
from jax import lax
from jax.experimental import pallas as pl
from jax.experimental.pallas import tpu as pltpu
from jax.sharding import PartitionSpec as P

AXES = ("coarse", "member")
TILE = 16
PRIOR = 16.0
PARTS = 2
F32 = jnp.float32
BF16 = jnp.bfloat16


def pad_rows(blocks):
    return max(TILE, -(-blocks // TILE) * TILE)


def streams_of(width):
    wide = width // 2
    return ((0, wide), (wide, wide))


def orders_of(groups, members):
    inner = [(0, 1 << bit) for bit in range(1, members.bit_length() - 1)]
    outer = [((1 << (bit + 1)) - 1, 0) for bit in range(groups.bit_length() - 1)]
    cut = len(inner) // 2
    other = inner[cut:] + inner[:cut]
    found = {}
    found[0, 0] = inner[:cut] + outer[:1] + inner[cut:] + outer[1:]
    found[1, 0] = other[:cut] + outer[:1] + other[cut:] + outer[1:]
    found[0, 1] = found[1, 0]
    found[1, 1] = found[0, 0]
    return found


def exchange(array, partner, groups, members):
    pairs = []
    for z in range(groups):
        for m in range(members):
            to_z, to_m = partner(z, m)
            pairs.append((z * members + m, to_z * members + to_m))
    return lax.ppermute(array, AXES, pairs)


def coefficients(group_rel, member_rel, dims, outer_bits):
    out = []
    for group_mask, member_mask in dims:
        if member_mask:
            out.append((member_rel >> (member_mask.bit_length() - 1)) & 1)
        else:
            top = group_mask.bit_length() - 1
            bit = (group_rel >> top) & 1
            if top + 1 < outer_bits:
                bit = bit ^ ((group_rel >> (top + 1)) & 1)
            out.append(bit)
    return out


def block_position(group_rel, member_rel, dims, outer_bits):
    place = 0
    for bit in coefficients(group_rel, member_rel, dims, outer_bits):
        place = place * 2 + (1 - bit)
    return place


def relative_of(place, dims):
    group_rel = member_rel = 0
    for at, (group_mask, member_mask) in enumerate(dims):
        if not (place >> (len(dims) - 1 - at)) & 1:
            group_rel ^= group_mask
            member_rel ^= member_mask
    return group_rel, member_rel


def token_shape():
    return jax.ShapeDtypeStruct((8, 128), F32)


def hand_on(kernel, inputs):
    def run(*refs):
        kernel(*refs[:inputs], *refs[inputs + 1 : -1])
        refs[-1][...] = refs[inputs][...]

    return run


def sums_kernel(base, pos_ref, own_ref, other_ref, *rest):
    out_ref = rest[-1]
    rows = own_ref.shape[0]
    keys = out_ref.shape[0] - (rest[0].shape[0] if len(rest) > 1 else 0)
    key = lax.broadcasted_iota(jnp.int32, (keys, rows), 0) + base
    first = jnp.where(pos_ref[:, :rows] == key, 1.0, 0.0).astype(BF16)
    second = jnp.where(pos_ref[:, rows:] == key, 1.0, 0.0).astype(BF16)
    total = jnp.dot(first, own_ref[...], preferred_element_type=F32)
    total += jnp.dot(second, other_ref[...], preferred_element_type=F32)
    out_ref[:keys, :] = total.astype(BF16)
    if len(rest) > 1:
        out_ref[keys:, :] = rest[0][...]


def key_sums(token, pos_row, own, other, count_tile, base, keys, start, wide):
    rows = own.shape[0]
    extra = [] if count_tile is None else [count_tile]
    out_rows = keys + sum(e.shape[0] for e in extra)
    whole = lambda shape: pl.BlockSpec(shape, lambda i: (0, 0))
    return pl.pallas_call(
        hand_on(functools.partial(sums_kernel, base), 3 + len(extra)),
        grid=(1,),
        out_shape=[jax.ShapeDtypeStruct((out_rows, wide), BF16), token_shape()],
        in_specs=[
            whole((1, 2 * rows)),
            pl.BlockSpec((rows, wide), lambda i: (0, start // wide)),
            pl.BlockSpec((rows, wide), lambda i: (0, start // wide)),
        ]
        + [whole(e.shape) for e in extra]
        + [whole(token.shape)],
        out_specs=[whole((out_rows, wide)), whole(token.shape)],
        compiler_params=pltpu.CompilerParams(vmem_limit_bytes=16 << 20),
        cost_estimate=pl.CostEstimate(
            flops=2 * keys * 2 * rows * wide, bytes_accessed=(4 * rows + 2 * keys) * wide, transcendentals=0
        ),
        name="key_sums",
    )(pos_row, own, other, *extra, token)


def small_call(kernel, name, outs, token, *args):
    whole = pl.BlockSpec(memory_space=pltpu.VMEM)
    moved = sum(a.size * a.dtype.itemsize for a in (*args, *outs))
    return pl.pallas_call(
        hand_on(kernel, len(args)),
        out_shape=[*outs, token_shape()],
        in_specs=[whole] * (len(args) + 1),
        out_specs=[whole] * (len(outs) + 1),
        compiler_params=pltpu.CompilerParams(vmem_limit_bytes=4 << 20),
        cost_estimate=pl.CostEstimate(flops=moved // 2, bytes_accessed=moved, transcendentals=0),
        name=name,
    )(*args, token)


def add_pair(got_ref, keep_ref, start, stop):
    return got_ref[start:stop, :].astype(F32) + keep_ref[start:stop, :].astype(F32)


def add_tail(got_ref, keep_ref, body, shift):
    kept = keep_ref[body:, :].astype(F32)
    return (kept + pltpu.roll(got_ref[body:, :].astype(F32), shift, 0)).astype(BF16)


def fold_kernel(half, shift, got_ref, keep_ref, send_out, keep_out):
    send_out[:half, :] = add_pair(got_ref, keep_ref, 0, half).astype(BF16)
    keep_out[:half, :] = add_pair(got_ref, keep_ref, half, 2 * half).astype(BF16)
    if got_ref.shape[0] > 2 * half:
        tail = add_tail(got_ref, keep_ref, 2 * half, shift)
        send_out[half:, :] = tail
        keep_out[half:, :] = tail


def seed_kernel(share, shift, got_ref, keep_ref, old_ref, send_out, near_out):
    two = 2 * share
    near = add_pair(got_ref, keep_ref, share, two) + PRIOR * old_ref[...]
    near_out[...] = near
    send_out[:share, :] = add_pair(got_ref, keep_ref, 0, share).astype(BF16)
    send_out[share:two, :] = near.astype(BF16)
    if got_ref.shape[0] > two:
        send_out[two:, :] = add_tail(got_ref, keep_ref, two, shift)


def summed(share, block, got_ref, sent_ref, near_ref):
    if block == 0:
        return sent_ref[:share, :].astype(F32) + got_ref[share : 2 * share, :].astype(F32)
    return near_ref[...] + got_ref[:share, :].astype(F32)


def square_sums(rounded):
    return jnp.sum(jnp.square(rounded.astype(F32)), axis=1, keepdims=True)


def first_kernel(share, base, digits, got_ref, sent_ref, near_ref, fresh_out, cents_out, scale_out, norm_out):
    two = 2 * share
    wide = got_ref.shape[1]
    last = sent_ref.shape[0] - two - 1
    lane = lax.broadcasted_iota(jnp.int32, (share, wide), 1)
    line = lax.broadcasted_iota(jnp.int32, (share, wide), 0)
    mine = sent_ref[two:, :].astype(F32)
    theirs = got_ref[two:, :].astype(F32)
    for block in range(2):
        row = mine[last - 1 + block : last + block, :] + theirs[last - block : last - block + 1, :]
        count = jnp.full((share, 1), PRIOR, F32)
        for digit in range(digits):
            hit = jnp.where(lane == line + digit * share, row, 0.0)
            count += jnp.sum(hit, axis=1, keepdims=True) * float(base**digit)
        scale_out[block * share : (block + 1) * share, :] = count
        fresh = summed(share, block, got_ref, sent_ref, near_ref) / count
        rounded = fresh.astype(BF16)
        cents_out[block * share : (block + 1) * share, :] = rounded
        norm_out[block * share : (block + 1) * share, :] = square_sums(rounded)
        if block == 1:
            fresh_out[...] = fresh


def last_kernel(share, tail, got_ref, sent_ref, near_ref, scale_ref, norm_ref, first_ref, fresh_out, cents_out):
    two = 2 * share
    wide = got_ref.shape[1]
    lane = lax.broadcasted_iota(jnp.int32, (share, wide), 1)
    line = lax.broadcasted_iota(jnp.int32, (share, wide), 0)
    tile = jnp.zeros((tail, wide), F32)
    tile_row = lax.broadcasted_iota(jnp.int32, (tail, wide), 0)
    for block in range(2):
        part = slice(block * share, (block + 1) * share)
        fresh = summed(share, block, got_ref, sent_ref, near_ref) / scale_ref[part, :]
        rounded = fresh.astype(BF16)
        cents_out[part, :] = rounded
        if block == 1:
            before = first_ref.shape[1]
            fresh_out[:, :before] = first_ref[...]
            fresh_out[:, before:] = fresh
        norm = 0.5 * (norm_ref[part, :] + square_sums(rounded))
        spread = jnp.zeros((1, wide), F32)
        for term_at in range(PARTS):
            term = norm.astype(BF16).astype(F32)
            norm = norm - term
            hit = jnp.where(lane == line + term_at * share, term, 0.0)
            spread += jnp.sum(hit, axis=0, keepdims=True)
        tile = jnp.where(tile_row == tail - 2 + block, spread, tile)
    cents_out[two:, :] = tile.astype(BF16)


def join_kernel(body, shift, got_ref, held_ref, out_ref):
    out_ref[:body, :] = got_ref[:body, :]
    out_ref[body : 2 * body, :] = held_ref[:body, :]
    if held_ref.shape[0] > body:
        rows = held_ref.shape[0] - body
        moved = pltpu.roll(got_ref[body:, :].astype(F32), rows - shift, 0)
        out_ref[2 * body :, :] = (held_ref[body:, :].astype(F32) + moved).astype(BF16)


def behind(array, token):
    def kernel(in_ref, token_ref, out_ref):
        del in_ref, token_ref, out_ref

    return pl.pallas_call(
        kernel,
        out_shape=jax.ShapeDtypeStruct(array.shape, array.dtype),
        in_specs=[pl.BlockSpec(memory_space=pl.ANY)] * 2,
        out_specs=pl.BlockSpec(memory_space=pl.ANY),
        input_output_aliases={0: 0},
        compiler_params=pltpu.CompilerParams(vmem_limit_bytes=1 << 20),
        cost_estimate=pl.CostEstimate(flops=1, bytes_accessed=1, transcendentals=0),
        name="behind",
    )(array, token)


def row_loads(x_ref, gid_ref, x, gid, sem, start):
    return (
        pltpu.make_async_copy(x_ref.at[:, pl.ds(start, x.shape[1])], x, sem.at[0]),
        pltpu.make_async_copy(gid_ref, gid, sem.at[1]),
    )


def mask_rows(groups, x, gid, out):
    wide = x.shape[1]
    for group in range(groups):
        out[:, group * wide : (group + 1) * wide] = jnp.where(gid[...] == group, x[...], jnp.zeros_like(x))


def row_scratch(rows, groups, wide):
    return [
        pltpu.VMEM((rows, groups * wide), BF16),
        pltpu.VMEM((rows, wide), BF16),
        pltpu.VMEM((rows, 1), jnp.int32),
        pltpu.SemaphoreType.DMA((2,)),
    ]


def product(a, b):
    return lax.dot_general(a, b, (((1,), (1,)), ((), ())), preferred_element_type=F32)


def part_kernel(groups, share, start_at, code_ref, x_ref, gid_ref, own_ref, other_ref, *rest):
    out_ref, cents, rows_of, x, gid, sem = rest
    loads = row_loads(x_ref, gid_ref, x, gid, sem, start_at)
    wide = own_ref.shape[1]
    blocks = own_ref.shape[0] // share

    @pl.when(pl.program_id(0) == 0)
    def _():
        for load in loads:
            load.start()
        for piece, ref in enumerate((own_ref, other_ref)):
            for block in range(blocks):
                code = code_ref[piece * blocks + block]
                slot = pl.multiple_of(code // groups * share, share)
                cents[pl.ds(slot, share), pl.ds(pl.multiple_of(code % groups * wide, 128), wide)] = ref[block * share : (block + 1) * share, :]
        for load in loads:
            load.wait()
        mask_rows(groups, x, gid, rows_of)

    step = out_ref.shape[1]
    start = pl.multiple_of(pl.program_id(0) * step, step)
    out_ref[...] = product(rows_of[...], cents[pl.ds(start, step), :]).astype(BF16)


def part_scores(token, samples, gid, codes, pieces, before, groups, keys, share, start_at):
    rows = samples.shape[0]
    wide = pieces[0].shape[1]
    half = pieces[0].shape[0] * len(pieces) // groups
    step = min(256, half)
    steps = half // step
    at = 0 if before is None else steps
    whole = pl.BlockSpec(memory_space=pltpu.VMEM)
    extra = [] if before is None else [before]
    anywhere = pl.BlockSpec(memory_space=pl.ANY)

    def kernel(code_ref, *refs):
        count = 4 + len(extra)
        part_kernel(groups, share, start_at, code_ref, *refs[:4], refs[count + 1], *refs[-5:])
        refs[count + 2][...] = refs[count][...]

    return pl.pallas_call(
        kernel,
        grid_spec=pltpu.PrefetchScalarGridSpec(
            num_scalar_prefetch=1,
            grid=(steps,),
            in_specs=[anywhere] * 2 + [whole] * 2 + [anywhere] * len(extra) + [whole],
            out_specs=[pl.BlockSpec((rows, step), lambda i, w: (0, i + at)), whole],
            scratch_shapes=[
                pltpu.VMEM((half, groups * wide), BF16),
                *row_scratch(rows, groups, wide),
            ],
        ),
        out_shape=[jax.ShapeDtypeStruct((rows, keys), BF16), token_shape()],
        input_output_aliases={} if before is None else {5: 0},
        compiler_params=pltpu.CompilerParams(vmem_limit_bytes=51 << 20),
        cost_estimate=pl.CostEstimate(flops=1, bytes_accessed=1, transcendentals=0),
        name="part_scores",
    )(codes, samples, gid, *pieces, *extra, token)


def final_kernel(groups, share, start_at, code_ref, slot_ref, x_ref, gid_ref, half_ref, *rest):
    pieces = 4
    piece_refs, total_refs = rest[:pieces], rest[pieces : pieces + 2]
    out_ref, cents, half, pick, rows_of, x, gid, sem = rest[-8:]
    loads = row_loads(x_ref, gid_ref, x, gid, sem, start_at)
    keys = cents.shape[0]
    wide = cents.shape[1] // groups
    members = keys // share
    blocks = code_ref.shape[0] // pieces
    lanes = 128

    @pl.when(pl.program_id(0) == 0)
    def _():
        for load in loads:
            load.start()
        half[...] = half_ref[...]
        for piece, ref in enumerate(piece_refs):
            for block in range(blocks):
                code = code_ref[piece * blocks + block]
                group = code // members
                row_at = pl.multiple_of((code % members) * share, share)
                cents[pl.ds(row_at, share), pl.ds(pl.multiple_of(group * wide, lanes), wide)] = ref[
                    block * share : (block + 1) * share, :
                ]
                if share >= lanes:
                    tail = ref[blocks * share :, :].astype(F32)
                    at = tail.shape[0] - blocks + block
                    lines = pl.ds(pl.multiple_of(row_at, lanes), share)
                    line = lax.broadcasted_iota(jnp.int32, (half.shape[0], share), 0)
                    filled = half[:, lines]
                    for term in range(PARTS):
                        row = tail[at : at + 1, term * share : (term + 1) * share]
                        filled = jnp.where(line == group + term * groups, row, filled)
                    half[:, lines] = filled
        for load in loads:
            load.wait()
        mask_rows(groups, x, gid, rows_of)
        lane = lax.broadcasted_iota(jnp.int32, pick.shape, 1)
        hit = (lane % groups == gid[...]) & (lane < PARTS * groups)
        pick[...] = jnp.where(hit, -1.0, 0.0).astype(BF16)

    step = out_ref.shape[1]
    start = pl.multiple_of(pl.program_id(0) * step, step)
    dots = product(rows_of[...], cents[pl.ds(start, step), :])
    offsets = half[:, pl.ds(start, step)].astype(BF16)
    dots += jnp.dot(pick[...], offsets, preferred_element_type=F32)
    cut = step // 2
    out_ref[:, :cut] = (dots[:, :cut] + total_refs[0][...].astype(F32)).astype(BF16)
    out_ref[:, cut:] = (dots[:, cut:] + total_refs[1][...].astype(F32)).astype(BF16)


def final_scores(samples, gid, codes, slots, pieces, total, half, groups, keys, share, start_at):
    rows = samples.shape[0]
    wide = pieces[0].shape[1]
    step = min(256, keys)
    cut = step // 2
    whole = pl.BlockSpec(memory_space=pltpu.VMEM)
    return pl.pallas_call(
        functools.partial(final_kernel, groups, share, start_at),
        grid_spec=pltpu.PrefetchScalarGridSpec(
            num_scalar_prefetch=2,
            grid=(keys // step,),
            in_specs=[pl.BlockSpec(memory_space=pl.ANY)] * 2
            + [whole] * (1 + len(pieces))
            + [
                pl.BlockSpec((rows, cut), lambda i, c, s: (0, s[2 * i])),
                pl.BlockSpec((rows, cut), lambda i, c, s: (0, s[2 * i + 1])),
            ],
            out_specs=pl.BlockSpec((rows, step), lambda i, c, s: (0, i)),
            scratch_shapes=[
                pltpu.VMEM((keys, groups * wide), BF16),
                pltpu.VMEM(half.shape, F32),
                pltpu.VMEM((rows, TILE), BF16),
                *row_scratch(rows, groups, wide),
            ],
        ),
        out_shape=jax.ShapeDtypeStruct((rows, keys), BF16),
        compiler_params=pltpu.CompilerParams(vmem_limit_bytes=50 << 20),
        cost_estimate=pl.CostEstimate(flops=1, bytes_accessed=1, transcendentals=0),
        name="final_scores",
    )(codes, slots, samples, gid, half, *pieces, total, total)


def per_device(samples, coarse_label, fine_label, live_rows, old_centroids):
    groups = lax.axis_size("coarse")
    members = lax.axis_size("member")
    z = lax.axis_index("coarse")
    me = lax.axis_index("member")
    core = me & 1
    rows, width = samples.shape
    keys = old_centroids.shape[1]
    share = keys // members
    columns = streams_of(width)
    streams = range(len(columns))
    half_keys = groups * keys // 2
    blocks = half_keys // share
    outer_bits = groups.bit_length() - 1
    turned = orders_of(groups, members)
    stages = len(turned[0, 0])
    base = 256 // (groups * members // 2) + 1
    digits = 1
    while base**digits <= 2 * rows:
        digits += 1

    live = jnp.arange(rows, dtype=jnp.int32) < live_rows[0]
    label = jnp.where(live, coarse_label[:, 0] * keys + fine_label, -1)
    sibling = lambda a: exchange(a, lambda gz, m: (gz, m ^ 1), groups, members)
    other_samples = sibling(samples)
    label_all = jnp.concatenate([label, sibling(label)])

    group_of = label_all // keys
    fine = label_all % keys
    owner = fine // share
    mine = (label_all >= 0) & ((owner & 1) == core)

    def of_core(make):
        return jnp.where(core == 0, make(0), make(1))

    def pairing(stage, stream):
        def partner(gz, m):
            group_mask, member_mask = turned[m & 1, stream][stage]
            return gz ^ group_mask, m ^ member_mask

        return partner

    tail = pad_rows(blocks)
    token = start_token = jnp.zeros((8, 128), F32)
    rows_of, tiles = [], []
    for stream, (start, wide) in enumerate(columns):
        place = of_core(
            lambda c: block_position(group_of ^ z, owner ^ me, turned[c, stream], outer_bits)
        )
        rows_of.append(jnp.where(mine, place * share + fine % share, -1)[None, :])
        tile = None
        if stream == 0:
            in_block = (jnp.where(mine, place, -1)[:, None] == jnp.arange(tail)[None, :]).astype(BF16)
            in_lane = ((fine % share)[:, None] == jnp.arange(share)[None, :]).astype(BF16)
            counted = lax.dot_general(
                in_block, in_lane, (((0,), (0,)), ((), ())), preferred_element_type=F32
            ).astype(jnp.int32)
            tile = [(counted // base**digit) % base for digit in range(digits)]
            tile = jnp.concatenate(tile, axis=1).astype(BF16)
            tile = jnp.pad(tile, ((0, 0), (0, wide - digits * share)))
        tiles.append(tile)

    half_keys //= 2
    send, keep = [None] * 2, [None] * 2
    for part, found in enumerate((send, keep)):
        for stream, (start, wide) in enumerate(columns):
            found[stream], token = key_sums(
                token, rows_of[stream], samples, other_samples, tiles[stream], part * half_keys, half_keys, start, wide
            )

    tokens = [start_token] * 2
    own_turn = (2, 3, 4)

    def step_token(step, stream):
        return tokens[stream if stream == 0 and step in own_turn else 1 - stream]

    old_share = lax.dynamic_slice(old_centroids[0], (me * share, 0), (share, width))

    def bf(count, stream, tailed):
        rows_out = count * share + (tail if stream == tailed else 0)
        return jax.ShapeDtypeStruct((rows_out, columns[stream][1]), BF16)

    share_f32 = [jax.ShapeDtypeStruct((share, wide), F32) for _, wide in columns]
    held, fresh, near = [None] * 2, [None] * 2, [None] * 2
    count = blocks // 2
    for stage in range(stages - 1):
        for stream, (start, wide) in enumerate(columns):
            got = exchange(send[stream], pairing(stage, stream), groups, members)
            if stage < stages - 2:
                send[stream], keep[stream], tokens[stream] = small_call(
                    functools.partial(fold_kernel, count // 2 * share, count),
                    "fold",
                    [bf(count // 2, stream, 0)] * 2,
                    step_token(stage, stream),
                    got,
                    keep[stream],
                )
            else:
                send[stream], near[stream], tokens[stream] = small_call(
                    functools.partial(seed_kernel, share, count),
                    "seed",
                    [bf(2, stream, 0), share_f32[stream]],
                    step_token(stage, stream),
                    got,
                    keep[stream],
                    old_share[:, start : start + wide],
                )
        count //= 2
    column = jax.ShapeDtypeStruct((2 * share, 1), F32)
    for stream in streams:
        got = exchange(send[stream], pairing(stages - 1, stream), groups, members)
        if stream == 0:
            fresh[0], held[0], scale, norm, tokens[stream] = small_call(
                functools.partial(first_kernel, share, base, digits),
                "first_centroids",
                [share_f32[0], bf(2, 0, 1), column, column],
                step_token(stages - 1, stream),
                got,
                send[0],
                near[0],
            )
        else:
            fresh[1], held[1], tokens[stream] = small_call(
                functools.partial(last_kernel, share, tail),
                "last_centroids",
                [jax.ShapeDtypeStruct((share, width), F32), bf(2, 1, 1)],
                step_token(stages - 1, stream),
                got,
                send[1],
                near[1],
                scale,
                norm,
                fresh[0],
            )
    half_blocks = blocks // 2
    quarter = half_blocks // groups
    inner_of = [[dim for dim in turned[c, 0] if dim[1]] for c in range(2)]

    def part_codes(part):
        codes = []
        for flip in range(2):
            for block in range(half_blocks):
                code = []
                for c in range(2):
                    group_rel, member_rel = relative_of(part * half_blocks + block, turned[c, 0])
                    spot = block_position(0, member_rel, inner_of[c], outer_bits) % quarter
                    code.append((spot + flip * quarter) * groups + (z ^ group_rel))
                codes.append(jnp.where(core ^ flip == 0, *code))
        return jnp.stack(codes).astype(jnp.int32)

    gid = jnp.where(live, coarse_label[:, 0], -1)[:, None]
    count = 2
    arrived = [None] * 2
    for stage in reversed(range(stages - 1)):
        for stream in streams:
            got = exchange(held[stream], pairing(stage, stream), groups, members)
            if stage:
                held[stream], tokens[stream] = small_call(
                    functools.partial(join_kernel, count * share, count),
                    "join",
                    [bf(2 * count, stream, 1)],
                    step_token(2 * stages - 2 - stage, stream),
                    got,
                    held[stream],
                )
            else:
                arrived[stream] = got
            if (stage, stream) == (1, 0):
                total, tokens[0] = part_scores(
                    tokens[0], samples, gid, part_codes(1), [held[0], sibling(held[0])], None, groups, keys, share, 0
                )
        count *= 2

    def codes_of(stream, part, flip):
        codes = []
        for block in range(half_blocks):
            rel = [relative_of(part * half_blocks + block, turned[c, stream]) for c in range(2)]
            holder = core ^ flip
            group_rel = jnp.where(holder == 0, rel[0][0], rel[1][0])
            member_rel = jnp.where(holder == 0, rel[0][1], rel[1][1])
            codes.append((z ^ group_rel) * members + (me ^ flip ^ member_rel))
        return jnp.stack(codes).astype(jnp.int32)

    total, token = part_scores(
        tokens[1], samples, gid, part_codes(0), [arrived[0], sibling(arrived[0])], total, groups, keys, share, 0
    )
    last = behind(arrived[1], token)
    every = jnp.arange(members, dtype=jnp.int32)
    flip_of = (every ^ me) & 1
    spot = jnp.where(
        (core ^ flip_of) == 0,
        *(block_position(0, every ^ me, inner_of[c], outer_bits) for c in range(2)),
    )
    slots = jnp.where(spot >= quarter, spot - quarter, spot + 2 * quarter) + flip_of * quarter
    flat = [piece for got in (last, held[1]) for piece in (got, sibling(got))]
    codes = jnp.concatenate([codes_of(1, part, flip) for part in range(2) for flip in range(2)])
    half = jnp.zeros((TILE, keys), F32)
    if share < 128:
        norm_rows = []
        for piece in flat:
            norm_rows.append(piece[half_blocks * share + tail - half_blocks :].astype(F32))
        norm_rows = jnp.concatenate(norm_rows)
        spread = (codes[None, :] == jnp.arange(groups * members, dtype=jnp.int32)[:, None]).astype(F32)
        for term in range(PARTS):
            found = jnp.dot(
                spread, norm_rows[:, term * share : (term + 1) * share], precision=lax.Precision.HIGHEST
            )
            half = half.at[term * groups : (term + 1) * groups].set(found.reshape(groups, keys))
        lane = jnp.arange(keys, dtype=jnp.int32)
        source = jnp.repeat(slots, share) * share + lane % share
        move = (lane[:, None] == source[None, :]).astype(F32)
        total = jnp.dot(total, move.astype(BF16))
        slots = jnp.arange(keys // 128, dtype=jnp.int32)
    scores = final_scores(samples, gid, codes, slots, flat, total, half, groups, keys, share, columns[1][0])
    return scores, fresh[1][None]


def solution(mesh):
    return jax.shard_map(
        per_device,
        mesh=mesh,
        in_specs=(
            P(AXES, None),
            P(AXES, None),
            P(AXES),
            P(AXES),
            P("coarse", None, None),
        ),
        out_specs=(P(AXES, None), P("coarse", "member", None)),
        check_vma=False,
    )
```

```python
import functools

import jax
import jax.numpy as jnp
from jax import lax
from jax.experimental import pallas as pl
from jax.experimental.pallas import tpu as pltpu
from jax.sharding import PartitionSpec as P

AXES = ("coarse", "member")
TILE = 16
PRIOR = 16.0
PARTS = 2
F32 = jnp.float32
BF16 = jnp.bfloat16


def pad_rows(blocks):
    return max(TILE, -(-blocks // TILE) * TILE)


def streams_of(width):
    wide = width // 2
    return ((0, wide), (wide, wide))


def orders_of(groups, members):
    inner = [(0, 1 << bit) for bit in range(1, members.bit_length() - 1)]
    outer = [((1 << (bit + 1)) - 1, 0) for bit in range(groups.bit_length() - 1)]
    cut = len(inner) // 2
    other = inner[cut:] + inner[:cut]
    found = {}
    found[0, 0] = inner[:cut] + outer[:1] + inner[cut:] + outer[1:]
    found[1, 0] = other[:cut] + outer[:1] + other[cut:] + outer[1:]
    found[0, 1] = found[1, 0]
    found[1, 1] = found[0, 0]
    return found


def exchange(array, partner, groups, members):
    pairs = []
    for z in range(groups):
        for m in range(members):
            to_z, to_m = partner(z, m)
            pairs.append((z * members + m, to_z * members + to_m))
    return lax.ppermute(array, AXES, pairs)


def coefficients(group_rel, member_rel, dims, outer_bits):
    out = []
    for group_mask, member_mask in dims:
        if member_mask:
            out.append((member_rel >> (member_mask.bit_length() - 1)) & 1)
        else:
            top = group_mask.bit_length() - 1
            bit = (group_rel >> top) & 1
            if top + 1 < outer_bits:
                bit = bit ^ ((group_rel >> (top + 1)) & 1)
            out.append(bit)
    return out


def block_position(group_rel, member_rel, dims, outer_bits):
    place = 0
    for bit in coefficients(group_rel, member_rel, dims, outer_bits):
        place = place * 2 + (1 - bit)
    return place


def relative_of(place, dims):
    group_rel = member_rel = 0
    for at, (group_mask, member_mask) in enumerate(dims):
        if not (place >> (len(dims) - 1 - at)) & 1:
            group_rel ^= group_mask
            member_rel ^= member_mask
    return group_rel, member_rel


def token_shape():
    return jax.ShapeDtypeStruct((8, 128), F32)


def hand_on(kernel, inputs):
    def run(*refs):
        kernel(*refs[:inputs], *refs[inputs + 1 : -1])
        refs[-1][...] = refs[inputs][...]

    return run


def sums_kernel(base, pos_ref, own_ref, other_ref, *rest):
    out_ref = rest[-1]
    rows = own_ref.shape[0]
    keys = out_ref.shape[0] - (rest[0].shape[0] if len(rest) > 1 else 0)
    key = lax.broadcasted_iota(jnp.int32, (keys, rows), 0) + base
    first = jnp.where(pos_ref[:, :rows] == key, 1.0, 0.0).astype(BF16)
    second = jnp.where(pos_ref[:, rows:] == key, 1.0, 0.0).astype(BF16)
    total = jnp.dot(first, own_ref[...], preferred_element_type=F32)
    total += jnp.dot(second, other_ref[...], preferred_element_type=F32)
    out_ref[:keys, :] = total.astype(BF16)
    if len(rest) > 1:
        out_ref[keys:, :] = rest[0][...]


def key_sums(token, pos_row, own, other, count_tile, base, keys):
    rows, wide = own.shape
    extra = [] if count_tile is None else [count_tile]
    out_rows = keys + sum(e.shape[0] for e in extra)
    whole = lambda shape: pl.BlockSpec(shape, lambda i: (0, 0))
    return pl.pallas_call(
        hand_on(functools.partial(sums_kernel, base), 3 + len(extra)),
        grid=(1,),
        out_shape=[jax.ShapeDtypeStruct((out_rows, wide), BF16), token_shape()],
        in_specs=[
            whole((1, 2 * rows)),
            whole((rows, wide)),
            whole((rows, wide)),
        ]
        + [whole(e.shape) for e in extra]
        + [whole(token.shape)],
        out_specs=[whole((out_rows, wide)), whole(token.shape)],
        compiler_params=pltpu.CompilerParams(vmem_limit_bytes=16 << 20),
        cost_estimate=pl.CostEstimate(
            flops=2 * keys * 2 * rows * wide, bytes_accessed=(4 * rows + 2 * keys) * wide, transcendentals=0
        ),
        name="key_sums",
    )(pos_row, own, other, *extra, token)


def small_call(kernel, name, outs, token, *args):
    whole = pl.BlockSpec(memory_space=pltpu.VMEM)
    moved = sum(a.size * a.dtype.itemsize for a in (*args, *outs))
    return pl.pallas_call(
        hand_on(kernel, len(args)),
        out_shape=[*outs, token_shape()],
        in_specs=[whole] * (len(args) + 1),
        out_specs=[whole] * (len(outs) + 1),
        compiler_params=pltpu.CompilerParams(vmem_limit_bytes=4 << 20),
        cost_estimate=pl.CostEstimate(flops=moved // 2, bytes_accessed=moved, transcendentals=0),
        name=name,
    )(*args, token)


def add_pair(got_ref, keep_ref, start, stop):
    return got_ref[start:stop, :].astype(F32) + keep_ref[start:stop, :].astype(F32)


def add_tail(got_ref, keep_ref, body, shift):
    kept = keep_ref[body:, :].astype(F32)
    return (kept + pltpu.roll(got_ref[body:, :].astype(F32), shift, 0)).astype(BF16)


def fold_kernel(half, shift, got_ref, keep_ref, send_out, keep_out):
    send_out[:half, :] = add_pair(got_ref, keep_ref, 0, half).astype(BF16)
    keep_out[:half, :] = add_pair(got_ref, keep_ref, half, 2 * half).astype(BF16)
    if got_ref.shape[0] > 2 * half:
        tail = add_tail(got_ref, keep_ref, 2 * half, shift)
        send_out[half:, :] = tail
        keep_out[half:, :] = tail


def seed_kernel(share, shift, got_ref, keep_ref, old_ref, send_out, near_out):
    two = 2 * share
    near = add_pair(got_ref, keep_ref, share, two) + PRIOR * old_ref[...]
    near_out[...] = near
    send_out[:share, :] = add_pair(got_ref, keep_ref, 0, share).astype(BF16)
    send_out[share:two, :] = near.astype(BF16)
    if got_ref.shape[0] > two:
        send_out[two:, :] = add_tail(got_ref, keep_ref, two, shift)


def summed(share, block, got_ref, sent_ref, near_ref):
    if block == 0:
        return sent_ref[:share, :].astype(F32) + got_ref[share : 2 * share, :].astype(F32)
    return near_ref[...] + got_ref[:share, :].astype(F32)


def square_sums(rounded):
    return jnp.sum(jnp.square(rounded.astype(F32)), axis=1, keepdims=True)


def first_kernel(share, base, digits, got_ref, sent_ref, near_ref, fresh_out, cents_out, scale_out, norm_out):
    two = 2 * share
    wide = got_ref.shape[1]
    last = sent_ref.shape[0] - two - 1
    lane = lax.broadcasted_iota(jnp.int32, (share, wide), 1)
    line = lax.broadcasted_iota(jnp.int32, (share, wide), 0)
    mine = sent_ref[two:, :].astype(F32)
    theirs = got_ref[two:, :].astype(F32)
    for block in range(2):
        row = mine[last - 1 + block : last + block, :] + theirs[last - block : last - block + 1, :]
        count = jnp.full((share, 1), PRIOR, F32)
        for digit in range(digits):
            hit = jnp.where(lane == line + digit * share, row, 0.0)
            count += jnp.sum(hit, axis=1, keepdims=True) * float(base**digit)
        scale_out[block * share : (block + 1) * share, :] = count
        fresh = summed(share, block, got_ref, sent_ref, near_ref) / count
        rounded = fresh.astype(BF16)
        cents_out[block * share : (block + 1) * share, :] = rounded
        norm_out[block * share : (block + 1) * share, :] = square_sums(rounded)
        if block == 1:
            fresh_out[...] = fresh


def last_kernel(share, tail, got_ref, sent_ref, near_ref, scale_ref, norm_ref, first_ref, fresh_out, cents_out):
    two = 2 * share
    wide = got_ref.shape[1]
    lane = lax.broadcasted_iota(jnp.int32, (share, wide), 1)
    line = lax.broadcasted_iota(jnp.int32, (share, wide), 0)
    tile = jnp.zeros((tail, wide), F32)
    tile_row = lax.broadcasted_iota(jnp.int32, (tail, wide), 0)
    for block in range(2):
        part = slice(block * share, (block + 1) * share)
        fresh = summed(share, block, got_ref, sent_ref, near_ref) / scale_ref[part, :]
        rounded = fresh.astype(BF16)
        cents_out[part, :] = rounded
        if block == 1:
            before = first_ref.shape[1]
            fresh_out[:, :before] = first_ref[...]
            fresh_out[:, before:] = fresh
        norm = 0.5 * (norm_ref[part, :] + square_sums(rounded))
        spread = jnp.zeros((1, wide), F32)
        for term_at in range(PARTS):
            term = norm.astype(BF16).astype(F32)
            norm = norm - term
            hit = jnp.where(lane == line + term_at * share, term, 0.0)
            spread += jnp.sum(hit, axis=0, keepdims=True)
        tile = jnp.where(tile_row == tail - 2 + block, spread, tile)
    cents_out[two:, :] = tile.astype(BF16)


def join_kernel(body, shift, got_ref, held_ref, out_ref):
    out_ref[:body, :] = got_ref[:body, :]
    out_ref[body : 2 * body, :] = held_ref[:body, :]
    if held_ref.shape[0] > body:
        rows = held_ref.shape[0] - body
        moved = pltpu.roll(got_ref[body:, :].astype(F32), rows - shift, 0)
        out_ref[2 * body :, :] = (held_ref[body:, :].astype(F32) + moved).astype(BF16)


def behind(array, token):
    def kernel(in_ref, token_ref, out_ref):
        del in_ref, token_ref, out_ref

    return pl.pallas_call(
        kernel,
        out_shape=jax.ShapeDtypeStruct(array.shape, array.dtype),
        in_specs=[pl.BlockSpec(memory_space=pl.ANY)] * 2,
        out_specs=pl.BlockSpec(memory_space=pl.ANY),
        input_output_aliases={0: 0},
        compiler_params=pltpu.CompilerParams(vmem_limit_bytes=1 << 20),
        cost_estimate=pl.CostEstimate(flops=1, bytes_accessed=1, transcendentals=0),
        name="behind",
    )(array, token)


def row_load(x_ref, x, sem, start):
    return pltpu.make_async_copy(x_ref.at[:, pl.ds(start, x.shape[1])], x, sem)


def mask_rows(groups, x, gid_ref, out):
    wide = x.shape[1]
    gid = jnp.transpose(jnp.broadcast_to(gid_ref[...], (128, gid_ref.shape[1])))
    for group in range(groups):
        keep = gid == group
        for cut in range(0, wide, 128):
            part = x[:, cut : cut + 128]
            out[:, group * wide + cut : group * wide + cut + 128] = jnp.where(keep, part, jnp.zeros_like(part))
    return gid


def row_scratch(rows, groups, wide):
    return [
        pltpu.VMEM((rows, groups * wide), BF16),
        pltpu.VMEM((rows, wide), BF16),
        pltpu.SemaphoreType.DMA,
    ]


def product(a, b):
    return lax.dot_general(a, b, (((1,), (1,)), ((), ())), preferred_element_type=F32)


def part_kernel(groups, share, start_at, code_ref, x_ref, gid_ref, own_ref, other_ref, *rest):
    out_ref, cents, rows_of, x, sem = rest
    load = row_load(x_ref, x, sem, start_at)
    wide = own_ref.shape[1]
    blocks = own_ref.shape[0] // share

    @pl.when(pl.program_id(0) == 0)
    def _():
        load.start()
        for piece, ref in enumerate((own_ref, other_ref)):
            for block in range(blocks):
                code = code_ref[piece * blocks + block]
                slot = pl.multiple_of(code // groups * share, share)
                cents[pl.ds(slot, share), pl.ds(pl.multiple_of(code % groups * wide, 128), wide)] = ref[block * share : (block + 1) * share, :]
        load.wait()
        mask_rows(groups, x, gid_ref, rows_of)

    step = out_ref.shape[1]
    start = pl.multiple_of(pl.program_id(0) * step, step)
    out_ref[...] = product(rows_of[...], cents[pl.ds(start, step), :]).astype(BF16)


def part_scores(token, samples, gid, codes, pieces, before, groups, keys, share, start_at):
    rows = samples.shape[0]
    wide = pieces[0].shape[1]
    half = pieces[0].shape[0] * len(pieces) // groups
    step = min(256, half)
    steps = half // step
    at = 0 if before is None else steps
    whole = pl.BlockSpec(memory_space=pltpu.VMEM)
    extra = [] if before is None else [before]
    anywhere = pl.BlockSpec(memory_space=pl.ANY)

    def kernel(code_ref, *refs):
        count = 4 + len(extra)
        part_kernel(groups, share, start_at, code_ref, *refs[:4], refs[count + 1], *refs[-4:])
        refs[count + 2][...] = refs[count][...]

    return pl.pallas_call(
        kernel,
        grid_spec=pltpu.PrefetchScalarGridSpec(
            num_scalar_prefetch=1,
            grid=(steps,),
            in_specs=[anywhere] + [whole] * 3 + [anywhere] * len(extra) + [whole],
            out_specs=[pl.BlockSpec((rows, step), lambda i, w: (0, i + at)), whole],
            scratch_shapes=[
                pltpu.VMEM((half, groups * wide), BF16),
                *row_scratch(rows, groups, wide),
            ],
        ),
        out_shape=[jax.ShapeDtypeStruct((rows, keys), BF16), token_shape()],
        input_output_aliases={} if before is None else {5: 0},
        compiler_params=pltpu.CompilerParams(vmem_limit_bytes=51 << 20),
        cost_estimate=pl.CostEstimate(flops=1, bytes_accessed=1, transcendentals=0),
        name="part_scores",
    )(codes, samples, gid, *pieces, *extra, token)


def final_kernel(groups, share, start_at, code_ref, slot_ref, x_ref, gid_ref, half_ref, *rest):
    pieces = 4
    piece_refs, total_refs = rest[:pieces], rest[pieces : pieces + 2]
    out_ref, cents, half, pick, rows_of, x, sem = rest[-7:]
    load = row_load(x_ref, x, sem, start_at)
    keys = cents.shape[0]
    wide = cents.shape[1] // groups
    members = keys // share
    blocks = code_ref.shape[0] // pieces
    lanes = 128

    @pl.when(pl.program_id(0) == 0)
    def _():
        load.start()
        half[...] = half_ref[...]
        for piece, ref in enumerate(piece_refs):
            for block in range(blocks):
                code = code_ref[piece * blocks + block]
                group = code // members
                row_at = pl.multiple_of((code % members) * share, share)
                cents[pl.ds(row_at, share), pl.ds(pl.multiple_of(group * wide, lanes), wide)] = ref[
                    block * share : (block + 1) * share, :
                ]
                if share >= lanes:
                    tail = ref[blocks * share :, :].astype(F32)
                    at = tail.shape[0] - blocks + block
                    lines = pl.ds(pl.multiple_of(row_at, lanes), share)
                    line = lax.broadcasted_iota(jnp.int32, (half.shape[0], share), 0)
                    filled = half[:, lines]
                    for term in range(PARTS):
                        row = tail[at : at + 1, term * share : (term + 1) * share]
                        filled = jnp.where(line == group + term * groups, row, filled)
                    half[:, lines] = filled
        load.wait()
        gid = mask_rows(groups, x, gid_ref, rows_of)[:, : pick.shape[1]]
        lane = lax.broadcasted_iota(jnp.int32, pick.shape, 1)
        hit = (lane % groups == gid) & (lane < PARTS * groups)
        pick[...] = jnp.where(hit, -1.0, 0.0).astype(BF16)

    step = out_ref.shape[1]
    start = pl.multiple_of(pl.program_id(0) * step, step)
    dots = product(rows_of[...], cents[pl.ds(start, step), :])
    offsets = half[:, pl.ds(start, step)].astype(BF16)
    dots += jnp.dot(pick[...], offsets, preferred_element_type=F32)
    cut = step // 2
    out_ref[:, :cut] = (dots[:, :cut] + total_refs[0][...].astype(F32)).astype(BF16)
    out_ref[:, cut:] = (dots[:, cut:] + total_refs[1][...].astype(F32)).astype(BF16)


def final_scores(samples, gid, codes, slots, pieces, total, half, groups, keys, share, start_at):
    rows = samples.shape[0]
    wide = pieces[0].shape[1]
    step = min(256, keys)
    cut = step // 2
    whole = pl.BlockSpec(memory_space=pltpu.VMEM)
    return pl.pallas_call(
        functools.partial(final_kernel, groups, share, start_at),
        grid_spec=pltpu.PrefetchScalarGridSpec(
            num_scalar_prefetch=2,
            grid=(keys // step,),
            in_specs=[pl.BlockSpec(memory_space=pl.ANY)]
            + [whole] * (2 + len(pieces))
            + [
                pl.BlockSpec((rows, cut), lambda i, c, s: (0, s[2 * i])),
                pl.BlockSpec((rows, cut), lambda i, c, s: (0, s[2 * i + 1])),
            ],
            out_specs=pl.BlockSpec((rows, step), lambda i, c, s: (0, i)),
            scratch_shapes=[
                pltpu.VMEM((keys, groups * wide), BF16),
                pltpu.VMEM(half.shape, F32),
                pltpu.VMEM((rows, TILE), BF16),
                *row_scratch(rows, groups, wide),
            ],
        ),
        out_shape=jax.ShapeDtypeStruct((rows, keys), BF16),
        compiler_params=pltpu.CompilerParams(vmem_limit_bytes=50 << 20),
        cost_estimate=pl.CostEstimate(flops=1, bytes_accessed=1, transcendentals=0),
        name="final_scores",
    )(codes, slots, samples, gid, half, *pieces, total, total)


def per_device(samples, coarse_label, fine_label, live_rows, old_centroids):
    groups = lax.axis_size("coarse")
    members = lax.axis_size("member")
    z = lax.axis_index("coarse")
    me = lax.axis_index("member")
    core = me & 1
    rows, width = samples.shape
    keys = old_centroids.shape[1]
    share = keys // members
    columns = streams_of(width)
    streams = range(len(columns))
    half_keys = groups * keys // 2
    blocks = half_keys // share
    outer_bits = groups.bit_length() - 1
    turned = orders_of(groups, members)
    stages = len(turned[0, 0])
    base = 256 // (groups * members // 2) + 1
    digits = 1
    while base**digits <= 2 * rows:
        digits += 1

    live = jnp.arange(rows, dtype=jnp.int32) < live_rows[0]
    label = jnp.where(live, coarse_label[:, 0] * keys + fine_label, -1)
    sibling = lambda a: exchange(a, lambda gz, m: (gz, m ^ 1), groups, members)
    cut_rows = [samples[:, start : start + wide] for start, wide in streams_of(width)]
    other_rows = [sibling(part) for part in cut_rows]
    label_all = jnp.concatenate([label, sibling(label)])

    group_of = label_all // keys
    fine = label_all % keys
    owner = fine // share
    mine = (label_all >= 0) & ((owner & 1) == core)

    def of_core(make):
        return jnp.where(core == 0, make(0), make(1))

    def pairing(stage, stream):
        def partner(gz, m):
            group_mask, member_mask = turned[m & 1, stream][stage]
            return gz ^ group_mask, m ^ member_mask

        return partner

    tail = pad_rows(blocks)
    token = start_token = jnp.zeros((8, 128), F32)
    rows_of, tiles = [], []
    for stream, (start, wide) in enumerate(columns):
        place = of_core(
            lambda c: block_position(group_of ^ z, owner ^ me, turned[c, stream], outer_bits)
        )
        rows_of.append(jnp.where(mine, place * share + fine % share, -1)[None, :])
        tile = None
        if stream == 0:
            in_block = (jnp.where(mine, place, -1)[:, None] == jnp.arange(tail)[None, :]).astype(BF16)
            in_lane = ((fine % share)[:, None] == jnp.arange(share)[None, :]).astype(BF16)
            counted = lax.dot_general(
                in_block, in_lane, (((0,), (0,)), ((), ())), preferred_element_type=F32
            ).astype(jnp.int32)
            tile = [(counted // base**digit) % base for digit in range(digits)]
            tile = jnp.concatenate(tile, axis=1).astype(BF16)
            tile = jnp.pad(tile, ((0, 0), (0, wide - digits * share)))
        tiles.append(tile)

    half_keys //= 2
    send, keep = [None] * 2, [None] * 2
    for part, found in enumerate((send, keep)):
        for stream, (start, wide) in enumerate(columns):
            found[stream], token = key_sums(
                token, rows_of[stream], cut_rows[stream], other_rows[stream], tiles[stream], part * half_keys, half_keys
            )

    tokens = [start_token] * 2
    own_turn = (2, 3, 4)

    def step_token(step, stream):
        return tokens[stream if stream == 0 and step in own_turn else 1 - stream]

    old_share = lax.dynamic_slice(old_centroids[0], (me * share, 0), (share, width))

    def bf(count, stream, tailed):
        rows_out = count * share + (tail if stream == tailed else 0)
        return jax.ShapeDtypeStruct((rows_out, columns[stream][1]), BF16)

    share_f32 = [jax.ShapeDtypeStruct((share, wide), F32) for _, wide in columns]
    held, fresh, near = [None] * 2, [None] * 2, [None] * 2
    count = blocks // 2
    for stage in range(stages - 1):
        for stream, (start, wide) in enumerate(columns):
            got = exchange(send[stream], pairing(stage, stream), groups, members)
            if stage < stages - 2:
                send[stream], keep[stream], tokens[stream] = small_call(
                    functools.partial(fold_kernel, count // 2 * share, count),
                    "fold",
                    [bf(count // 2, stream, 0)] * 2,
                    step_token(stage, stream),
                    got,
                    keep[stream],
                )
            else:
                send[stream], near[stream], tokens[stream] = small_call(
                    functools.partial(seed_kernel, share, count),
                    "seed",
                    [bf(2, stream, 0), share_f32[stream]],
                    step_token(stage, stream),
                    got,
                    keep[stream],
                    old_share[:, start : start + wide],
                )
        count //= 2
    column = jax.ShapeDtypeStruct((2 * share, 1), F32)
    for stream in streams:
        got = exchange(send[stream], pairing(stages - 1, stream), groups, members)
        if stream == 0:
            fresh[0], held[0], scale, norm, tokens[stream] = small_call(
                functools.partial(first_kernel, share, base, digits),
                "first_centroids",
                [share_f32[0], bf(2, 0, 1), column, column],
                step_token(stages - 1, stream),
                got,
                send[0],
                near[0],
            )
        else:
            fresh[1], held[1], tokens[stream] = small_call(
                functools.partial(last_kernel, share, tail),
                "last_centroids",
                [jax.ShapeDtypeStruct((share, width), F32), bf(2, 1, 1)],
                step_token(stages - 1, stream),
                got,
                send[1],
                near[1],
                scale,
                norm,
                fresh[0],
            )
    half_blocks = blocks // 2
    quarter = half_blocks // groups
    inner_of = [[dim for dim in turned[c, 0] if dim[1]] for c in range(2)]

    def part_codes(part):
        codes = []
        for flip in range(2):
            for block in range(half_blocks):
                code = []
                for c in range(2):
                    group_rel, member_rel = relative_of(part * half_blocks + block, turned[c, 0])
                    spot = block_position(0, member_rel, inner_of[c], outer_bits) % quarter
                    code.append((spot + flip * quarter) * groups + (z ^ group_rel))
                codes.append(jnp.where(core ^ flip == 0, *code))
        return jnp.stack(codes).astype(jnp.int32)

    gid = jnp.where(live, coarse_label[:, 0], -1)[None, :]
    count = 2
    arrived = [None] * 2
    for stage in reversed(range(stages - 1)):
        for stream in streams:
            got = exchange(held[stream], pairing(stage, stream), groups, members)
            if stage:
                held[stream], tokens[stream] = small_call(
                    functools.partial(join_kernel, count * share, count),
                    "join",
                    [bf(2 * count, stream, 1)],
                    step_token(2 * stages - 2 - stage, stream),
                    got,
                    held[stream],
                )
            else:
                arrived[stream] = got
            if (stage, stream) == (1, 0):
                total, tokens[0] = part_scores(
                    tokens[0], samples, gid, part_codes(1), [held[0], sibling(held[0])], None, groups, keys, share, 0
                )
        count *= 2

    def codes_of(stream, part, flip):
        codes = []
        for block in range(half_blocks):
            rel = [relative_of(part * half_blocks + block, turned[c, stream]) for c in range(2)]
            holder = core ^ flip
            group_rel = jnp.where(holder == 0, rel[0][0], rel[1][0])
            member_rel = jnp.where(holder == 0, rel[0][1], rel[1][1])
            codes.append((z ^ group_rel) * members + (me ^ flip ^ member_rel))
        return jnp.stack(codes).astype(jnp.int32)

    total, token = part_scores(
        tokens[1], samples, gid, part_codes(0), [arrived[0], sibling(arrived[0])], total, groups, keys, share, 0
    )
    last = behind(arrived[1], token)
    every = jnp.arange(members, dtype=jnp.int32)
    flip_of = (every ^ me) & 1
    spot = jnp.where(
        (core ^ flip_of) == 0,
        *(block_position(0, every ^ me, inner_of[c], outer_bits) for c in range(2)),
    )
    slots = jnp.where(spot >= quarter, spot - quarter, spot + 2 * quarter) + flip_of * quarter
    flat = [piece for got in (last, held[1]) for piece in (got, sibling(got))]
    codes = jnp.concatenate([codes_of(1, part, flip) for part in range(2) for flip in range(2)])
    half = jnp.zeros((TILE, keys), F32)
    if share < 128:
        norm_rows = []
        for piece in flat:
            norm_rows.append(piece[half_blocks * share + tail - half_blocks :].astype(F32))
        norm_rows = jnp.concatenate(norm_rows)
        spread = (codes[None, :] == jnp.arange(groups * members, dtype=jnp.int32)[:, None]).astype(F32)
        for term in range(PARTS):
            found = jnp.dot(
                spread, norm_rows[:, term * share : (term + 1) * share], precision=lax.Precision.HIGHEST
            )
            half = half.at[term * groups : (term + 1) * groups].set(found.reshape(groups, keys))
        lane = jnp.arange(keys, dtype=jnp.int32)
        source = jnp.repeat(slots, share) * share + lane % share
        move = (lane[:, None] == source[None, :]).astype(F32)
        total = jnp.dot(total, move.astype(BF16))
        slots = jnp.arange(keys // 128, dtype=jnp.int32)
    scores = final_scores(samples, gid, codes, slots, flat, total, half, groups, keys, share, columns[1][0])
    return scores, fresh[1][None]


def solution(mesh):
    return jax.shard_map(
        per_device,
        mesh=mesh,
        in_specs=(
            P(AXES, None),
            P(AXES, None),
            P(AXES),
            P(AXES),
            P("coarse", None, None),
        ),
        out_specs=(P(AXES, None), P("coarse", "member", None)),
        check_vma=False,
    )
```

```python
import functools

import jax
import jax.numpy as jnp
from jax import lax
from jax.experimental import pallas as pl
from jax.experimental.pallas import tpu as pltpu
from jax.sharding import PartitionSpec as P

AXES = ("coarse", "member")
TILE = 16
PRIOR = 16.0
PARTS = 2
F32 = jnp.float32
BF16 = jnp.bfloat16


def pad_rows(blocks):
    return max(TILE, -(-blocks // TILE) * TILE)


def streams_of(width):
    wide = width // 2
    return ((0, wide), (wide, wide))


def orders_of(groups, members):
    inner = [(0, 1 << bit) for bit in range(1, members.bit_length() - 1)]
    outer = [((1 << (bit + 1)) - 1, 0) for bit in range(groups.bit_length() - 1)]
    cut = len(inner) // 2
    other = inner[cut:] + inner[:cut]
    found = {}
    found[0, 0] = inner[:cut] + outer[:1] + inner[cut:] + outer[1:]
    found[1, 0] = other[:cut] + outer[:1] + other[cut:] + outer[1:]
    found[0, 1] = found[1, 0]
    found[1, 1] = found[0, 0]
    return found


def exchange(array, partner, groups, members):
    pairs = []
    for z in range(groups):
        for m in range(members):
            to_z, to_m = partner(z, m)
            pairs.append((z * members + m, to_z * members + to_m))
    return lax.ppermute(array, AXES, pairs)


def coefficients(group_rel, member_rel, dims, outer_bits):
    out = []
    for group_mask, member_mask in dims:
        if member_mask:
            out.append((member_rel >> (member_mask.bit_length() - 1)) & 1)
        else:
            top = group_mask.bit_length() - 1
            bit = (group_rel >> top) & 1
            if top + 1 < outer_bits:
                bit = bit ^ ((group_rel >> (top + 1)) & 1)
            out.append(bit)
    return out


def block_position(group_rel, member_rel, dims, outer_bits):
    place = 0
    for bit in coefficients(group_rel, member_rel, dims, outer_bits):
        place = place * 2 + (1 - bit)
    return place


def relative_of(place, dims):
    group_rel = member_rel = 0
    for at, (group_mask, member_mask) in enumerate(dims):
        if not (place >> (len(dims) - 1 - at)) & 1:
            group_rel ^= group_mask
            member_rel ^= member_mask
    return group_rel, member_rel


def token_shape():
    return jax.ShapeDtypeStruct((8, 128), F32)


def hand_on(kernel, inputs):
    def run(*refs):
        kernel(*refs[:inputs], *refs[inputs + 1 : -1])
        refs[-1][...] = refs[inputs][...]

    return run


def sums_kernel(base, pos_ref, own_ref, other_ref, *rest):
    out_ref = rest[-1]
    rows = own_ref.shape[0]
    keys = out_ref.shape[0] - (rest[0].shape[0] if len(rest) > 1 else 0)
    key = lax.broadcasted_iota(jnp.int32, (keys, rows), 0) + base
    first = jnp.where(pos_ref[:, :rows] == key, 1.0, 0.0).astype(BF16)
    second = jnp.where(pos_ref[:, rows:] == key, 1.0, 0.0).astype(BF16)
    total = jnp.dot(first, own_ref[...], preferred_element_type=F32)
    total += jnp.dot(second, other_ref[...], preferred_element_type=F32)
    out_ref[:keys, :] = total.astype(BF16)
    if len(rest) > 1:
        out_ref[keys:, :] = rest[0][...]


def key_sums(token, pos_row, own, other, count_tile, base, keys):
    rows, wide = own.shape
    extra = [] if count_tile is None else [count_tile]
    out_rows = keys + sum(e.shape[0] for e in extra)
    whole = lambda shape: pl.BlockSpec(shape, lambda i: (0, 0))
    return pl.pallas_call(
        hand_on(functools.partial(sums_kernel, base), 3 + len(extra)),
        grid=(1,),
        out_shape=[jax.ShapeDtypeStruct((out_rows, wide), BF16), token_shape()],
        in_specs=[
            whole((1, 2 * rows)),
            whole((rows, wide)),
            whole((rows, wide)),
        ]
        + [whole(e.shape) for e in extra]
        + [whole(token.shape)],
        out_specs=[whole((out_rows, wide)), whole(token.shape)],
        compiler_params=pltpu.CompilerParams(vmem_limit_bytes=16 << 20),
        cost_estimate=pl.CostEstimate(
            flops=2 * keys * 2 * rows * wide, bytes_accessed=(4 * rows + 2 * keys) * wide, transcendentals=0
        ),
        name="key_sums",
    )(pos_row, own, other, *extra, token)


def small_call(kernel, name, outs, token, *args):
    whole = pl.BlockSpec(memory_space=pltpu.VMEM)
    moved = sum(a.size * a.dtype.itemsize for a in (*args, *outs))
    return pl.pallas_call(
        hand_on(kernel, len(args)),
        out_shape=[*outs, token_shape()],
        in_specs=[whole] * (len(args) + 1),
        out_specs=[whole] * (len(outs) + 1),
        compiler_params=pltpu.CompilerParams(vmem_limit_bytes=4 << 20),
        cost_estimate=pl.CostEstimate(flops=moved // 2, bytes_accessed=moved, transcendentals=0),
        name=name,
    )(*args, token)


def add_pair(got_ref, keep_ref, start, stop):
    return got_ref[start:stop, :].astype(F32) + keep_ref[start:stop, :].astype(F32)


def add_tail(got_ref, keep_ref, body, shift):
    kept = keep_ref[body:, :].astype(F32)
    return (kept + pltpu.roll(got_ref[body:, :].astype(F32), shift, 0)).astype(BF16)


def fold_kernel(half, shift, got_ref, keep_ref, send_out, keep_out):
    send_out[:half, :] = add_pair(got_ref, keep_ref, 0, half).astype(BF16)
    keep_out[:half, :] = add_pair(got_ref, keep_ref, half, 2 * half).astype(BF16)
    if got_ref.shape[0] > 2 * half:
        tail = add_tail(got_ref, keep_ref, 2 * half, shift)
        send_out[half:, :] = tail
        keep_out[half:, :] = tail


def seed_kernel(share, shift, got_ref, keep_ref, old_ref, send_out, near_out):
    two = 2 * share
    near = add_pair(got_ref, keep_ref, share, two) + PRIOR * old_ref[...]
    near_out[...] = near
    send_out[:share, :] = add_pair(got_ref, keep_ref, 0, share).astype(BF16)
    send_out[share:two, :] = near.astype(BF16)
    if got_ref.shape[0] > two:
        send_out[two:, :] = add_tail(got_ref, keep_ref, two, shift)


def summed(share, block, got_ref, sent_ref, near_ref):
    if block == 0:
        return sent_ref[:share, :].astype(F32) + got_ref[share : 2 * share, :].astype(F32)
    return near_ref[...] + got_ref[:share, :].astype(F32)


def square_sums(rounded):
    return jnp.sum(jnp.square(rounded.astype(F32)), axis=1, keepdims=True)


def first_kernel(share, base, digits, got_ref, sent_ref, near_ref, fresh_out, cents_out, scale_out, norm_out):
    two = 2 * share
    wide = got_ref.shape[1]
    last = sent_ref.shape[0] - two - 1
    lane = lax.broadcasted_iota(jnp.int32, (share, wide), 1)
    line = lax.broadcasted_iota(jnp.int32, (share, wide), 0)
    mine = sent_ref[two:, :].astype(F32)
    theirs = got_ref[two:, :].astype(F32)
    for block in range(2):
        row = mine[last - 1 + block : last + block, :] + theirs[last - block : last - block + 1, :]
        count = jnp.full((share, 1), PRIOR, F32)
        for digit in range(digits):
            hit = jnp.where(lane == line + digit * share, row, 0.0)
            count += jnp.sum(hit, axis=1, keepdims=True) * float(base**digit)
        scale_out[block * share : (block + 1) * share, :] = count
        fresh = summed(share, block, got_ref, sent_ref, near_ref) / count
        rounded = fresh.astype(BF16)
        cents_out[block * share : (block + 1) * share, :] = rounded
        norm_out[block * share : (block + 1) * share, :] = square_sums(rounded)
        if block == 1:
            fresh_out[...] = fresh


def last_kernel(share, tail, got_ref, sent_ref, near_ref, scale_ref, norm_ref, first_ref, fresh_out, cents_out):
    two = 2 * share
    wide = got_ref.shape[1]
    lane = lax.broadcasted_iota(jnp.int32, (share, wide), 1)
    line = lax.broadcasted_iota(jnp.int32, (share, wide), 0)
    tile = jnp.zeros((tail, wide), F32)
    tile_row = lax.broadcasted_iota(jnp.int32, (tail, wide), 0)
    for block in range(2):
        part = slice(block * share, (block + 1) * share)
        fresh = summed(share, block, got_ref, sent_ref, near_ref) / scale_ref[part, :]
        rounded = fresh.astype(BF16)
        cents_out[part, :] = rounded
        if block == 1:
            before = first_ref.shape[1]
            fresh_out[:, :before] = first_ref[...]
            fresh_out[:, before:] = fresh
        norm = 0.5 * (norm_ref[part, :] + square_sums(rounded))
        spread = jnp.zeros((1, wide), F32)
        for term_at in range(PARTS):
            term = norm.astype(BF16).astype(F32)
            norm = norm - term
            hit = jnp.where(lane == line + term_at * share, term, 0.0)
            spread += jnp.sum(hit, axis=0, keepdims=True)
        tile = jnp.where(tile_row == tail - 2 + block, spread, tile)
    cents_out[two:, :] = tile.astype(BF16)


def join_kernel(body, shift, got_ref, held_ref, out_ref):
    out_ref[:body, :] = got_ref[:body, :]
    out_ref[body : 2 * body, :] = held_ref[:body, :]
    if held_ref.shape[0] > body:
        rows = held_ref.shape[0] - body
        moved = pltpu.roll(got_ref[body:, :].astype(F32), rows - shift, 0)
        out_ref[2 * body :, :] = (held_ref[body:, :].astype(F32) + moved).astype(BF16)


def behind(array, token):
    def kernel(in_ref, token_ref, out_ref):
        del in_ref, token_ref, out_ref

    return pl.pallas_call(
        kernel,
        out_shape=jax.ShapeDtypeStruct(array.shape, array.dtype),
        in_specs=[pl.BlockSpec(memory_space=pl.ANY)] * 2,
        out_specs=pl.BlockSpec(memory_space=pl.ANY),
        input_output_aliases={0: 0},
        compiler_params=pltpu.CompilerParams(vmem_limit_bytes=1 << 20),
        cost_estimate=pl.CostEstimate(flops=1, bytes_accessed=1, transcendentals=0),
        name="behind",
    )(array, token)


def row_loads(x_ref, gid_ref, x, gid, sem, start):
    return (
        pltpu.make_async_copy(x_ref.at[:, pl.ds(start, x.shape[1])], x, sem.at[0]),
        pltpu.make_async_copy(gid_ref, gid, sem.at[1]),
    )


def mask_rows(groups, x, gid_ref, out):
    wide = x.shape[1]
    gid = jnp.transpose(jnp.broadcast_to(gid_ref[...], (128, gid_ref.shape[1])))
    for group in range(groups):
        keep = gid == group
        for cut in range(0, wide, 128):
            part = x[:, cut : cut + 128]
            out[:, group * wide + cut : group * wide + cut + 128] = jnp.where(keep, part, jnp.zeros_like(part))
    return gid


def row_scratch(rows, groups, wide):
    return [
        pltpu.VMEM((rows, groups * wide), BF16),
        pltpu.VMEM((rows, wide), BF16),
        pltpu.VMEM((1, rows), jnp.int32),
        pltpu.SemaphoreType.DMA((2,)),
    ]


def product(a, b):
    return lax.dot_general(a, b, (((1,), (1,)), ((), ())), preferred_element_type=F32)


def part_kernel(groups, share, start_at, code_ref, x_ref, gid_ref, own_ref, other_ref, *rest):
    out_ref, cents, rows_of, x, gid_row, sem = rest
    loads = row_loads(x_ref, gid_ref, x, gid_row, sem, start_at)
    wide = own_ref.shape[1]
    blocks = own_ref.shape[0] // share

    @pl.when(pl.program_id(0) == 0)
    def _():
        for load in loads:
            load.start()
        for piece, ref in enumerate((own_ref, other_ref)):
            for block in range(blocks):
                code = code_ref[piece * blocks + block]
                slot = pl.multiple_of(code // groups * share, share)
                cents[pl.ds(slot, share), pl.ds(pl.multiple_of(code % groups * wide, 128), wide)] = ref[block * share : (block + 1) * share, :]
        for load in loads:
            load.wait()
        mask_rows(groups, x, gid_row, rows_of)

    step = out_ref.shape[1]
    start = pl.multiple_of(pl.program_id(0) * step, step)
    out_ref[...] = product(rows_of[...], cents[pl.ds(start, step), :]).astype(BF16)


def part_scores(token, samples, gid, codes, pieces, before, groups, keys, share, start_at):
    rows = samples.shape[0]
    wide = pieces[0].shape[1]
    half = pieces[0].shape[0] * len(pieces) // groups
    step = min(256, half)
    steps = half // step
    at = 0 if before is None else steps
    whole = pl.BlockSpec(memory_space=pltpu.VMEM)
    extra = [] if before is None else [before]
    anywhere = pl.BlockSpec(memory_space=pl.ANY)

    def kernel(code_ref, *refs):
        count = 4 + len(extra)
        part_kernel(groups, share, start_at, code_ref, *refs[:4], refs[count + 1], *refs[-5:])
        refs[count + 2][...] = refs[count][...]

    return pl.pallas_call(
        kernel,
        grid_spec=pltpu.PrefetchScalarGridSpec(
            num_scalar_prefetch=1,
            grid=(steps,),
            in_specs=[anywhere] * 2 + [whole] * 2 + [anywhere] * len(extra) + [whole],
            out_specs=[pl.BlockSpec((rows, step), lambda i, w: (0, i + at)), whole],
            scratch_shapes=[
                pltpu.VMEM((half, groups * wide), BF16),
                *row_scratch(rows, groups, wide),
            ],
        ),
        out_shape=[jax.ShapeDtypeStruct((rows, keys), BF16), token_shape()],
        input_output_aliases={} if before is None else {5: 0},
        compiler_params=pltpu.CompilerParams(vmem_limit_bytes=51 << 20),
        cost_estimate=pl.CostEstimate(flops=1, bytes_accessed=1, transcendentals=0),
        name="part_scores",
    )(codes, samples, gid, *pieces, *extra, token)


def final_kernel(groups, share, start_at, code_ref, slot_ref, x_ref, gid_ref, half_ref, *rest):
    pieces = 4
    piece_refs, total_refs = rest[:pieces], rest[pieces : pieces + 2]
    out_ref, cents, half, pick, rows_of, x, gid_row, sem = rest[-8:]
    loads = row_loads(x_ref, gid_ref, x, gid_row, sem, start_at)
    keys = cents.shape[0]
    wide = cents.shape[1] // groups
    members = keys // share
    blocks = code_ref.shape[0] // pieces
    lanes = 128

    @pl.when(pl.program_id(0) == 0)
    def _():
        for load in loads:
            load.start()
        half[...] = half_ref[...]
        for piece, ref in enumerate(piece_refs):
            for block in range(blocks):
                code = code_ref[piece * blocks + block]
                group = code // members
                row_at = pl.multiple_of((code % members) * share, share)
                cents[pl.ds(row_at, share), pl.ds(pl.multiple_of(group * wide, lanes), wide)] = ref[
                    block * share : (block + 1) * share, :
                ]
                if share >= lanes:
                    tail = ref[blocks * share :, :].astype(F32)
                    at = tail.shape[0] - blocks + block
                    lines = pl.ds(pl.multiple_of(row_at, lanes), share)
                    line = lax.broadcasted_iota(jnp.int32, (half.shape[0], share), 0)
                    filled = half[:, lines]
                    for term in range(PARTS):
                        row = tail[at : at + 1, term * share : (term + 1) * share]
                        filled = jnp.where(line == group + term * groups, row, filled)
                    half[:, lines] = filled
        for load in loads:
            load.wait()
        gid = mask_rows(groups, x, gid_row, rows_of)[:, : pick.shape[1]]
        lane = lax.broadcasted_iota(jnp.int32, pick.shape, 1)
        hit = (lane % groups == gid) & (lane < PARTS * groups)
        pick[...] = jnp.where(hit, -1.0, 0.0).astype(BF16)

    step = out_ref.shape[1]
    start = pl.multiple_of(pl.program_id(0) * step, step)
    dots = product(rows_of[...], cents[pl.ds(start, step), :])
    offsets = half[:, pl.ds(start, step)].astype(BF16)
    dots += jnp.dot(pick[...], offsets, preferred_element_type=F32)
    cut = step // 2
    out_ref[:, :cut] = (dots[:, :cut] + total_refs[0][...].astype(F32)).astype(BF16)
    out_ref[:, cut:] = (dots[:, cut:] + total_refs[1][...].astype(F32)).astype(BF16)


def final_scores(samples, gid, codes, slots, pieces, total, half, groups, keys, share, start_at):
    rows = samples.shape[0]
    wide = pieces[0].shape[1]
    step = min(256, keys)
    cut = step // 2
    whole = pl.BlockSpec(memory_space=pltpu.VMEM)
    return pl.pallas_call(
        functools.partial(final_kernel, groups, share, start_at),
        grid_spec=pltpu.PrefetchScalarGridSpec(
            num_scalar_prefetch=2,
            grid=(keys // step,),
            in_specs=[pl.BlockSpec(memory_space=pl.ANY)] * 2
            + [whole] * (1 + len(pieces))
            + [
                pl.BlockSpec((rows, cut), lambda i, c, s: (0, s[2 * i])),
                pl.BlockSpec((rows, cut), lambda i, c, s: (0, s[2 * i + 1])),
            ],
            out_specs=pl.BlockSpec((rows, step), lambda i, c, s: (0, i)),
            scratch_shapes=[
                pltpu.VMEM((keys, groups * wide), BF16),
                pltpu.VMEM(half.shape, F32),
                pltpu.VMEM((rows, TILE), BF16),
                *row_scratch(rows, groups, wide),
            ],
        ),
        out_shape=jax.ShapeDtypeStruct((rows, keys), BF16),
        compiler_params=pltpu.CompilerParams(vmem_limit_bytes=50 << 20),
        cost_estimate=pl.CostEstimate(flops=1, bytes_accessed=1, transcendentals=0),
        name="final_scores",
    )(codes, slots, samples, gid, half, *pieces, total, total)


def per_device(samples, coarse_label, fine_label, live_rows, old_centroids):
    groups = lax.axis_size("coarse")
    members = lax.axis_size("member")
    z = lax.axis_index("coarse")
    me = lax.axis_index("member")
    core = me & 1
    rows, width = samples.shape
    keys = old_centroids.shape[1]
    share = keys // members
    columns = streams_of(width)
    streams = range(len(columns))
    half_keys = groups * keys // 2
    blocks = half_keys // share
    outer_bits = groups.bit_length() - 1
    turned = orders_of(groups, members)
    stages = len(turned[0, 0])
    base = 256 // (groups * members // 2) + 1
    digits = 1
    while base**digits <= 2 * rows:
        digits += 1

    live = jnp.arange(rows, dtype=jnp.int32) < live_rows[0]
    label = jnp.where(live, coarse_label[:, 0] * keys + fine_label, -1)
    sibling = lambda a: exchange(a, lambda gz, m: (gz, m ^ 1), groups, members)
    cut_rows = [samples[:, start : start + wide] for start, wide in streams_of(width)]
    other_rows = [sibling(part) for part in cut_rows]
    label_all = jnp.concatenate([label, sibling(label)])

    group_of = label_all // keys
    fine = label_all % keys
    owner = fine // share
    mine = (label_all >= 0) & ((owner & 1) == core)

    def of_core(make):
        return jnp.where(core == 0, make(0), make(1))

    def pairing(stage, stream):
        def partner(gz, m):
            group_mask, member_mask = turned[m & 1, stream][stage]
            return gz ^ group_mask, m ^ member_mask

        return partner

    tail = pad_rows(blocks)
    token = start_token = jnp.zeros((8, 128), F32)
    rows_of, tiles = [], []
    for stream, (start, wide) in enumerate(columns):
        place = of_core(
            lambda c: block_position(group_of ^ z, owner ^ me, turned[c, stream], outer_bits)
        )
        rows_of.append(jnp.where(mine, place * share + fine % share, -1)[None, :])
        tile = None
        if stream == 0:
            in_block = (jnp.where(mine, place, -1)[:, None] == jnp.arange(tail)[None, :]).astype(BF16)
            in_lane = ((fine % share)[:, None] == jnp.arange(share)[None, :]).astype(BF16)
            counted = lax.dot_general(
                in_block, in_lane, (((0,), (0,)), ((), ())), preferred_element_type=F32
            ).astype(jnp.int32)
            tile = [(counted // base**digit) % base for digit in range(digits)]
            tile = jnp.concatenate(tile, axis=1).astype(BF16)
            tile = jnp.pad(tile, ((0, 0), (0, wide - digits * share)))
        tiles.append(tile)

    half_keys //= 2
    send, keep = [None] * 2, [None] * 2
    for part, found in enumerate((send, keep)):
        for stream, (start, wide) in enumerate(columns):
            found[stream], token = key_sums(
                token, rows_of[stream], cut_rows[stream], other_rows[stream], tiles[stream], part * half_keys, half_keys
            )

    tokens = [start_token] * 2
    own_turn = (2, 3, 4)

    def step_token(step, stream):
        return tokens[stream if stream == 0 and step in own_turn else 1 - stream]

    old_share = lax.dynamic_slice(old_centroids[0], (me * share, 0), (share, width))

    def bf(count, stream, tailed):
        rows_out = count * share + (tail if stream == tailed else 0)
        return jax.ShapeDtypeStruct((rows_out, columns[stream][1]), BF16)

    share_f32 = [jax.ShapeDtypeStruct((share, wide), F32) for _, wide in columns]
    held, fresh, near = [None] * 2, [None] * 2, [None] * 2
    count = blocks // 2
    for stage in range(stages - 1):
        for stream, (start, wide) in enumerate(columns):
            got = exchange(send[stream], pairing(stage, stream), groups, members)
            if stage < stages - 2:
                send[stream], keep[stream], tokens[stream] = small_call(
                    functools.partial(fold_kernel, count // 2 * share, count),
                    "fold",
                    [bf(count // 2, stream, 0)] * 2,
                    step_token(stage, stream),
                    got,
                    keep[stream],
                )
            else:
                send[stream], near[stream], tokens[stream] = small_call(
                    functools.partial(seed_kernel, share, count),
                    "seed",
                    [bf(2, stream, 0), share_f32[stream]],
                    step_token(stage, stream),
                    got,
                    keep[stream],
                    old_share[:, start : start + wide],
                )
        count //= 2
    column = jax.ShapeDtypeStruct((2 * share, 1), F32)
    for stream in streams:
        got = exchange(send[stream], pairing(stages - 1, stream), groups, members)
        if stream == 0:
            fresh[0], held[0], scale, norm, tokens[stream] = small_call(
                functools.partial(first_kernel, share, base, digits),
                "first_centroids",
                [share_f32[0], bf(2, 0, 1), column, column],
                step_token(stages - 1, stream),
                got,
                send[0],
                near[0],
            )
        else:
            fresh[1], held[1], tokens[stream] = small_call(
                functools.partial(last_kernel, share, tail),
                "last_centroids",
                [jax.ShapeDtypeStruct((share, width), F32), bf(2, 1, 1)],
                step_token(stages - 1, stream),
                got,
                send[1],
                near[1],
                scale,
                norm,
                fresh[0],
            )
    half_blocks = blocks // 2
    quarter = half_blocks // groups
    inner_of = [[dim for dim in turned[c, 0] if dim[1]] for c in range(2)]

    def part_codes(part):
        codes = []
        for flip in range(2):
            for block in range(half_blocks):
                code = []
                for c in range(2):
                    group_rel, member_rel = relative_of(part * half_blocks + block, turned[c, 0])
                    spot = block_position(0, member_rel, inner_of[c], outer_bits) % quarter
                    code.append((spot + flip * quarter) * groups + (z ^ group_rel))
                codes.append(jnp.where(core ^ flip == 0, *code))
        return jnp.stack(codes).astype(jnp.int32)

    gid = jnp.where(live, coarse_label[:, 0], -1)[None, :]
    count = 2
    arrived = [None] * 2
    for stage in reversed(range(stages - 1)):
        for stream in streams:
            got = exchange(held[stream], pairing(stage, stream), groups, members)
            if stage:
                held[stream], tokens[stream] = small_call(
                    functools.partial(join_kernel, count * share, count),
                    "join",
                    [bf(2 * count, stream, 1)],
                    step_token(2 * stages - 2 - stage, stream),
                    got,
                    held[stream],
                )
            else:
                arrived[stream] = got
            if (stage, stream) == (1, 0):
                total, tokens[0] = part_scores(
                    tokens[0], samples, gid, part_codes(1), [held[0], sibling(held[0])], None, groups, keys, share, 0
                )
        count *= 2

    def codes_of(stream, part, flip):
        codes = []
        for block in range(half_blocks):
            rel = [relative_of(part * half_blocks + block, turned[c, stream]) for c in range(2)]
            holder = core ^ flip
            group_rel = jnp.where(holder == 0, rel[0][0], rel[1][0])
            member_rel = jnp.where(holder == 0, rel[0][1], rel[1][1])
            codes.append((z ^ group_rel) * members + (me ^ flip ^ member_rel))
        return jnp.stack(codes).astype(jnp.int32)

    total, token = part_scores(
        tokens[1], samples, gid, part_codes(0), [arrived[0], sibling(arrived[0])], total, groups, keys, share, 0
    )
    last = behind(arrived[1], token)
    every = jnp.arange(members, dtype=jnp.int32)
    flip_of = (every ^ me) & 1
    spot = jnp.where(
        (core ^ flip_of) == 0,
        *(block_position(0, every ^ me, inner_of[c], outer_bits) for c in range(2)),
    )
    slots = jnp.where(spot >= quarter, spot - quarter, spot + 2 * quarter) + flip_of * quarter
    flat = [piece for got in (last, held[1]) for piece in (got, sibling(got))]
    codes = jnp.concatenate([codes_of(1, part, flip) for part in range(2) for flip in range(2)])
    half = jnp.zeros((TILE, keys), F32)
    if share < 128:
        norm_rows = []
        for piece in flat:
            norm_rows.append(piece[half_blocks * share + tail - half_blocks :].astype(F32))
        norm_rows = jnp.concatenate(norm_rows)
        spread = (codes[None, :] == jnp.arange(groups * members, dtype=jnp.int32)[:, None]).astype(F32)
        for term in range(PARTS):
            found = jnp.dot(
                spread, norm_rows[:, term * share : (term + 1) * share], precision=lax.Precision.HIGHEST
            )
            half = half.at[term * groups : (term + 1) * groups].set(found.reshape(groups, keys))
        lane = jnp.arange(keys, dtype=jnp.int32)
        source = jnp.repeat(slots, share) * share + lane % share
        move = (lane[:, None] == source[None, :]).astype(F32)
        total = jnp.dot(total, move.astype(BF16))
        slots = jnp.arange(keys // 128, dtype=jnp.int32)
    scores = final_scores(samples, gid, codes, slots, flat, total, half, groups, keys, share, columns[1][0])
    return scores, fresh[1][None]


def solution(mesh):
    return jax.shard_map(
        per_device,
        mesh=mesh,
        in_specs=(
            P(AXES, None),
            P(AXES, None),
            P(AXES),
            P(AXES),
            P("coarse", None, None),
        ),
        out_specs=(P(AXES, None), P("coarse", "member", None)),
        check_vma=False,
    )
```

```python
import functools

import jax
import jax.numpy as jnp
from jax import lax
from jax.experimental import pallas as pl
from jax.experimental.pallas import tpu as pltpu
from jax.sharding import PartitionSpec as P

AXES = ("coarse", "member")
TILE = 16
PRIOR = 16.0
PARTS = 2
F32 = jnp.float32
BF16 = jnp.bfloat16


def pad_rows(blocks):
    return max(TILE, -(-blocks // TILE) * TILE)


def streams_of(width):
    wide = width // 2
    return ((0, wide), (wide, wide))


def orders_of(groups, members):
    inner = [(0, 1 << bit) for bit in range(1, members.bit_length() - 1)]
    outer = [((1 << (bit + 1)) - 1, 0) for bit in range(groups.bit_length() - 1)]
    cut = len(inner) // 2
    other = inner[cut:] + inner[:cut]
    found = {}
    found[0, 0] = inner[:cut] + outer[:1] + inner[cut:] + outer[1:]
    found[1, 0] = other[:cut] + outer[:1] + other[cut:] + outer[1:]
    found[0, 1] = found[1, 0]
    found[1, 1] = found[0, 0]
    return found


def exchange(array, partner, groups, members):
    pairs = []
    for z in range(groups):
        for m in range(members):
            to_z, to_m = partner(z, m)
            pairs.append((z * members + m, to_z * members + to_m))
    return lax.ppermute(array, AXES, pairs)


def coefficients(group_rel, member_rel, dims, outer_bits):
    out = []
    for group_mask, member_mask in dims:
        if member_mask:
            out.append((member_rel >> (member_mask.bit_length() - 1)) & 1)
        else:
            top = group_mask.bit_length() - 1
            bit = (group_rel >> top) & 1
            if top + 1 < outer_bits:
                bit = bit ^ ((group_rel >> (top + 1)) & 1)
            out.append(bit)
    return out


def block_position(group_rel, member_rel, dims, outer_bits):
    place = 0
    for bit in coefficients(group_rel, member_rel, dims, outer_bits):
        place = place * 2 + (1 - bit)
    return place


def relative_of(place, dims):
    group_rel = member_rel = 0
    for at, (group_mask, member_mask) in enumerate(dims):
        if not (place >> (len(dims) - 1 - at)) & 1:
            group_rel ^= group_mask
            member_rel ^= member_mask
    return group_rel, member_rel


def token_shape():
    return jax.ShapeDtypeStruct((8, 128), F32)


def hand_on(kernel, inputs):
    def run(*refs):
        kernel(*refs[:inputs], *refs[inputs + 1 : -1])
        refs[-1][...] = refs[inputs][...]

    return run


def sums_kernel(base, pos_ref, own_ref, other_ref, *rest):
    out_ref = rest[-1]
    rows = own_ref.shape[0]
    keys = out_ref.shape[0] - (rest[0].shape[0] if len(rest) > 1 else 0)
    key = lax.broadcasted_iota(jnp.int32, (keys, rows), 0) + base
    first = jnp.where(pos_ref[:, :rows] == key, 1.0, 0.0).astype(BF16)
    second = jnp.where(pos_ref[:, rows:] == key, 1.0, 0.0).astype(BF16)
    total = jnp.dot(first, own_ref[...], preferred_element_type=F32)
    total += jnp.dot(second, other_ref[...], preferred_element_type=F32)
    out_ref[:keys, :] = total.astype(BF16)
    if len(rest) > 1:
        out_ref[keys:, :] = rest[0][...]


def key_sums(token, pos_row, own, other, count_tile, base, keys, start, wide):
    rows = own.shape[0]
    extra = [] if count_tile is None else [count_tile]
    out_rows = keys + sum(e.shape[0] for e in extra)
    whole = lambda shape: pl.BlockSpec(shape, lambda i: (0, 0))
    return pl.pallas_call(
        hand_on(functools.partial(sums_kernel, base), 3 + len(extra)),
        grid=(1,),
        out_shape=[jax.ShapeDtypeStruct((out_rows, wide), BF16), token_shape()],
        in_specs=[
            whole((1, 2 * rows)),
            pl.BlockSpec((rows, wide), lambda i: (0, start // wide)),
            pl.BlockSpec((rows, wide), lambda i: (0, start // wide)),
        ]
        + [whole(e.shape) for e in extra]
        + [whole(token.shape)],
        out_specs=[whole((out_rows, wide)), whole(token.shape)],
        compiler_params=pltpu.CompilerParams(vmem_limit_bytes=56 << 20),
        cost_estimate=pl.CostEstimate(
            flops=2 * keys * 2 * rows * wide, bytes_accessed=(4 * rows + 2 * keys) * wide, transcendentals=0
        ),
        name="key_sums",
    )(pos_row, own, other, *extra, token)


def small_call(kernel, name, outs, token, *args):
    whole = pl.BlockSpec(memory_space=pltpu.VMEM)
    moved = sum(a.size * a.dtype.itemsize for a in (*args, *outs))
    return pl.pallas_call(
        hand_on(kernel, len(args)),
        out_shape=[*outs, token_shape()],
        in_specs=[whole] * (len(args) + 1),
        out_specs=[whole] * (len(outs) + 1),
        compiler_params=pltpu.CompilerParams(vmem_limit_bytes=4 << 20),
        cost_estimate=pl.CostEstimate(flops=moved // 2, bytes_accessed=moved, transcendentals=0),
        name=name,
    )(*args, token)


def add_pair(got_ref, keep_ref, start, stop):
    return got_ref[start:stop, :].astype(F32) + keep_ref[start:stop, :].astype(F32)


def add_tail(got_ref, keep_ref, body, shift):
    kept = keep_ref[body:, :].astype(F32)
    return (kept + pltpu.roll(got_ref[body:, :].astype(F32), shift, 0)).astype(BF16)


def fold_kernel(half, shift, got_ref, keep_ref, send_out, keep_out):
    send_out[:half, :] = add_pair(got_ref, keep_ref, 0, half).astype(BF16)
    keep_out[:half, :] = add_pair(got_ref, keep_ref, half, 2 * half).astype(BF16)
    if got_ref.shape[0] > 2 * half:
        tail = add_tail(got_ref, keep_ref, 2 * half, shift)
        send_out[half:, :] = tail
        keep_out[half:, :] = tail


def seed_kernel(share, shift, got_ref, keep_ref, old_ref, send_out, near_out):
    two = 2 * share
    near = add_pair(got_ref, keep_ref, share, two) + PRIOR * old_ref[...]
    near_out[...] = near
    send_out[:share, :] = add_pair(got_ref, keep_ref, 0, share).astype(BF16)
    send_out[share:two, :] = near.astype(BF16)
    if got_ref.shape[0] > two:
        send_out[two:, :] = add_tail(got_ref, keep_ref, two, shift)


def summed(share, block, got_ref, sent_ref, near_ref):
    if block == 0:
        return sent_ref[:share, :].astype(F32) + got_ref[share : 2 * share, :].astype(F32)
    return near_ref[...] + got_ref[:share, :].astype(F32)


def square_sums(rounded):
    return jnp.sum(jnp.square(rounded.astype(F32)), axis=1, keepdims=True)


def first_kernel(share, base, digits, got_ref, sent_ref, near_ref, fresh_out, cents_out, scale_out, norm_out):
    two = 2 * share
    wide = got_ref.shape[1]
    last = sent_ref.shape[0] - two - 1
    lane = lax.broadcasted_iota(jnp.int32, (share, wide), 1)
    line = lax.broadcasted_iota(jnp.int32, (share, wide), 0)
    mine = sent_ref[two:, :].astype(F32)
    theirs = got_ref[two:, :].astype(F32)
    for block in range(2):
        row = mine[last - 1 + block : last + block, :] + theirs[last - block : last - block + 1, :]
        count = jnp.full((share, 1), PRIOR, F32)
        for digit in range(digits):
            hit = jnp.where(lane == line + digit * share, row, 0.0)
            count += jnp.sum(hit, axis=1, keepdims=True) * float(base**digit)
        scale_out[block * share : (block + 1) * share, :] = count
        fresh = summed(share, block, got_ref, sent_ref, near_ref) / count
        rounded = fresh.astype(BF16)
        cents_out[block * share : (block + 1) * share, :] = rounded
        norm_out[block * share : (block + 1) * share, :] = square_sums(rounded)
        if block == 1:
            fresh_out[...] = fresh


def last_kernel(share, tail, got_ref, sent_ref, near_ref, scale_ref, norm_ref, first_ref, fresh_out, cents_out):
    two = 2 * share
    wide = got_ref.shape[1]
    lane = lax.broadcasted_iota(jnp.int32, (share, wide), 1)
    line = lax.broadcasted_iota(jnp.int32, (share, wide), 0)
    tile = jnp.zeros((tail, wide), F32)
    tile_row = lax.broadcasted_iota(jnp.int32, (tail, wide), 0)
    for block in range(2):
        part = slice(block * share, (block + 1) * share)
        fresh = summed(share, block, got_ref, sent_ref, near_ref) / scale_ref[part, :]
        rounded = fresh.astype(BF16)
        cents_out[part, :] = rounded
        if block == 1:
            before = first_ref.shape[1]
            fresh_out[:, :before] = first_ref[...]
            fresh_out[:, before:] = fresh
        norm = 0.5 * (norm_ref[part, :] + square_sums(rounded))
        spread = jnp.zeros((1, wide), F32)
        for term_at in range(PARTS):
            term = norm.astype(BF16).astype(F32)
            norm = norm - term
            hit = jnp.where(lane == line + term_at * share, term, 0.0)
            spread += jnp.sum(hit, axis=0, keepdims=True)
        tile = jnp.where(tile_row == tail - 2 + block, spread, tile)
    cents_out[two:, :] = tile.astype(BF16)


def join_kernel(body, shift, got_ref, held_ref, out_ref):
    out_ref[:body, :] = got_ref[:body, :]
    out_ref[body : 2 * body, :] = held_ref[:body, :]
    if held_ref.shape[0] > body:
        rows = held_ref.shape[0] - body
        moved = pltpu.roll(got_ref[body:, :].astype(F32), rows - shift, 0)
        out_ref[2 * body :, :] = (held_ref[body:, :].astype(F32) + moved).astype(BF16)


def behind(array, token):
    def kernel(in_ref, token_ref, out_ref):
        del in_ref, token_ref, out_ref

    return pl.pallas_call(
        kernel,
        out_shape=jax.ShapeDtypeStruct(array.shape, array.dtype),
        in_specs=[pl.BlockSpec(memory_space=pl.ANY)] * 2,
        out_specs=pl.BlockSpec(memory_space=pl.ANY),
        input_output_aliases={0: 0},
        compiler_params=pltpu.CompilerParams(vmem_limit_bytes=1 << 20),
        cost_estimate=pl.CostEstimate(flops=1, bytes_accessed=1, transcendentals=0),
        name="behind",
    )(array, token)


def row_loads(x_ref, gid_ref, x, gid, sem, start):
    return (
        pltpu.make_async_copy(x_ref.at[:, pl.ds(start, x.shape[1])], x, sem.at[0]),
        pltpu.make_async_copy(gid_ref, gid, sem.at[1]),
    )


def mask_rows(groups, x, gid_ref, out):
    wide = x.shape[1]
    gid = jnp.transpose(jnp.broadcast_to(gid_ref[...], (128, gid_ref.shape[1])))
    for group in range(groups):
        keep = gid == group
        for cut in range(0, wide, 128):
            part = x[:, cut : cut + 128]
            out[:, group * wide + cut : group * wide + cut + 128] = jnp.where(keep, part, jnp.zeros_like(part))
    return gid


def row_scratch(rows, groups, wide):
    return [
        pltpu.VMEM((rows, groups * wide), BF16),
        pltpu.VMEM((rows, wide), BF16),
        pltpu.VMEM((1, rows), jnp.int32),
        pltpu.SemaphoreType.DMA((2,)),
    ]


def product(a, b):
    return lax.dot_general(a, b, (((1,), (1,)), ((), ())), preferred_element_type=F32)


def part_kernel(groups, share, start_at, code_ref, x_ref, gid_ref, own_ref, other_ref, *rest):
    out_ref, cents, rows_of, x, gid_row, sem = rest
    loads = row_loads(x_ref, gid_ref, x, gid_row, sem, start_at)
    wide = own_ref.shape[1]
    blocks = own_ref.shape[0] // share

    @pl.when(pl.program_id(0) == 0)
    def _():
        for load in loads:
            load.start()
        for piece, ref in enumerate((own_ref, other_ref)):
            for block in range(blocks):
                code = code_ref[piece * blocks + block]
                slot = pl.multiple_of(code // groups * share, share)
                cents[pl.ds(slot, share), pl.ds(pl.multiple_of(code % groups * wide, 128), wide)] = ref[block * share : (block + 1) * share, :]
        for load in loads:
            load.wait()
        mask_rows(groups, x, gid_row, rows_of)

    step = out_ref.shape[1]
    start = pl.multiple_of(pl.program_id(0) * step, step)
    out_ref[...] = product(rows_of[...], cents[pl.ds(start, step), :]).astype(BF16)


def part_scores(token, samples, gid, codes, pieces, before, groups, keys, share, start_at):
    rows = samples.shape[0]
    wide = pieces[0].shape[1]
    half = pieces[0].shape[0] * len(pieces) // groups
    step = min(256, half)
    steps = half // step
    at = 0 if before is None else steps
    whole = pl.BlockSpec(memory_space=pltpu.VMEM)
    extra = [] if before is None else [before]
    anywhere = pl.BlockSpec(memory_space=pl.ANY)

    def kernel(code_ref, *refs):
        count = 4 + len(extra)
        part_kernel(groups, share, start_at, code_ref, *refs[:4], refs[count + 1], *refs[-5:])
        refs[count + 2][...] = refs[count][...]

    return pl.pallas_call(
        kernel,
        grid_spec=pltpu.PrefetchScalarGridSpec(
            num_scalar_prefetch=1,
            grid=(steps,),
            in_specs=[anywhere] * 2 + [whole] * 2 + [anywhere] * len(extra) + [whole],
            out_specs=[pl.BlockSpec((rows, step), lambda i, w: (0, i + at)), whole],
            scratch_shapes=[
                pltpu.VMEM((half, groups * wide), BF16),
                *row_scratch(rows, groups, wide),
            ],
        ),
        out_shape=[jax.ShapeDtypeStruct((rows, keys), BF16), token_shape()],
        input_output_aliases={} if before is None else {5: 0},
        compiler_params=pltpu.CompilerParams(vmem_limit_bytes=51 << 20),
        cost_estimate=pl.CostEstimate(flops=1, bytes_accessed=1, transcendentals=0),
        name="part_scores",
    )(codes, samples, gid, *pieces, *extra, token)


def final_kernel(groups, share, start_at, code_ref, slot_ref, x_ref, gid_ref, half_ref, *rest):
    pieces = 4
    piece_refs, total_refs = rest[:pieces], rest[pieces : pieces + 2]
    out_ref, cents, half, pick, rows_of, x, gid_row, sem = rest[-8:]
    loads = row_loads(x_ref, gid_ref, x, gid_row, sem, start_at)
    keys = cents.shape[0]
    wide = cents.shape[1] // groups
    members = keys // share
    blocks = code_ref.shape[0] // pieces
    lanes = 128

    @pl.when(pl.program_id(0) == 0)
    def _():
        for load in loads:
            load.start()
        half[...] = half_ref[...]
        for piece, ref in enumerate(piece_refs):
            for block in range(blocks):
                code = code_ref[piece * blocks + block]
                group = code // members
                row_at = pl.multiple_of((code % members) * share, share)
                cents[pl.ds(row_at, share), pl.ds(pl.multiple_of(group * wide, lanes), wide)] = ref[
                    block * share : (block + 1) * share, :
                ]
                if share >= lanes:
                    tail = ref[blocks * share :, :].astype(F32)
                    at = tail.shape[0] - blocks + block
                    lines = pl.ds(pl.multiple_of(row_at, lanes), share)
                    line = lax.broadcasted_iota(jnp.int32, (half.shape[0], share), 0)
                    filled = half[:, lines]
                    for term in range(PARTS):
                        row = tail[at : at + 1, term * share : (term + 1) * share]
                        filled = jnp.where(line == group + term * groups, row, filled)
                    half[:, lines] = filled
        for load in loads:
            load.wait()
        gid = mask_rows(groups, x, gid_row, rows_of)[:, : pick.shape[1]]
        lane = lax.broadcasted_iota(jnp.int32, pick.shape, 1)
        hit = (lane % groups == gid) & (lane < PARTS * groups)
        pick[...] = jnp.where(hit, -1.0, 0.0).astype(BF16)

    step = out_ref.shape[1]
    start = pl.multiple_of(pl.program_id(0) * step, step)
    dots = product(rows_of[...], cents[pl.ds(start, step), :])
    offsets = half[:, pl.ds(start, step)].astype(BF16)
    dots += jnp.dot(pick[...], offsets, preferred_element_type=F32)
    cut = step // 2
    out_ref[:, :cut] = (dots[:, :cut] + total_refs[0][...].astype(F32)).astype(BF16)
    out_ref[:, cut:] = (dots[:, cut:] + total_refs[1][...].astype(F32)).astype(BF16)


def final_scores(samples, gid, codes, slots, pieces, total, half, groups, keys, share, start_at):
    rows = samples.shape[0]
    wide = pieces[0].shape[1]
    step = min(256, keys)
    cut = step // 2
    whole = pl.BlockSpec(memory_space=pltpu.VMEM)
    return pl.pallas_call(
        functools.partial(final_kernel, groups, share, start_at),
        grid_spec=pltpu.PrefetchScalarGridSpec(
            num_scalar_prefetch=2,
            grid=(keys // step,),
            in_specs=[pl.BlockSpec(memory_space=pl.ANY)] * 2
            + [whole] * (1 + len(pieces))
            + [
                pl.BlockSpec((rows, cut), lambda i, c, s: (0, s[2 * i])),
                pl.BlockSpec((rows, cut), lambda i, c, s: (0, s[2 * i + 1])),
            ],
            out_specs=pl.BlockSpec((rows, step), lambda i, c, s: (0, i)),
            scratch_shapes=[
                pltpu.VMEM((keys, groups * wide), BF16),
                pltpu.VMEM(half.shape, F32),
                pltpu.VMEM((rows, TILE), BF16),
                *row_scratch(rows, groups, wide),
            ],
        ),
        out_shape=jax.ShapeDtypeStruct((rows, keys), BF16),
        compiler_params=pltpu.CompilerParams(vmem_limit_bytes=50 << 20),
        cost_estimate=pl.CostEstimate(flops=1, bytes_accessed=1, transcendentals=0),
        name="final_scores",
    )(codes, slots, samples, gid, half, *pieces, total, total)


def per_device(samples, coarse_label, fine_label, live_rows, old_centroids):
    groups = lax.axis_size("coarse")
    members = lax.axis_size("member")
    z = lax.axis_index("coarse")
    me = lax.axis_index("member")
    core = me & 1
    rows, width = samples.shape
    keys = old_centroids.shape[1]
    share = keys // members
    columns = streams_of(width)
    streams = range(len(columns))
    half_keys = groups * keys // 2
    blocks = half_keys // share
    outer_bits = groups.bit_length() - 1
    turned = orders_of(groups, members)
    stages = len(turned[0, 0])
    base = 256 // (groups * members // 2) + 1
    digits = 1
    while base**digits <= 2 * rows:
        digits += 1

    live = jnp.arange(rows, dtype=jnp.int32) < live_rows[0]
    label = jnp.where(live, coarse_label[:, 0] * keys + fine_label, -1)
    sibling = lambda a: exchange(a, lambda gz, m: (gz, m ^ 1), groups, members)
    other_samples = sibling(samples)
    label_all = jnp.concatenate([label, sibling(label)])

    group_of = label_all // keys
    fine = label_all % keys
    owner = fine // share
    mine = (label_all >= 0) & ((owner & 1) == core)

    def of_core(make):
        return jnp.where(core == 0, make(0), make(1))

    def pairing(stage, stream):
        def partner(gz, m):
            group_mask, member_mask = turned[m & 1, stream][stage]
            return gz ^ group_mask, m ^ member_mask

        return partner

    tail = pad_rows(blocks)
    token = start_token = jnp.zeros((8, 128), F32)
    rows_of, tiles = [], []
    for stream, (start, wide) in enumerate(columns):
        place = of_core(
            lambda c: block_position(group_of ^ z, owner ^ me, turned[c, stream], outer_bits)
        )
        rows_of.append(jnp.where(mine, place * share + fine % share, -1)[None, :])
        tile = None
        if stream == 0:
            in_block = (jnp.where(mine, place, -1)[:, None] == jnp.arange(tail)[None, :]).astype(BF16)
            in_lane = ((fine % share)[:, None] == jnp.arange(share)[None, :]).astype(BF16)
            counted = lax.dot_general(
                in_block, in_lane, (((0,), (0,)), ((), ())), preferred_element_type=F32
            ).astype(jnp.int32)
            tile = [(counted // base**digit) % base for digit in range(digits)]
            tile = jnp.concatenate(tile, axis=1).astype(BF16)
            tile = jnp.pad(tile, ((0, 0), (0, wide - digits * share)))
        tiles.append(tile)

    half_keys //= 2
    send, keep = [None] * 2, [None] * 2
    for part, found in enumerate((send, keep)):
        for stream, (start, wide) in enumerate(columns):
            found[stream], token = key_sums(
                token, rows_of[stream], samples, other_samples, tiles[stream], part * half_keys, half_keys, start, wide
            )

    tokens = [start_token] * 2
    own_turn = (2, 3, 4)

    def step_token(step, stream):
        return tokens[stream if stream == 0 and step in own_turn else 1 - stream]

    old_share = lax.dynamic_slice(old_centroids[0], (me * share, 0), (share, width))

    def bf(count, stream, tailed):
        rows_out = count * share + (tail if stream == tailed else 0)
        return jax.ShapeDtypeStruct((rows_out, columns[stream][1]), BF16)

    share_f32 = [jax.ShapeDtypeStruct((share, wide), F32) for _, wide in columns]
    held, fresh, near = [None] * 2, [None] * 2, [None] * 2
    count = blocks // 2
    for stage in range(stages - 1):
        for stream, (start, wide) in enumerate(columns):
            got = exchange(send[stream], pairing(stage, stream), groups, members)
            if stage < stages - 2:
                send[stream], keep[stream], tokens[stream] = small_call(
                    functools.partial(fold_kernel, count // 2 * share, count),
                    "fold",
                    [bf(count // 2, stream, 0)] * 2,
                    step_token(stage, stream),
                    got,
                    keep[stream],
                )
            else:
                send[stream], near[stream], tokens[stream] = small_call(
                    functools.partial(seed_kernel, share, count),
                    "seed",
                    [bf(2, stream, 0), share_f32[stream]],
                    step_token(stage, stream),
                    got,
                    keep[stream],
                    old_share[:, start : start + wide],
                )
        count //= 2
    column = jax.ShapeDtypeStruct((2 * share, 1), F32)
    for stream in streams:
        got = exchange(send[stream], pairing(stages - 1, stream), groups, members)
        if stream == 0:
            fresh[0], held[0], scale, norm, tokens[stream] = small_call(
                functools.partial(first_kernel, share, base, digits),
                "first_centroids",
                [share_f32[0], bf(2, 0, 1), column, column],
                step_token(stages - 1, stream),
                got,
                send[0],
                near[0],
            )
        else:
            fresh[1], held[1], tokens[stream] = small_call(
                functools.partial(last_kernel, share, tail),
                "last_centroids",
                [jax.ShapeDtypeStruct((share, width), F32), bf(2, 1, 1)],
                step_token(stages - 1, stream),
                got,
                send[1],
                near[1],
                scale,
                norm,
                fresh[0],
            )
    half_blocks = blocks // 2
    quarter = half_blocks // groups
    inner_of = [[dim for dim in turned[c, 0] if dim[1]] for c in range(2)]

    def part_codes(part):
        codes = []
        for flip in range(2):
            for block in range(half_blocks):
                code = []
                for c in range(2):
                    group_rel, member_rel = relative_of(part * half_blocks + block, turned[c, 0])
                    spot = block_position(0, member_rel, inner_of[c], outer_bits) % quarter
                    code.append((spot + flip * quarter) * groups + (z ^ group_rel))
                codes.append(jnp.where(core ^ flip == 0, *code))
        return jnp.stack(codes).astype(jnp.int32)

    gid = jnp.where(live, coarse_label[:, 0], -1)[None, :]
    count = 2
    arrived = [None] * 2
    for stage in reversed(range(stages - 1)):
        for stream in streams:
            got = exchange(held[stream], pairing(stage, stream), groups, members)
            if stage:
                held[stream], tokens[stream] = small_call(
                    functools.partial(join_kernel, count * share, count),
                    "join",
                    [bf(2 * count, stream, 1)],
                    step_token(2 * stages - 2 - stage, stream),
                    got,
                    held[stream],
                )
            else:
                arrived[stream] = got
            if (stage, stream) == (1, 0):
                total, tokens[0] = part_scores(
                    tokens[0], samples, gid, part_codes(1), [held[0], sibling(held[0])], None, groups, keys, share, 0
                )
        count *= 2

    def codes_of(stream, part, flip):
        codes = []
        for block in range(half_blocks):
            rel = [relative_of(part * half_blocks + block, turned[c, stream]) for c in range(2)]
            holder = core ^ flip
            group_rel = jnp.where(holder == 0, rel[0][0], rel[1][0])
            member_rel = jnp.where(holder == 0, rel[0][1], rel[1][1])
            codes.append((z ^ group_rel) * members + (me ^ flip ^ member_rel))
        return jnp.stack(codes).astype(jnp.int32)

    total, token = part_scores(
        tokens[1], samples, gid, part_codes(0), [arrived[0], sibling(arrived[0])], total, groups, keys, share, 0
    )
    last = behind(arrived[1], token)
    every = jnp.arange(members, dtype=jnp.int32)
    flip_of = (every ^ me) & 1
    spot = jnp.where(
        (core ^ flip_of) == 0,
        *(block_position(0, every ^ me, inner_of[c], outer_bits) for c in range(2)),
    )
    slots = jnp.where(spot >= quarter, spot - quarter, spot + 2 * quarter) + flip_of * quarter
    flat = [piece for got in (last, held[1]) for piece in (got, sibling(got))]
    codes = jnp.concatenate([codes_of(1, part, flip) for part in range(2) for flip in range(2)])
    half = jnp.zeros((TILE, keys), F32)
    if share < 128:
        norm_rows = []
        for piece in flat:
            norm_rows.append(piece[half_blocks * share + tail - half_blocks :].astype(F32))
        norm_rows = jnp.concatenate(norm_rows)
        spread = (codes[None, :] == jnp.arange(groups * members, dtype=jnp.int32)[:, None]).astype(F32)
        for term in range(PARTS):
            found = jnp.dot(
                spread, norm_rows[:, term * share : (term + 1) * share], precision=lax.Precision.HIGHEST
            )
            half = half.at[term * groups : (term + 1) * groups].set(found.reshape(groups, keys))
        lane = jnp.arange(keys, dtype=jnp.int32)
        source = jnp.repeat(slots, share) * share + lane % share
        move = (lane[:, None] == source[None, :]).astype(F32)
        total = jnp.dot(total, move.astype(BF16))
        slots = jnp.arange(keys // 128, dtype=jnp.int32)
    scores = final_scores(samples, gid, codes, slots, flat, total, half, groups, keys, share, columns[1][0])
    return scores, fresh[1][None]


def solution(mesh):
    return jax.shard_map(
        per_device,
        mesh=mesh,
        in_specs=(
            P(AXES, None),
            P(AXES, None),
            P(AXES),
            P(AXES),
            P("coarse", None, None),
        ),
        out_specs=(P(AXES, None), P("coarse", "member", None)),
        check_vma=False,
    )
```

```python
import functools

import jax
import jax.numpy as jnp
from jax import lax
from jax.experimental import pallas as pl
from jax.experimental.pallas import tpu as pltpu
from jax.sharding import PartitionSpec as P

AXES = ("coarse", "member")
TILE = 16
PRIOR = 16.0
PARTS = 2
F32 = jnp.float32
BF16 = jnp.bfloat16


def pad_rows(blocks):
    return max(TILE, -(-blocks // TILE) * TILE)


def streams_of(width):
    wide = width // 2
    return ((0, wide), (wide, wide))


def orders_of(groups, members):
    inner = [(0, 1 << bit) for bit in range(1, members.bit_length() - 1)]
    outer = [((1 << (bit + 1)) - 1, 0) for bit in range(groups.bit_length() - 1)]
    cut = len(inner) // 2
    other = inner[cut:] + inner[:cut]
    found = {}
    found[0, 0] = inner[:cut] + outer[:1] + inner[cut:] + outer[1:]
    found[1, 0] = other[:cut] + outer[:1] + other[cut:] + outer[1:]
    found[0, 1] = found[1, 0]
    found[1, 1] = found[0, 0]
    return found


def exchange(array, partner, groups, members):
    pairs = []
    for z in range(groups):
        for m in range(members):
            to_z, to_m = partner(z, m)
            pairs.append((z * members + m, to_z * members + to_m))
    return lax.ppermute(array, AXES, pairs)


def coefficients(group_rel, member_rel, dims, outer_bits):
    out = []
    for group_mask, member_mask in dims:
        if member_mask:
            out.append((member_rel >> (member_mask.bit_length() - 1)) & 1)
        else:
            top = group_mask.bit_length() - 1
            bit = (group_rel >> top) & 1
            if top + 1 < outer_bits:
                bit = bit ^ ((group_rel >> (top + 1)) & 1)
            out.append(bit)
    return out


def block_position(group_rel, member_rel, dims, outer_bits):
    place = 0
    for bit in coefficients(group_rel, member_rel, dims, outer_bits):
        place = place * 2 + (1 - bit)
    return place


def relative_of(place, dims):
    group_rel = member_rel = 0
    for at, (group_mask, member_mask) in enumerate(dims):
        if not (place >> (len(dims) - 1 - at)) & 1:
            group_rel ^= group_mask
            member_rel ^= member_mask
    return group_rel, member_rel


def token_shape():
    return jax.ShapeDtypeStruct((8, 128), F32)


def hand_on(kernel, inputs):
    def run(*refs):
        kernel(*refs[:inputs], *refs[inputs + 1 : -1])
        refs[-1][...] = refs[inputs][...]

    return run


def sums_kernel(base, pos_ref, own_ref, other_ref, *rest):
    out_ref = rest[-1]
    rows = own_ref.shape[0]
    keys = out_ref.shape[0] - (rest[0].shape[0] if len(rest) > 1 else 0)
    key = lax.broadcasted_iota(jnp.int32, (keys, rows), 0) + base
    first = jnp.where(pos_ref[:, :rows] == key, 1.0, 0.0).astype(BF16)
    second = jnp.where(pos_ref[:, rows:] == key, 1.0, 0.0).astype(BF16)
    total = jnp.dot(first, own_ref[...], preferred_element_type=F32)
    total += jnp.dot(second, other_ref[...], preferred_element_type=F32)
    out_ref[:keys, :] = total.astype(BF16)
    if len(rest) > 1:
        out_ref[keys:, :] = rest[0][...]


def key_sums(token, pos_row, own, other, count_tile, base, keys):
    rows, wide = own.shape
    extra = [] if count_tile is None else [count_tile]
    out_rows = keys + sum(e.shape[0] for e in extra)
    whole = lambda shape: pl.BlockSpec(shape, lambda i: (0, 0))
    return pl.pallas_call(
        hand_on(functools.partial(sums_kernel, base), 3 + len(extra)),
        grid=(1,),
        out_shape=[jax.ShapeDtypeStruct((out_rows, wide), BF16), token_shape()],
        in_specs=[
            whole((1, 2 * rows)),
            whole((rows, wide)),
            whole((rows, wide)),
        ]
        + [whole(e.shape) for e in extra]
        + [whole(token.shape)],
        out_specs=[whole((out_rows, wide)), whole(token.shape)],
        compiler_params=pltpu.CompilerParams(vmem_limit_bytes=16 << 20),
        cost_estimate=pl.CostEstimate(
            flops=2 * keys * 2 * rows * wide, bytes_accessed=(4 * rows + 2 * keys) * wide, transcendentals=0
        ),
        name="key_sums",
    )(pos_row, own, other, *extra, token)


def small_call(kernel, name, outs, token, *args):
    whole = pl.BlockSpec(memory_space=pltpu.VMEM)
    moved = sum(a.size * a.dtype.itemsize for a in (*args, *outs))
    return pl.pallas_call(
        hand_on(kernel, len(args)),
        out_shape=[*outs, token_shape()],
        in_specs=[whole] * (len(args) + 1),
        out_specs=[whole] * (len(outs) + 1),
        compiler_params=pltpu.CompilerParams(vmem_limit_bytes=4 << 20),
        cost_estimate=pl.CostEstimate(flops=moved // 2, bytes_accessed=moved, transcendentals=0),
        name=name,
    )(*args, token)


def add_pair(got_ref, keep_ref, start, stop):
    return got_ref[start:stop, :].astype(F32) + keep_ref[start:stop, :].astype(F32)


def add_tail(got_ref, keep_ref, body, shift):
    kept = keep_ref[body:, :].astype(F32)
    return (kept + pltpu.roll(got_ref[body:, :].astype(F32), shift, 0)).astype(BF16)


def fold_kernel(half, shift, got_ref, keep_ref, send_out, keep_out):
    send_out[:half, :] = add_pair(got_ref, keep_ref, 0, half).astype(BF16)
    keep_out[:half, :] = add_pair(got_ref, keep_ref, half, 2 * half).astype(BF16)
    if got_ref.shape[0] > 2 * half:
        tail = add_tail(got_ref, keep_ref, 2 * half, shift)
        send_out[half:, :] = tail
        keep_out[half:, :] = tail


def seed_kernel(share, shift, got_ref, keep_ref, old_ref, send_out, near_out):
    two = 2 * share
    near = add_pair(got_ref, keep_ref, share, two) + PRIOR * old_ref[...]
    near_out[...] = near
    send_out[:share, :] = add_pair(got_ref, keep_ref, 0, share).astype(BF16)
    send_out[share:two, :] = near.astype(BF16)
    if got_ref.shape[0] > two:
        send_out[two:, :] = add_tail(got_ref, keep_ref, two, shift)


def summed(share, block, got_ref, sent_ref, near_ref):
    if block == 0:
        return sent_ref[:share, :].astype(F32) + got_ref[share : 2 * share, :].astype(F32)
    return near_ref[...] + got_ref[:share, :].astype(F32)


def square_sums(rounded):
    return jnp.sum(jnp.square(rounded.astype(F32)), axis=1, keepdims=True)


def first_kernel(share, base, digits, got_ref, sent_ref, near_ref, fresh_out, cents_out, scale_out, norm_out):
    two = 2 * share
    wide = got_ref.shape[1]
    last = sent_ref.shape[0] - two - 1
    lane = lax.broadcasted_iota(jnp.int32, (share, wide), 1)
    line = lax.broadcasted_iota(jnp.int32, (share, wide), 0)
    mine = sent_ref[two:, :].astype(F32)
    theirs = got_ref[two:, :].astype(F32)
    for block in range(2):
        row = mine[last - 1 + block : last + block, :] + theirs[last - block : last - block + 1, :]
        count = jnp.full((share, 1), PRIOR, F32)
        for digit in range(digits):
            hit = jnp.where(lane == line + digit * share, row, 0.0)
            count += jnp.sum(hit, axis=1, keepdims=True) * float(base**digit)
        scale_out[block * share : (block + 1) * share, :] = count
        fresh = summed(share, block, got_ref, sent_ref, near_ref) / count
        rounded = fresh.astype(BF16)
        cents_out[block * share : (block + 1) * share, :] = rounded
        norm_out[block * share : (block + 1) * share, :] = square_sums(rounded)
        if block == 1:
            fresh_out[...] = fresh


def last_kernel(share, tail, got_ref, sent_ref, near_ref, scale_ref, norm_ref, first_ref, fresh_out, cents_out):
    two = 2 * share
    wide = got_ref.shape[1]
    lane = lax.broadcasted_iota(jnp.int32, (share, wide), 1)
    line = lax.broadcasted_iota(jnp.int32, (share, wide), 0)
    tile = jnp.zeros((tail, wide), F32)
    tile_row = lax.broadcasted_iota(jnp.int32, (tail, wide), 0)
    for block in range(2):
        part = slice(block * share, (block + 1) * share)
        fresh = summed(share, block, got_ref, sent_ref, near_ref) / scale_ref[part, :]
        rounded = fresh.astype(BF16)
        cents_out[part, :] = rounded
        if block == 1:
            before = first_ref.shape[1]
            fresh_out[:, :before] = first_ref[...]
            fresh_out[:, before:] = fresh
        norm = 0.5 * (norm_ref[part, :] + square_sums(rounded))
        spread = jnp.zeros((1, wide), F32)
        for term_at in range(PARTS):
            term = norm.astype(BF16).astype(F32)
            norm = norm - term
            hit = jnp.where(lane == line + term_at * share, term, 0.0)
            spread += jnp.sum(hit, axis=0, keepdims=True)
        tile = jnp.where(tile_row == tail - 2 + block, spread, tile)
    cents_out[two:, :] = tile.astype(BF16)


def join_kernel(body, shift, got_ref, held_ref, out_ref):
    out_ref[:body, :] = got_ref[:body, :]
    out_ref[body : 2 * body, :] = held_ref[:body, :]
    if held_ref.shape[0] > body:
        rows = held_ref.shape[0] - body
        moved = pltpu.roll(got_ref[body:, :].astype(F32), rows - shift, 0)
        out_ref[2 * body :, :] = (held_ref[body:, :].astype(F32) + moved).astype(BF16)


def behind(array, token):
    def kernel(in_ref, token_ref, out_ref):
        del in_ref, token_ref, out_ref

    return pl.pallas_call(
        kernel,
        out_shape=jax.ShapeDtypeStruct(array.shape, array.dtype),
        in_specs=[pl.BlockSpec(memory_space=pl.ANY)] * 2,
        out_specs=pl.BlockSpec(memory_space=pl.ANY),
        input_output_aliases={0: 0},
        compiler_params=pltpu.CompilerParams(vmem_limit_bytes=1 << 20),
        cost_estimate=pl.CostEstimate(flops=1, bytes_accessed=1, transcendentals=0),
        name="behind",
    )(array, token)


def row_loads(x_ref, gid_ref, x, gid, sem, start):
    return (
        pltpu.make_async_copy(x_ref.at[:, pl.ds(start, x.shape[1])], x, sem.at[0]),
        pltpu.make_async_copy(gid_ref, gid, sem.at[1]),
    )


def mask_rows(groups, x, gid_ref, out):
    wide = x.shape[1]
    gid = jnp.transpose(jnp.broadcast_to(gid_ref[...], (128, gid_ref.shape[1])))
    for group in range(groups):
        keep = gid == group
        for cut in range(0, wide, 128):
            part = x[:, cut : cut + 128]
            out[:, group * wide + cut : group * wide + cut + 128] = jnp.where(keep, part, jnp.zeros_like(part))
    return gid


def row_scratch(rows, groups, wide):
    return [
        pltpu.VMEM((rows, groups * wide), BF16),
        pltpu.VMEM((rows, wide), BF16),
        pltpu.VMEM((1, rows), jnp.int32),
        pltpu.SemaphoreType.DMA((2,)),
    ]


def product(a, b):
    return lax.dot_general(a, b, (((1,), (1,)), ((), ())), preferred_element_type=F32)


def part_kernel(groups, share, start_at, code_ref, x_ref, gid_ref, own_ref, other_ref, *rest):
    out_ref, cents, rows_of, x, gid_row, sem = rest
    loads = row_loads(x_ref, gid_ref, x, gid_row, sem, start_at)
    wide = own_ref.shape[1]
    blocks = own_ref.shape[0] // share

    @pl.when(pl.program_id(0) == 0)
    def _():
        for load in loads:
            load.start()
        for piece, ref in enumerate((own_ref, other_ref)):
            for block in range(blocks):
                code = code_ref[piece * blocks + block]
                slot = pl.multiple_of(code // groups * share, share)
                cents[pl.ds(slot, share), pl.ds(pl.multiple_of(code % groups * wide, 128), wide)] = ref[block * share : (block + 1) * share, :]
        for load in loads:
            load.wait()
        mask_rows(groups, x, gid_row, rows_of)

    step = out_ref.shape[1]
    start = pl.multiple_of(pl.program_id(0) * step, step)
    out_ref[...] = product(rows_of[...], cents[pl.ds(start, step), :]).astype(BF16)


def part_scores(token, samples, gid, codes, pieces, before, groups, keys, share, start_at):
    rows = samples.shape[0]
    wide = pieces[0].shape[1]
    half = pieces[0].shape[0] * len(pieces) // groups
    step = min(256, half)
    steps = half // step
    at = 0 if before is None else steps
    whole = pl.BlockSpec(memory_space=pltpu.VMEM)
    extra = [] if before is None else [before]
    anywhere = pl.BlockSpec(memory_space=pl.ANY)

    def kernel(code_ref, *refs):
        count = 4 + len(extra)
        part_kernel(groups, share, start_at, code_ref, *refs[:4], refs[count + 1], *refs[-5:])
        refs[count + 2][...] = refs[count][...]

    return pl.pallas_call(
        kernel,
        grid_spec=pltpu.PrefetchScalarGridSpec(
            num_scalar_prefetch=1,
            grid=(steps,),
            in_specs=[anywhere] * 2 + [whole] * 2 + [anywhere] * len(extra) + [whole],
            out_specs=[pl.BlockSpec((rows, step), lambda i, w: (0, i + at)), whole],
            scratch_shapes=[
                pltpu.VMEM((half, groups * wide), BF16),
                *row_scratch(rows, groups, wide),
            ],
        ),
        out_shape=[jax.ShapeDtypeStruct((rows, keys), BF16), token_shape()],
        input_output_aliases={} if before is None else {5: 0},
        compiler_params=pltpu.CompilerParams(vmem_limit_bytes=51 << 20),
        cost_estimate=pl.CostEstimate(flops=1, bytes_accessed=1, transcendentals=0),
        name="part_scores",
    )(codes, samples, gid, *pieces, *extra, token)


def final_kernel(groups, share, start_at, code_ref, slot_ref, x_ref, gid_ref, half_ref, *rest):
    pieces = 4
    piece_refs, total_refs = rest[:pieces], rest[pieces : pieces + 2]
    out_ref, cents, half, pick, rows_of, x, gid_row, sem = rest[-8:]
    loads = row_loads(x_ref, gid_ref, x, gid_row, sem, start_at)
    keys = cents.shape[0]
    wide = cents.shape[1] // groups
    members = keys // share
    blocks = code_ref.shape[0] // pieces
    lanes = 128

    @pl.when(pl.program_id(0) == 0)
    def _():
        for load in loads:
            load.start()
        half[...] = half_ref[...]
        for piece, ref in enumerate(piece_refs):
            for block in range(blocks):
                code = code_ref[piece * blocks + block]
                group = code // members
                row_at = pl.multiple_of((code % members) * share, share)
                cents[pl.ds(row_at, share), pl.ds(pl.multiple_of(group * wide, lanes), wide)] = ref[
                    block * share : (block + 1) * share, :
                ]
                if share >= lanes:
                    tail = ref[blocks * share :, :].astype(F32)
                    at = tail.shape[0] - blocks + block
                    lines = pl.ds(pl.multiple_of(row_at, lanes), share)
                    line = lax.broadcasted_iota(jnp.int32, (half.shape[0], share), 0)
                    filled = half[:, lines]
                    for term in range(PARTS):
                        row = tail[at : at + 1, term * share : (term + 1) * share]
                        filled = jnp.where(line == group + term * groups, row, filled)
                    half[:, lines] = filled
        for load in loads:
            load.wait()
        gid = mask_rows(groups, x, gid_row, rows_of)[:, : pick.shape[1]]
        lane = lax.broadcasted_iota(jnp.int32, pick.shape, 1)
        hit = (lane % groups == gid) & (lane < PARTS * groups)
        pick[...] = jnp.where(hit, -1.0, 0.0).astype(BF16)

    step = out_ref.shape[1]
    start = pl.multiple_of(pl.program_id(0) * step, step)
    dots = product(rows_of[...], cents[pl.ds(start, step), :])
    offsets = half[:, pl.ds(start, step)].astype(BF16)
    dots += jnp.dot(pick[...], offsets, preferred_element_type=F32)
    cut = step // 2
    out_ref[:, :cut] = (dots[:, :cut] + total_refs[0][...].astype(F32)).astype(BF16)
    out_ref[:, cut:] = (dots[:, cut:] + total_refs[1][...].astype(F32)).astype(BF16)


def final_scores(samples, gid, codes, slots, pieces, total, half, groups, keys, share, start_at):
    rows = samples.shape[0]
    wide = pieces[0].shape[1]
    step = min(256, keys)
    cut = step // 2
    whole = pl.BlockSpec(memory_space=pltpu.VMEM)
    return pl.pallas_call(
        functools.partial(final_kernel, groups, share, start_at),
        grid_spec=pltpu.PrefetchScalarGridSpec(
            num_scalar_prefetch=2,
            grid=(keys // step,),
            in_specs=[pl.BlockSpec(memory_space=pl.ANY)] * 2
            + [whole] * (1 + len(pieces))
            + [
                pl.BlockSpec((rows, cut), lambda i, c, s: (0, s[2 * i])),
                pl.BlockSpec((rows, cut), lambda i, c, s: (0, s[2 * i + 1])),
            ],
            out_specs=pl.BlockSpec((rows, step), lambda i, c, s: (0, i)),
            scratch_shapes=[
                pltpu.VMEM((keys, groups * wide), BF16),
                pltpu.VMEM(half.shape, F32),
                pltpu.VMEM((rows, TILE), BF16),
                *row_scratch(rows, groups, wide),
            ],
        ),
        out_shape=jax.ShapeDtypeStruct((rows, keys), BF16),
        compiler_params=pltpu.CompilerParams(vmem_limit_bytes=50 << 20),
        cost_estimate=pl.CostEstimate(flops=1, bytes_accessed=1, transcendentals=0),
        name="final_scores",
    )(codes, slots, samples, gid, half, *pieces, total, total)


def per_device(samples, coarse_label, fine_label, live_rows, old_centroids):
    groups = lax.axis_size("coarse")
    members = lax.axis_size("member")
    z = lax.axis_index("coarse")
    me = lax.axis_index("member")
    core = me & 1
    rows, width = samples.shape
    keys = old_centroids.shape[1]
    share = keys // members
    columns = streams_of(width)
    streams = range(len(columns))
    half_keys = groups * keys // 2
    blocks = half_keys // share
    outer_bits = groups.bit_length() - 1
    turned = orders_of(groups, members)
    stages = len(turned[0, 0])
    base = 256 // (groups * members // 2) + 1
    digits = 1
    while base**digits <= 2 * rows:
        digits += 1

    live = jnp.arange(rows, dtype=jnp.int32) < live_rows[0]
    label = jnp.where(live, coarse_label[:, 0] * keys + fine_label, -1)
    sibling = lambda a: exchange(a, lambda gz, m: (gz, m ^ 1), groups, members)
    cut_rows = [samples[:, start : start + wide] for start, wide in streams_of(width)]
    other_rows = [sibling(part) for part in cut_rows]
    label_all = jnp.concatenate([label, sibling(label)])

    group_of = label_all // keys
    fine = label_all % keys
    owner = fine // share
    mine = (label_all >= 0) & ((owner & 1) == core)

    def of_core(make):
        return jnp.where(core == 0, make(0), make(1))

    def pairing(stage, stream):
        def partner(gz, m):
            group_mask, member_mask = turned[m & 1, stream][stage]
            return gz ^ group_mask, m ^ member_mask

        return partner

    tail = pad_rows(blocks)
    token = start_token = jnp.zeros((8, 128), F32)
    rows_of, tiles = [], []
    for stream, (start, wide) in enumerate(columns):
        place = of_core(
            lambda c: block_position(group_of ^ z, owner ^ me, turned[c, stream], outer_bits)
        )
        rows_of.append(jnp.where(mine, place * share + fine % share, -1)[None, :])
        tile = None
        if stream == 0:
            in_block = (jnp.where(mine, place, -1)[:, None] == jnp.arange(tail)[None, :]).astype(BF16)
            in_lane = ((fine % share)[:, None] == jnp.arange(share)[None, :]).astype(BF16)
            counted = lax.dot_general(
                in_block, in_lane, (((0,), (0,)), ((), ())), preferred_element_type=F32
            ).astype(jnp.int32)
            tile = [(counted // base**digit) % base for digit in range(digits)]
            tile = jnp.concatenate(tile, axis=1).astype(BF16)
            tile = jnp.pad(tile, ((0, 0), (0, wide - digits * share)))
        tiles.append(tile)

    half_keys //= 2
    send, keep = [None] * 2, [None] * 2
    for part, found in enumerate((send, keep)):
        for stream, (start, wide) in enumerate(columns):
            found[stream], token = key_sums(
                token, rows_of[stream], cut_rows[stream], other_rows[stream], tiles[stream], part * half_keys, half_keys
            )

    tokens = [start_token] * 2
    own_turn = (2, 3, 4)

    def step_token(step, stream):
        return tokens[stream if stream == 0 and step in own_turn else 1 - stream]

    old_share = lax.dynamic_slice(old_centroids[0], (me * share, 0), (share, width))

    def bf(count, stream, tailed):
        rows_out = count * share + (tail if stream == tailed else 0)
        return jax.ShapeDtypeStruct((rows_out, columns[stream][1]), BF16)

    share_f32 = [jax.ShapeDtypeStruct((share, wide), F32) for _, wide in columns]
    held, fresh, near = [None] * 2, [None] * 2, [None] * 2
    count = blocks // 2
    for stage in range(stages - 1):
        for stream, (start, wide) in enumerate(columns):
            got = exchange(send[stream], pairing(stage, stream), groups, members)
            if stage < stages - 2:
                send[stream], keep[stream], tokens[stream] = small_call(
                    functools.partial(fold_kernel, count // 2 * share, count),
                    "fold",
                    [bf(count // 2, stream, 0)] * 2,
                    step_token(stage, stream),
                    got,
                    keep[stream],
                )
            else:
                send[stream], near[stream], tokens[stream] = small_call(
                    functools.partial(seed_kernel, share, count),
                    "seed",
                    [bf(2, stream, 0), share_f32[stream]],
                    step_token(stage, stream),
                    got,
                    keep[stream],
                    old_share[:, start : start + wide],
                )
        count //= 2
    column = jax.ShapeDtypeStruct((2 * share, 1), F32)
    for stream in streams:
        got = exchange(send[stream], pairing(stages - 1, stream), groups, members)
        if stream == 0:
            fresh[0], held[0], scale, norm, tokens[stream] = small_call(
                functools.partial(first_kernel, share, base, digits),
                "first_centroids",
                [share_f32[0], bf(2, 0, 1), column, column],
                step_token(stages - 1, stream),
                got,
                send[0],
                near[0],
            )
        else:
            fresh[1], held[1], tokens[stream] = small_call(
                functools.partial(last_kernel, share, tail),
                "last_centroids",
                [jax.ShapeDtypeStruct((share, width), F32), bf(2, 1, 1)],
                step_token(stages - 1, stream),
                got,
                send[1],
                near[1],
                scale,
                norm,
                fresh[0],
            )
    half_blocks = blocks // 2
    quarter = half_blocks // groups
    inner_of = [[dim for dim in turned[c, 0] if dim[1]] for c in range(2)]

    def part_codes(part):
        codes = []
        for flip in range(2):
            for block in range(half_blocks):
                code = []
                for c in range(2):
                    group_rel, member_rel = relative_of(part * half_blocks + block, turned[c, 0])
                    spot = block_position(0, member_rel, inner_of[c], outer_bits) % quarter
                    code.append((spot + flip * quarter) * groups + (z ^ group_rel))
                codes.append(jnp.where(core ^ flip == 0, *code))
        return jnp.stack(codes).astype(jnp.int32)

    gid = jnp.where(live, coarse_label[:, 0], -1)[None, :]
    count = 2
    arrived = [None] * 2
    for stage in reversed(range(stages - 1)):
        for stream in streams:
            got = exchange(held[stream], pairing(stage, stream), groups, members)
            if stage:
                held[stream], tokens[stream] = small_call(
                    functools.partial(join_kernel, count * share, count),
                    "join",
                    [bf(2 * count, stream, 1)],
                    step_token(2 * stages - 2 - stage, stream),
                    got,
                    held[stream],
                )
            else:
                arrived[stream] = got
            if (stage, stream) == (1, 1):
                total, tokens[1] = part_scores(
                    tokens[1], samples, gid, part_codes(1), [held[0], sibling(held[0])], None, groups, keys, share, 0
                )
        count *= 2

    def codes_of(stream, part, flip):
        codes = []
        for block in range(half_blocks):
            rel = [relative_of(part * half_blocks + block, turned[c, stream]) for c in range(2)]
            holder = core ^ flip
            group_rel = jnp.where(holder == 0, rel[0][0], rel[1][0])
            member_rel = jnp.where(holder == 0, rel[0][1], rel[1][1])
            codes.append((z ^ group_rel) * members + (me ^ flip ^ member_rel))
        return jnp.stack(codes).astype(jnp.int32)

    total, token = part_scores(
        tokens[1], samples, gid, part_codes(0), [arrived[0], sibling(arrived[0])], total, groups, keys, share, 0
    )
    last = behind(arrived[1], tokens[1])
    every = jnp.arange(members, dtype=jnp.int32)
    flip_of = (every ^ me) & 1
    spot = jnp.where(
        (core ^ flip_of) == 0,
        *(block_position(0, every ^ me, inner_of[c], outer_bits) for c in range(2)),
    )
    slots = jnp.where(spot >= quarter, spot - quarter, spot + 2 * quarter) + flip_of * quarter
    flat = [piece for got in (last, held[1]) for piece in (got, sibling(got))]
    codes = jnp.concatenate([codes_of(1, part, flip) for part in range(2) for flip in range(2)])
    half = jnp.zeros((TILE, keys), F32)
    if share < 128:
        norm_rows = []
        for piece in flat:
            norm_rows.append(piece[half_blocks * share + tail - half_blocks :].astype(F32))
        norm_rows = jnp.concatenate(norm_rows)
        spread = (codes[None, :] == jnp.arange(groups * members, dtype=jnp.int32)[:, None]).astype(F32)
        for term in range(PARTS):
            found = jnp.dot(
                spread, norm_rows[:, term * share : (term + 1) * share], precision=lax.Precision.HIGHEST
            )
            half = half.at[term * groups : (term + 1) * groups].set(found.reshape(groups, keys))
        lane = jnp.arange(keys, dtype=jnp.int32)
        source = jnp.repeat(slots, share) * share + lane % share
        move = (lane[:, None] == source[None, :]).astype(F32)
        total = jnp.dot(total, move.astype(BF16))
        slots = jnp.arange(keys // 128, dtype=jnp.int32)
    scores = final_scores(samples, gid, codes, slots, flat, total, half, groups, keys, share, columns[1][0])
    return scores, fresh[1][None]


def solution(mesh):
    return jax.shard_map(
        per_device,
        mesh=mesh,
        in_specs=(
            P(AXES, None),
            P(AXES, None),
            P(AXES),
            P(AXES),
            P("coarse", None, None),
        ),
        out_specs=(P(AXES, None), P("coarse", "member", None)),
        check_vma=False,
    )
```

```python
import functools

import jax
import jax.numpy as jnp
from jax import lax
from jax.experimental import pallas as pl
from jax.experimental.pallas import tpu as pltpu
from jax.sharding import PartitionSpec as P

AXES = ("coarse", "member")
TILE = 16
PRIOR = 16.0
PARTS = 2
F32 = jnp.float32
BF16 = jnp.bfloat16


def pad_rows(blocks):
    return max(TILE, -(-blocks // TILE) * TILE)


def streams_of(width):
    wide = width // 2
    return ((0, wide), (wide, wide))


def orders_of(groups, members):
    inner = [(0, 1 << bit) for bit in range(1, members.bit_length() - 1)]
    outer = [((1 << (bit + 1)) - 1, 0) for bit in range(groups.bit_length() - 1)]
    cut = len(inner) // 2
    other = inner[cut:] + inner[:cut]
    found = {}
    found[0, 0] = inner[:cut] + outer[:1] + inner[cut:] + outer[1:]
    found[1, 0] = other + outer
    found[0, 1] = other[:cut] + outer[:1] + other[cut:] + outer[1:]
    found[1, 1] = inner + outer
    return found


def exchange(array, partner, groups, members):
    pairs = []
    for z in range(groups):
        for m in range(members):
            to_z, to_m = partner(z, m)
            pairs.append((z * members + m, to_z * members + to_m))
    return lax.ppermute(array, AXES, pairs)


def coefficients(group_rel, member_rel, dims, outer_bits):
    out = []
    for group_mask, member_mask in dims:
        if member_mask:
            out.append((member_rel >> (member_mask.bit_length() - 1)) & 1)
        else:
            top = group_mask.bit_length() - 1
            bit = (group_rel >> top) & 1
            if top + 1 < outer_bits:
                bit = bit ^ ((group_rel >> (top + 1)) & 1)
            out.append(bit)
    return out


def block_position(group_rel, member_rel, dims, outer_bits):
    place = 0
    for bit in coefficients(group_rel, member_rel, dims, outer_bits):
        place = place * 2 + (1 - bit)
    return place


def relative_of(place, dims):
    group_rel = member_rel = 0
    for at, (group_mask, member_mask) in enumerate(dims):
        if not (place >> (len(dims) - 1 - at)) & 1:
            group_rel ^= group_mask
            member_rel ^= member_mask
    return group_rel, member_rel


def token_shape():
    return jax.ShapeDtypeStruct((8, 128), F32)


def hand_on(kernel, inputs):
    def run(*refs):
        kernel(*refs[:inputs], *refs[inputs + 1 : -1])
        refs[-1][...] = refs[inputs][...]

    return run


def sums_kernel(base, pos_ref, own_ref, other_ref, *rest):
    out_ref = rest[-1]
    rows = own_ref.shape[0]
    keys = out_ref.shape[0] - (rest[0].shape[0] if len(rest) > 1 else 0)
    key = lax.broadcasted_iota(jnp.int32, (keys, rows), 0) + base
    first = jnp.where(pos_ref[:, :rows] == key, 1.0, 0.0).astype(BF16)
    second = jnp.where(pos_ref[:, rows:] == key, 1.0, 0.0).astype(BF16)
    total = jnp.dot(first, own_ref[...], preferred_element_type=F32)
    total += jnp.dot(second, other_ref[...], preferred_element_type=F32)
    out_ref[:keys, :] = total.astype(BF16)
    if len(rest) > 1:
        out_ref[keys:, :] = rest[0][...]


def key_sums(token, pos_row, own, other, count_tile, base, keys):
    rows, wide = own.shape
    extra = [] if count_tile is None else [count_tile]
    out_rows = keys + sum(e.shape[0] for e in extra)
    whole = lambda shape: pl.BlockSpec(shape, lambda i: (0, 0))
    return pl.pallas_call(
        hand_on(functools.partial(sums_kernel, base), 3 + len(extra)),
        grid=(1,),
        out_shape=[jax.ShapeDtypeStruct((out_rows, wide), BF16), token_shape()],
        in_specs=[
            whole((1, 2 * rows)),
            whole((rows, wide)),
            whole((rows, wide)),
        ]
        + [whole(e.shape) for e in extra]
        + [whole(token.shape)],
        out_specs=[whole((out_rows, wide)), whole(token.shape)],
        compiler_params=pltpu.CompilerParams(vmem_limit_bytes=16 << 20),
        cost_estimate=pl.CostEstimate(
            flops=2 * keys * 2 * rows * wide, bytes_accessed=(4 * rows + 2 * keys) * wide, transcendentals=0
        ),
        name="key_sums",
    )(pos_row, own, other, *extra, token)


def small_call(kernel, name, outs, token, *args):
    whole = pl.BlockSpec(memory_space=pltpu.VMEM)
    moved = sum(a.size * a.dtype.itemsize for a in (*args, *outs))
    return pl.pallas_call(
        hand_on(kernel, len(args)),
        out_shape=[*outs, token_shape()],
        in_specs=[whole] * (len(args) + 1),
        out_specs=[whole] * (len(outs) + 1),
        compiler_params=pltpu.CompilerParams(vmem_limit_bytes=4 << 20),
        cost_estimate=pl.CostEstimate(flops=moved // 2, bytes_accessed=moved, transcendentals=0),
        name=name,
    )(*args, token)


def add_pair(got_ref, keep_ref, start, stop):
    return got_ref[start:stop, :].astype(F32) + keep_ref[start:stop, :].astype(F32)


def add_tail(got_ref, keep_ref, body, shift):
    kept = keep_ref[body:, :].astype(F32)
    return (kept + pltpu.roll(got_ref[body:, :].astype(F32), shift, 0)).astype(BF16)


def fold_kernel(half, shift, got_ref, keep_ref, send_out, keep_out):
    send_out[:half, :] = add_pair(got_ref, keep_ref, 0, half).astype(BF16)
    keep_out[:half, :] = add_pair(got_ref, keep_ref, half, 2 * half).astype(BF16)
    if got_ref.shape[0] > 2 * half:
        tail = add_tail(got_ref, keep_ref, 2 * half, shift)
        send_out[half:, :] = tail
        keep_out[half:, :] = tail


def seed_kernel(share, shift, got_ref, keep_ref, old_ref, send_out, near_out):
    two = 2 * share
    near = add_pair(got_ref, keep_ref, share, two) + PRIOR * old_ref[...]
    near_out[...] = near
    send_out[:share, :] = add_pair(got_ref, keep_ref, 0, share).astype(BF16)
    send_out[share:two, :] = near.astype(BF16)
    if got_ref.shape[0] > two:
        send_out[two:, :] = add_tail(got_ref, keep_ref, two, shift)


def summed(share, block, got_ref, sent_ref, near_ref):
    if block == 0:
        return sent_ref[:share, :].astype(F32) + got_ref[share : 2 * share, :].astype(F32)
    return near_ref[...] + got_ref[:share, :].astype(F32)


def square_sums(rounded):
    return jnp.sum(jnp.square(rounded.astype(F32)), axis=1, keepdims=True)


def first_kernel(share, base, digits, got_ref, sent_ref, near_ref, fresh_out, cents_out, scale_out, norm_out):
    two = 2 * share
    wide = got_ref.shape[1]
    last = sent_ref.shape[0] - two - 1
    lane = lax.broadcasted_iota(jnp.int32, (share, wide), 1)
    line = lax.broadcasted_iota(jnp.int32, (share, wide), 0)
    mine = sent_ref[two:, :].astype(F32)
    theirs = got_ref[two:, :].astype(F32)
    for block in range(2):
        row = mine[last - 1 + block : last + block, :] + theirs[last - block : last - block + 1, :]
        count = jnp.full((share, 1), PRIOR, F32)
        for digit in range(digits):
            hit = jnp.where(lane == line + digit * share, row, 0.0)
            count += jnp.sum(hit, axis=1, keepdims=True) * float(base**digit)
        scale_out[block * share : (block + 1) * share, :] = count
        fresh = summed(share, block, got_ref, sent_ref, near_ref) / count
        rounded = fresh.astype(BF16)
        cents_out[block * share : (block + 1) * share, :] = rounded
        norm_out[block * share : (block + 1) * share, :] = square_sums(rounded)
        if block == 1:
            fresh_out[...] = fresh


def last_kernel(share, tail, got_ref, sent_ref, near_ref, scale_ref, norm_ref, first_ref, fresh_out, cents_out):
    two = 2 * share
    wide = got_ref.shape[1]
    lane = lax.broadcasted_iota(jnp.int32, (share, wide), 1)
    line = lax.broadcasted_iota(jnp.int32, (share, wide), 0)
    tile = jnp.zeros((tail, wide), F32)
    tile_row = lax.broadcasted_iota(jnp.int32, (tail, wide), 0)
    for block in range(2):
        part = slice(block * share, (block + 1) * share)
        fresh = summed(share, block, got_ref, sent_ref, near_ref) / scale_ref[part, :]
        rounded = fresh.astype(BF16)
        cents_out[part, :] = rounded
        if block == 1:
            before = first_ref.shape[1]
            fresh_out[:, :before] = first_ref[...]
            fresh_out[:, before:] = fresh
        norm = 0.5 * (norm_ref[part, :] + square_sums(rounded))
        spread = jnp.zeros((1, wide), F32)
        for term_at in range(PARTS):
            term = norm.astype(BF16).astype(F32)
            norm = norm - term
            hit = jnp.where(lane == line + term_at * share, term, 0.0)
            spread += jnp.sum(hit, axis=0, keepdims=True)
        tile = jnp.where(tile_row == tail - 2 + block, spread, tile)
    cents_out[two:, :] = tile.astype(BF16)


def join_kernel(body, shift, got_ref, held_ref, out_ref):
    out_ref[:body, :] = got_ref[:body, :]
    out_ref[body : 2 * body, :] = held_ref[:body, :]
    if held_ref.shape[0] > body:
        rows = held_ref.shape[0] - body
        moved = pltpu.roll(got_ref[body:, :].astype(F32), rows - shift, 0)
        out_ref[2 * body :, :] = (held_ref[body:, :].astype(F32) + moved).astype(BF16)


def behind(array, token):
    def kernel(in_ref, token_ref, out_ref):
        del in_ref, token_ref, out_ref

    return pl.pallas_call(
        kernel,
        out_shape=jax.ShapeDtypeStruct(array.shape, array.dtype),
        in_specs=[pl.BlockSpec(memory_space=pl.ANY)] * 2,
        out_specs=pl.BlockSpec(memory_space=pl.ANY),
        input_output_aliases={0: 0},
        compiler_params=pltpu.CompilerParams(vmem_limit_bytes=1 << 20),
        cost_estimate=pl.CostEstimate(flops=1, bytes_accessed=1, transcendentals=0),
        name="behind",
    )(array, token)


def row_loads(x_ref, gid_ref, x, gid, sem, start):
    return (
        pltpu.make_async_copy(x_ref.at[:, pl.ds(start, x.shape[1])], x, sem.at[0]),
        pltpu.make_async_copy(gid_ref, gid, sem.at[1]),
    )


def mask_rows(groups, x, gid_ref, out):
    wide = x.shape[1]
    gid = jnp.transpose(jnp.broadcast_to(gid_ref[...], (128, gid_ref.shape[1])))
    for group in range(groups):
        keep = gid == group
        for cut in range(0, wide, 128):
            part = x[:, cut : cut + 128]
            out[:, group * wide + cut : group * wide + cut + 128] = jnp.where(keep, part, jnp.zeros_like(part))
    return gid


def row_scratch(rows, groups, wide):
    return [
        pltpu.VMEM((rows, groups * wide), BF16),
        pltpu.VMEM((rows, wide), BF16),
        pltpu.VMEM((1, rows), jnp.int32),
        pltpu.SemaphoreType.DMA((2,)),
    ]


def product(a, b):
    return lax.dot_general(a, b, (((1,), (1,)), ((), ())), preferred_element_type=F32)


def part_kernel(groups, share, start_at, code_ref, x_ref, gid_ref, own_ref, other_ref, *rest):
    out_ref, cents, rows_of, x, gid_row, sem = rest
    loads = row_loads(x_ref, gid_ref, x, gid_row, sem, start_at)
    wide = own_ref.shape[1]
    blocks = own_ref.shape[0] // share

    @pl.when(pl.program_id(0) == 0)
    def _():
        for load in loads:
            load.start()
        for piece, ref in enumerate((own_ref, other_ref)):
            for block in range(blocks):
                code = code_ref[piece * blocks + block]
                slot = pl.multiple_of(code // groups * share, share)
                cents[pl.ds(slot, share), pl.ds(pl.multiple_of(code % groups * wide, 128), wide)] = ref[block * share : (block + 1) * share, :]
        for load in loads:
            load.wait()
        mask_rows(groups, x, gid_row, rows_of)

    step = out_ref.shape[1]
    start = pl.multiple_of(pl.program_id(0) * step, step)
    out_ref[...] = product(rows_of[...], cents[pl.ds(start, step), :]).astype(BF16)


def part_scores(token, samples, gid, codes, pieces, before, groups, keys, share, start_at):
    rows = samples.shape[0]
    wide = pieces[0].shape[1]
    half = pieces[0].shape[0] * len(pieces) // groups
    step = min(256, half)
    steps = half // step
    at = 0 if before is None else steps
    whole = pl.BlockSpec(memory_space=pltpu.VMEM)
    extra = [] if before is None else [before]
    anywhere = pl.BlockSpec(memory_space=pl.ANY)

    def kernel(code_ref, *refs):
        count = 4 + len(extra)
        part_kernel(groups, share, start_at, code_ref, *refs[:4], refs[count + 1], *refs[-5:])
        refs[count + 2][...] = refs[count][...]

    return pl.pallas_call(
        kernel,
        grid_spec=pltpu.PrefetchScalarGridSpec(
            num_scalar_prefetch=1,
            grid=(steps,),
            in_specs=[anywhere] * 2 + [whole] * 2 + [anywhere] * len(extra) + [whole],
            out_specs=[pl.BlockSpec((rows, step), lambda i, w: (0, i + at)), whole],
            scratch_shapes=[
                pltpu.VMEM((half, groups * wide), BF16),
                *row_scratch(rows, groups, wide),
            ],
        ),
        out_shape=[jax.ShapeDtypeStruct((rows, keys), BF16), token_shape()],
        input_output_aliases={} if before is None else {5: 0},
        compiler_params=pltpu.CompilerParams(vmem_limit_bytes=51 << 20),
        cost_estimate=pl.CostEstimate(flops=1, bytes_accessed=1, transcendentals=0),
        name="part_scores",
    )(codes, samples, gid, *pieces, *extra, token)


def final_kernel(groups, share, start_at, code_ref, slot_ref, x_ref, gid_ref, half_ref, *rest):
    pieces = 4
    piece_refs, total_refs = rest[:pieces], rest[pieces : pieces + 2]
    out_ref, cents, half, pick, rows_of, x, gid_row, sem = rest[-8:]
    loads = row_loads(x_ref, gid_ref, x, gid_row, sem, start_at)
    keys = cents.shape[0]
    wide = cents.shape[1] // groups
    members = keys // share
    blocks = code_ref.shape[0] // pieces
    lanes = 128

    @pl.when(pl.program_id(0) == 0)
    def _():
        for load in loads:
            load.start()
        half[...] = half_ref[...]
        for piece, ref in enumerate(piece_refs):
            for block in range(blocks):
                code = code_ref[piece * blocks + block]
                group = code // members
                row_at = pl.multiple_of((code % members) * share, share)
                cents[pl.ds(row_at, share), pl.ds(pl.multiple_of(group * wide, lanes), wide)] = ref[
                    block * share : (block + 1) * share, :
                ]
                if share >= lanes:
                    tail = ref[blocks * share :, :].astype(F32)
                    at = tail.shape[0] - blocks + block
                    lines = pl.ds(pl.multiple_of(row_at, lanes), share)
                    line = lax.broadcasted_iota(jnp.int32, (half.shape[0], share), 0)
                    filled = half[:, lines]
                    for term in range(PARTS):
                        row = tail[at : at + 1, term * share : (term + 1) * share]
                        filled = jnp.where(line == group + term * groups, row, filled)
                    half[:, lines] = filled
        for load in loads:
            load.wait()
        gid = mask_rows(groups, x, gid_row, rows_of)[:, : pick.shape[1]]
        lane = lax.broadcasted_iota(jnp.int32, pick.shape, 1)
        hit = (lane % groups == gid) & (lane < PARTS * groups)
        pick[...] = jnp.where(hit, -1.0, 0.0).astype(BF16)

    step = out_ref.shape[1]
    start = pl.multiple_of(pl.program_id(0) * step, step)
    dots = product(rows_of[...], cents[pl.ds(start, step), :])
    offsets = half[:, pl.ds(start, step)].astype(BF16)
    dots += jnp.dot(pick[...], offsets, preferred_element_type=F32)
    cut = step // 2
    out_ref[:, :cut] = (dots[:, :cut] + total_refs[0][...].astype(F32)).astype(BF16)
    out_ref[:, cut:] = (dots[:, cut:] + total_refs[1][...].astype(F32)).astype(BF16)


def final_scores(samples, gid, codes, slots, pieces, total, half, groups, keys, share, start_at):
    rows = samples.shape[0]
    wide = pieces[0].shape[1]
    step = min(256, keys)
    cut = step // 2
    whole = pl.BlockSpec(memory_space=pltpu.VMEM)
    return pl.pallas_call(
        functools.partial(final_kernel, groups, share, start_at),
        grid_spec=pltpu.PrefetchScalarGridSpec(
            num_scalar_prefetch=2,
            grid=(keys // step,),
            in_specs=[pl.BlockSpec(memory_space=pl.ANY)] * 2
            + [whole] * (1 + len(pieces))
            + [
                pl.BlockSpec((rows, cut), lambda i, c, s: (0, s[2 * i])),
                pl.BlockSpec((rows, cut), lambda i, c, s: (0, s[2 * i + 1])),
            ],
            out_specs=pl.BlockSpec((rows, step), lambda i, c, s: (0, i)),
            scratch_shapes=[
                pltpu.VMEM((keys, groups * wide), BF16),
                pltpu.VMEM(half.shape, F32),
                pltpu.VMEM((rows, TILE), BF16),
                *row_scratch(rows, groups, wide),
            ],
        ),
        out_shape=jax.ShapeDtypeStruct((rows, keys), BF16),
        compiler_params=pltpu.CompilerParams(vmem_limit_bytes=50 << 20),
        cost_estimate=pl.CostEstimate(flops=1, bytes_accessed=1, transcendentals=0),
        name="final_scores",
    )(codes, slots, samples, gid, half, *pieces, total, total)


def per_device(samples, coarse_label, fine_label, live_rows, old_centroids):
    groups = lax.axis_size("coarse")
    members = lax.axis_size("member")
    z = lax.axis_index("coarse")
    me = lax.axis_index("member")
    core = me & 1
    rows, width = samples.shape
    keys = old_centroids.shape[1]
    share = keys // members
    columns = streams_of(width)
    streams = range(len(columns))
    half_keys = groups * keys // 2
    blocks = half_keys // share
    outer_bits = groups.bit_length() - 1
    turned = orders_of(groups, members)
    stages = len(turned[0, 0])
    base = 256 // (groups * members // 2) + 1
    digits = 1
    while base**digits <= 2 * rows:
        digits += 1

    live = jnp.arange(rows, dtype=jnp.int32) < live_rows[0]
    label = jnp.where(live, coarse_label[:, 0] * keys + fine_label, -1)
    sibling = lambda a: exchange(a, lambda gz, m: (gz, m ^ 1), groups, members)
    cut_rows = [samples[:, start : start + wide] for start, wide in streams_of(width)]
    other_rows = [sibling(part) for part in cut_rows]
    label_all = jnp.concatenate([label, sibling(label)])

    group_of = label_all // keys
    fine = label_all % keys
    owner = fine // share
    mine = (label_all >= 0) & ((owner & 1) == core)

    def of_core(make):
        return jnp.where(core == 0, make(0), make(1))

    def pairing(stage, stream):
        def partner(gz, m):
            group_mask, member_mask = turned[m & 1, stream][stage]
            return gz ^ group_mask, m ^ member_mask

        return partner

    tail = pad_rows(blocks)
    token = start_token = jnp.zeros((8, 128), F32)
    rows_of, tiles = [], []
    for stream, (start, wide) in enumerate(columns):
        place = of_core(
            lambda c: block_position(group_of ^ z, owner ^ me, turned[c, stream], outer_bits)
        )
        rows_of.append(jnp.where(mine, place * share + fine % share, -1)[None, :])
        tile = None
        if stream == 0:
            in_block = (jnp.where(mine, place, -1)[:, None] == jnp.arange(tail)[None, :]).astype(BF16)
            in_lane = ((fine % share)[:, None] == jnp.arange(share)[None, :]).astype(BF16)
            counted = lax.dot_general(
                in_block, in_lane, (((0,), (0,)), ((), ())), preferred_element_type=F32
            ).astype(jnp.int32)
            tile = [(counted // base**digit) % base for digit in range(digits)]
            tile = jnp.concatenate(tile, axis=1).astype(BF16)
            tile = jnp.pad(tile, ((0, 0), (0, wide - digits * share)))
        tiles.append(tile)

    half_keys //= 2
    send, keep = [None] * 2, [None] * 2
    for part, found in enumerate((send, keep)):
        for stream, (start, wide) in enumerate(columns):
            found[stream], token = key_sums(
                token, rows_of[stream], cut_rows[stream], other_rows[stream], tiles[stream], part * half_keys, half_keys
            )

    tokens = [start_token] * 2
    own_turn = (2, 3, 4)

    def step_token(step, stream):
        return tokens[stream if stream == 0 and step in own_turn else 1 - stream]

    old_share = lax.dynamic_slice(old_centroids[0], (me * share, 0), (share, width))

    def bf(count, stream, tailed):
        rows_out = count * share + (tail if stream == tailed else 0)
        return jax.ShapeDtypeStruct((rows_out, columns[stream][1]), BF16)

    share_f32 = [jax.ShapeDtypeStruct((share, wide), F32) for _, wide in columns]
    held, fresh, near = [None] * 2, [None] * 2, [None] * 2
    count = blocks // 2
    for stage in range(stages - 1):
        for stream, (start, wide) in enumerate(columns):
            got = exchange(send[stream], pairing(stage, stream), groups, members)
            if stage < stages - 2:
                send[stream], keep[stream], tokens[stream] = small_call(
                    functools.partial(fold_kernel, count // 2 * share, count),
                    "fold",
                    [bf(count // 2, stream, 0)] * 2,
                    step_token(stage, stream),
                    got,
                    keep[stream],
                )
            else:
                send[stream], near[stream], tokens[stream] = small_call(
                    functools.partial(seed_kernel, share, count),
                    "seed",
                    [bf(2, stream, 0), share_f32[stream]],
                    step_token(stage, stream),
                    got,
                    keep[stream],
                    old_share[:, start : start + wide],
                )
        count //= 2
    column = jax.ShapeDtypeStruct((2 * share, 1), F32)
    for stream in streams:
        got = exchange(send[stream], pairing(stages - 1, stream), groups, members)
        if stream == 0:
            fresh[0], held[0], scale, norm, tokens[stream] = small_call(
                functools.partial(first_kernel, share, base, digits),
                "first_centroids",
                [share_f32[0], bf(2, 0, 1), column, column],
                step_token(stages - 1, stream),
                got,
                send[0],
                near[0],
            )
        else:
            fresh[1], held[1], tokens[stream] = small_call(
                functools.partial(last_kernel, share, tail),
                "last_centroids",
                [jax.ShapeDtypeStruct((share, width), F32), bf(2, 1, 1)],
                step_token(stages - 1, stream),
                got,
                send[1],
                near[1],
                scale,
                norm,
                fresh[0],
            )
    half_blocks = blocks // 2
    quarter = half_blocks // groups
    inner_of = [[dim for dim in turned[c, 0] if dim[1]] for c in range(2)]

    def part_codes(part):
        codes = []
        for flip in range(2):
            for block in range(half_blocks):
                code = []
                for c in range(2):
                    group_rel, member_rel = relative_of(part * half_blocks + block, turned[c, 0])
                    spot = block_position(0, member_rel, inner_of[c], outer_bits) % quarter
                    code.append((spot + flip * quarter) * groups + (z ^ group_rel))
                codes.append(jnp.where(core ^ flip == 0, *code))
        return jnp.stack(codes).astype(jnp.int32)

    gid = jnp.where(live, coarse_label[:, 0], -1)[None, :]
    count = 2
    arrived = [None] * 2
    for stage in reversed(range(stages - 1)):
        for stream in streams:
            got = exchange(held[stream], pairing(stage, stream), groups, members)
            if stage:
                held[stream], tokens[stream] = small_call(
                    functools.partial(join_kernel, count * share, count),
                    "join",
                    [bf(2 * count, stream, 1)],
                    step_token(2 * stages - 2 - stage, stream),
                    got,
                    held[stream],
                )
            else:
                arrived[stream] = got
            if (stage, stream) == (1, 0):
                total, tokens[0] = part_scores(
                    tokens[0], samples, gid, part_codes(1), [held[0], sibling(held[0])], None, groups, keys, share, 0
                )
        count *= 2

    def codes_of(stream, part, flip):
        codes = []
        for block in range(half_blocks):
            rel = [relative_of(part * half_blocks + block, turned[c, stream]) for c in range(2)]
            holder = core ^ flip
            group_rel = jnp.where(holder == 0, rel[0][0], rel[1][0])
            member_rel = jnp.where(holder == 0, rel[0][1], rel[1][1])
            codes.append((z ^ group_rel) * members + (me ^ flip ^ member_rel))
        return jnp.stack(codes).astype(jnp.int32)

    total, token = part_scores(
        tokens[1], samples, gid, part_codes(0), [arrived[0], sibling(arrived[0])], total, groups, keys, share, 0
    )
    last = behind(arrived[1], token)
    every = jnp.arange(members, dtype=jnp.int32)
    flip_of = (every ^ me) & 1
    spot = jnp.where(
        (core ^ flip_of) == 0,
        *(block_position(0, every ^ me, inner_of[c], outer_bits) for c in range(2)),
    )
    slots = jnp.where(spot >= quarter, spot - quarter, spot + 2 * quarter) + flip_of * quarter
    flat = [piece for got in (last, held[1]) for piece in (got, sibling(got))]
    codes = jnp.concatenate([codes_of(1, part, flip) for part in range(2) for flip in range(2)])
    half = jnp.zeros((TILE, keys), F32)
    if share < 128:
        norm_rows = []
        for piece in flat:
            norm_rows.append(piece[half_blocks * share + tail - half_blocks :].astype(F32))
        norm_rows = jnp.concatenate(norm_rows)
        spread = (codes[None, :] == jnp.arange(groups * members, dtype=jnp.int32)[:, None]).astype(F32)
        for term in range(PARTS):
            found = jnp.dot(
                spread, norm_rows[:, term * share : (term + 1) * share], precision=lax.Precision.HIGHEST
            )
            half = half.at[term * groups : (term + 1) * groups].set(found.reshape(groups, keys))
        lane = jnp.arange(keys, dtype=jnp.int32)
        source = jnp.repeat(slots, share) * share + lane % share
        move = (lane[:, None] == source[None, :]).astype(F32)
        total = jnp.dot(total, move.astype(BF16))
        slots = jnp.arange(keys // 128, dtype=jnp.int32)
    scores = final_scores(samples, gid, codes, slots, flat, total, half, groups, keys, share, columns[1][0])
    return scores, fresh[1][None]


def solution(mesh):
    return jax.shard_map(
        per_device,
        mesh=mesh,
        in_specs=(
            P(AXES, None),
            P(AXES, None),
            P(AXES),
            P(AXES),
            P("coarse", None, None),
        ),
        out_specs=(P(AXES, None), P("coarse", "member", None)),
        check_vma=False,
    )
```

```python
import functools

import jax
import jax.numpy as jnp
from jax import lax
from jax.experimental import pallas as pl
from jax.experimental.pallas import tpu as pltpu
from jax.sharding import PartitionSpec as P

AXES = ("coarse", "member")
TILE = 16
PRIOR = 16.0
PARTS = 2
F32 = jnp.float32
BF16 = jnp.bfloat16


def pad_rows(blocks):
    return max(TILE, -(-blocks // TILE) * TILE)


def streams_of(width):
    wide = width // 2
    return ((0, wide), (wide, wide))


def orders_of(groups, members):
    inner = [(0, 1 << bit) for bit in range(1, members.bit_length() - 1)]
    outer = [((1 << (bit + 1)) - 1, 0) for bit in range(groups.bit_length() - 1)]
    cut = len(inner) // 2
    other = inner[cut:] + inner[:cut]
    found = {}
    found[0, 0] = inner[:cut] + outer[:1] + inner[cut:] + outer[1:]
    found[1, 0] = other[:cut] + outer[:1] + other[cut:] + outer[1:]
    found[0, 1] = found[1, 0]
    found[1, 1] = found[0, 0]
    return found


def exchange(array, partner, groups, members):
    pairs = []
    for z in range(groups):
        for m in range(members):
            to_z, to_m = partner(z, m)
            pairs.append((z * members + m, to_z * members + to_m))
    return lax.ppermute(array, AXES, pairs)


def coefficients(group_rel, member_rel, dims, outer_bits):
    out = []
    for group_mask, member_mask in dims:
        if member_mask:
            out.append((member_rel >> (member_mask.bit_length() - 1)) & 1)
        else:
            top = group_mask.bit_length() - 1
            bit = (group_rel >> top) & 1
            if top + 1 < outer_bits:
                bit = bit ^ ((group_rel >> (top + 1)) & 1)
            out.append(bit)
    return out


def block_position(group_rel, member_rel, dims, outer_bits):
    place = 0
    for bit in coefficients(group_rel, member_rel, dims, outer_bits):
        place = place * 2 + (1 - bit)
    return place


def relative_of(place, dims):
    group_rel = member_rel = 0
    for at, (group_mask, member_mask) in enumerate(dims):
        if not (place >> (len(dims) - 1 - at)) & 1:
            group_rel ^= group_mask
            member_rel ^= member_mask
    return group_rel, member_rel


def token_shape():
    return jax.ShapeDtypeStruct((8, 128), F32)


def hand_on(kernel, inputs):
    def run(*refs):
        kernel(*refs[:inputs], *refs[inputs + 1 : -1])
        refs[-1][...] = refs[inputs][...]

    return run


def sums_kernel(base, pos_ref, own_ref, other_ref, *rest):
    out_ref = rest[-1]
    rows = own_ref.shape[0]
    keys = out_ref.shape[0] - (rest[0].shape[0] if len(rest) > 1 else 0)
    key = lax.broadcasted_iota(jnp.int32, (keys, rows), 0) + base
    first = jnp.where(pos_ref[:, :rows] == key, 1.0, 0.0).astype(BF16)
    second = jnp.where(pos_ref[:, rows:] == key, 1.0, 0.0).astype(BF16)
    total = jnp.dot(first, own_ref[...], preferred_element_type=F32)
    total += jnp.dot(second, other_ref[...], preferred_element_type=F32)
    out_ref[:keys, :] = total.astype(BF16)
    if len(rest) > 1:
        out_ref[keys:, :] = rest[0][...]


def key_sums(token, pos_row, own, other, count_tile, base, keys, start, wide):
    rows = own.shape[0]
    extra = [] if count_tile is None else [count_tile]
    out_rows = keys + sum(e.shape[0] for e in extra)
    whole = lambda shape: pl.BlockSpec(shape, lambda i: (0, 0))
    return pl.pallas_call(
        hand_on(functools.partial(sums_kernel, base), 3 + len(extra)),
        grid=(1,),
        out_shape=[jax.ShapeDtypeStruct((out_rows, wide), BF16), token_shape()],
        in_specs=[
            whole((1, 2 * rows)),
            pl.BlockSpec((rows, wide), lambda i: (0, start // wide)),
            pl.BlockSpec((rows, wide), lambda i: (0, start // wide)),
        ]
        + [whole(e.shape) for e in extra]
        + [whole(token.shape)],
        out_specs=[whole((out_rows, wide)), whole(token.shape)],
        compiler_params=pltpu.CompilerParams(vmem_limit_bytes=16 << 20),
        cost_estimate=pl.CostEstimate(
            flops=2 * keys * 2 * rows * wide, bytes_accessed=(4 * rows + 2 * keys) * wide, transcendentals=0
        ),
        name="key_sums",
    )(pos_row, own, other, *extra, token)


def small_call(kernel, name, outs, token, *args):
    whole = pl.BlockSpec(memory_space=pltpu.VMEM)
    moved = sum(a.size * a.dtype.itemsize for a in (*args, *outs))
    return pl.pallas_call(
        hand_on(kernel, len(args)),
        out_shape=[*outs, token_shape()],
        in_specs=[whole] * (len(args) + 1),
        out_specs=[whole] * (len(outs) + 1),
        compiler_params=pltpu.CompilerParams(vmem_limit_bytes=4 << 20),
        cost_estimate=pl.CostEstimate(flops=moved // 2, bytes_accessed=moved, transcendentals=0),
        name=name,
    )(*args, token)


def add_pair(got_ref, keep_ref, start, stop):
    return got_ref[start:stop, :].astype(F32) + keep_ref[start:stop, :].astype(F32)


def add_tail(got_ref, keep_ref, body, shift):
    kept = keep_ref[body:, :].astype(F32)
    return (kept + pltpu.roll(got_ref[body:, :].astype(F32), shift, 0)).astype(BF16)


def fold_kernel(half, shift, got_ref, keep_ref, send_out, keep_out):
    send_out[:half, :] = add_pair(got_ref, keep_ref, 0, half).astype(BF16)
    keep_out[:half, :] = add_pair(got_ref, keep_ref, half, 2 * half).astype(BF16)
    if got_ref.shape[0] > 2 * half:
        tail = add_tail(got_ref, keep_ref, 2 * half, shift)
        send_out[half:, :] = tail
        keep_out[half:, :] = tail


def seed_kernel(share, shift, got_ref, keep_ref, old_ref, send_out, near_out):
    two = 2 * share
    near = add_pair(got_ref, keep_ref, share, two) + PRIOR * old_ref[...]
    near_out[...] = near
    send_out[:share, :] = add_pair(got_ref, keep_ref, 0, share).astype(BF16)
    send_out[share:two, :] = near.astype(BF16)
    if got_ref.shape[0] > two:
        send_out[two:, :] = add_tail(got_ref, keep_ref, two, shift)


def summed(share, block, got_ref, sent_ref, near_ref):
    if block == 0:
        return sent_ref[:share, :].astype(F32) + got_ref[share : 2 * share, :].astype(F32)
    return near_ref[...] + got_ref[:share, :].astype(F32)


def square_sums(rounded):
    return jnp.sum(jnp.square(rounded.astype(F32)), axis=1, keepdims=True)


def first_kernel(share, base, digits, got_ref, sent_ref, near_ref, fresh_out, cents_out, scale_out, norm_out):
    two = 2 * share
    wide = got_ref.shape[1]
    last = sent_ref.shape[0] - two - 1
    lane = lax.broadcasted_iota(jnp.int32, (share, wide), 1)
    line = lax.broadcasted_iota(jnp.int32, (share, wide), 0)
    mine = sent_ref[two:, :].astype(F32)
    theirs = got_ref[two:, :].astype(F32)
    for block in range(2):
        row = mine[last - 1 + block : last + block, :] + theirs[last - block : last - block + 1, :]
        count = jnp.full((share, 1), PRIOR, F32)
        for digit in range(digits):
            hit = jnp.where(lane == line + digit * share, row, 0.0)
            count += jnp.sum(hit, axis=1, keepdims=True) * float(base**digit)
        scale_out[block * share : (block + 1) * share, :] = count
        fresh = summed(share, block, got_ref, sent_ref, near_ref) / count
        rounded = fresh.astype(BF16)
        cents_out[block * share : (block + 1) * share, :] = rounded
        norm_out[block * share : (block + 1) * share, :] = square_sums(rounded)
        if block == 1:
            fresh_out[...] = fresh


def last_kernel(share, tail, got_ref, sent_ref, near_ref, scale_ref, norm_ref, first_ref, fresh_out, cents_out):
    two = 2 * share
    wide = got_ref.shape[1]
    lane = lax.broadcasted_iota(jnp.int32, (share, wide), 1)
    line = lax.broadcasted_iota(jnp.int32, (share, wide), 0)
    tile = jnp.zeros((tail, wide), F32)
    tile_row = lax.broadcasted_iota(jnp.int32, (tail, wide), 0)
    for block in range(2):
        part = slice(block * share, (block + 1) * share)
        fresh = summed(share, block, got_ref, sent_ref, near_ref) / scale_ref[part, :]
        rounded = fresh.astype(BF16)
        cents_out[part, :] = rounded
        if block == 1:
            before = first_ref.shape[1]
            fresh_out[:, :before] = first_ref[...]
            fresh_out[:, before:] = fresh
        norm = 0.5 * (norm_ref[part, :] + square_sums(rounded))
        spread = jnp.zeros((1, wide), F32)
        for term_at in range(PARTS):
            term = norm.astype(BF16).astype(F32)
            norm = norm - term
            hit = jnp.where(lane == line + term_at * share, term, 0.0)
            spread += jnp.sum(hit, axis=0, keepdims=True)
        tile = jnp.where(tile_row == tail - 2 + block, spread, tile)
    cents_out[two:, :] = tile.astype(BF16)


def join_kernel(body, shift, got_ref, held_ref, out_ref):
    out_ref[:body, :] = got_ref[:body, :]
    out_ref[body : 2 * body, :] = held_ref[:body, :]
    if held_ref.shape[0] > body:
        rows = held_ref.shape[0] - body
        moved = pltpu.roll(got_ref[body:, :].astype(F32), rows - shift, 0)
        out_ref[2 * body :, :] = (held_ref[body:, :].astype(F32) + moved).astype(BF16)


def behind(array, token):
    def kernel(in_ref, token_ref, out_ref):
        del in_ref, token_ref, out_ref

    return pl.pallas_call(
        kernel,
        out_shape=jax.ShapeDtypeStruct(array.shape, array.dtype),
        in_specs=[pl.BlockSpec(memory_space=pl.ANY)] * 2,
        out_specs=pl.BlockSpec(memory_space=pl.ANY),
        input_output_aliases={0: 0},
        compiler_params=pltpu.CompilerParams(vmem_limit_bytes=1 << 20),
        cost_estimate=pl.CostEstimate(flops=1, bytes_accessed=1, transcendentals=0),
        name="behind",
    )(array, token)


def row_loads(x_ref, gid_ref, x, gid, sem, start):
    return (
        pltpu.make_async_copy(x_ref.at[:, pl.ds(start, x.shape[1])], x, sem.at[0]),
        pltpu.make_async_copy(gid_ref, gid, sem.at[1]),
    )


def mask_rows(groups, x, gid_ref, out):
    wide = x.shape[1]
    gid = jnp.transpose(jnp.broadcast_to(gid_ref[...], (128, gid_ref.shape[1])))
    for group in range(groups):
        keep = gid == group
        for cut in range(0, wide, 128):
            part = x[:, cut : cut + 128]
            out[:, group * wide + cut : group * wide + cut + 128] = jnp.where(keep, part, jnp.zeros_like(part))
    return gid


def row_scratch(rows, groups, wide):
    return [
        pltpu.VMEM((rows, groups * wide), BF16),
        pltpu.VMEM((rows, wide), BF16),
        pltpu.VMEM((1, rows), jnp.int32),
        pltpu.SemaphoreType.DMA((2,)),
    ]


def product(a, b):
    return lax.dot_general(a, b, (((1,), (1,)), ((), ())), preferred_element_type=F32)


def part_kernel(groups, share, start_at, code_ref, x_ref, gid_ref, own_ref, other_ref, *rest):
    out_ref, cents, rows_of, x, gid_row, sem = rest
    loads = row_loads(x_ref, gid_ref, x, gid_row, sem, start_at)
    wide = own_ref.shape[1]
    blocks = own_ref.shape[0] // share

    @pl.when(pl.program_id(0) == 0)
    def _():
        for load in loads:
            load.start()
        for piece, ref in enumerate((own_ref, other_ref)):
            for block in range(blocks):
                code = code_ref[piece * blocks + block]
                slot = pl.multiple_of(code // groups * share, share)
                cents[pl.ds(slot, share), pl.ds(pl.multiple_of(code % groups * wide, 128), wide)] = ref[block * share : (block + 1) * share, :]
        for load in loads:
            load.wait()
        mask_rows(groups, x, gid_row, rows_of)

    step = out_ref.shape[1]
    start = pl.multiple_of(pl.program_id(0) * step, step)
    out_ref[...] = product(rows_of[...], cents[pl.ds(start, step), :]).astype(BF16)


def part_scores(token, samples, gid, codes, pieces, before, groups, keys, share, start_at):
    rows = samples.shape[0]
    wide = pieces[0].shape[1]
    half = pieces[0].shape[0] * len(pieces) // groups
    step = min(256, half)
    steps = half // step
    at = 0 if before is None else steps
    whole = pl.BlockSpec(memory_space=pltpu.VMEM)
    extra = [] if before is None else [before]
    anywhere = pl.BlockSpec(memory_space=pl.ANY)

    def kernel(code_ref, *refs):
        count = 4 + len(extra)
        part_kernel(groups, share, start_at, code_ref, *refs[:4], refs[count + 1], *refs[-5:])
        refs[count + 2][...] = refs[count][...]

    return pl.pallas_call(
        kernel,
        grid_spec=pltpu.PrefetchScalarGridSpec(
            num_scalar_prefetch=1,
            grid=(steps,),
            in_specs=[anywhere] * 2 + [whole] * 2 + [anywhere] * len(extra) + [whole],
            out_specs=[pl.BlockSpec((rows, step), lambda i, w: (0, i + at)), whole],
            scratch_shapes=[
                pltpu.VMEM((half, groups * wide), BF16),
                *row_scratch(rows, groups, wide),
            ],
        ),
        out_shape=[jax.ShapeDtypeStruct((rows, keys), BF16), token_shape()],
        input_output_aliases={} if before is None else {5: 0},
        compiler_params=pltpu.CompilerParams(vmem_limit_bytes=51 << 20),
        cost_estimate=pl.CostEstimate(flops=1, bytes_accessed=1, transcendentals=0),
        name="part_scores",
    )(codes, samples, gid, *pieces, *extra, token)


def final_kernel(groups, share, start_at, code_ref, slot_ref, x_ref, gid_ref, half_ref, *rest):
    pieces = 4
    piece_refs, total_refs = rest[:pieces], rest[pieces : pieces + 2]
    out_ref, cents, half, pick, rows_of, x, gid_row, sem = rest[-8:]
    loads = row_loads(x_ref, gid_ref, x, gid_row, sem, start_at)
    keys = cents.shape[0]
    wide = cents.shape[1] // groups
    members = keys // share
    blocks = code_ref.shape[0] // pieces
    lanes = 128

    @pl.when(pl.program_id(0) == 0)
    def _():
        for load in loads:
            load.start()
        half[...] = half_ref[...]
        for piece, ref in enumerate(piece_refs):
            for block in range(blocks):
                code = code_ref[piece * blocks + block]
                group = code // members
                row_at = pl.multiple_of((code % members) * share, share)
                cents[pl.ds(row_at, share), pl.ds(pl.multiple_of(group * wide, lanes), wide)] = ref[
                    block * share : (block + 1) * share, :
                ]
                if share >= lanes:
                    tail = ref[blocks * share :, :].astype(F32)
                    at = tail.shape[0] - blocks + block
                    lines = pl.ds(pl.multiple_of(row_at, lanes), share)
                    line = lax.broadcasted_iota(jnp.int32, (half.shape[0], share), 0)
                    filled = half[:, lines]
                    for term in range(PARTS):
                        row = tail[at : at + 1, term * share : (term + 1) * share]
                        filled = jnp.where(line == group + term * groups, row, filled)
                    half[:, lines] = filled
        for load in loads:
            load.wait()
        gid = mask_rows(groups, x, gid_row, rows_of)[:, : pick.shape[1]]
        lane = lax.broadcasted_iota(jnp.int32, pick.shape, 1)
        hit = (lane % groups == gid) & (lane < PARTS * groups)
        pick[...] = jnp.where(hit, -1.0, 0.0).astype(BF16)

    step = out_ref.shape[1]
    start = pl.multiple_of(pl.program_id(0) * step, step)
    dots = product(rows_of[...], cents[pl.ds(start, step), :])
    offsets = half[:, pl.ds(start, step)].astype(BF16)
    dots += jnp.dot(pick[...], offsets, preferred_element_type=F32)
    cut = step // 2
    out_ref[:, :cut] = (dots[:, :cut] + total_refs[0][...].astype(F32)).astype(BF16)
    out_ref[:, cut:] = (dots[:, cut:] + total_refs[1][...].astype(F32)).astype(BF16)


def final_scores(samples, gid, codes, slots, pieces, total, half, groups, keys, share, start_at):
    rows = samples.shape[0]
    wide = pieces[0].shape[1]
    step = min(256, keys)
    cut = step // 2
    whole = pl.BlockSpec(memory_space=pltpu.VMEM)
    return pl.pallas_call(
        functools.partial(final_kernel, groups, share, start_at),
        grid_spec=pltpu.PrefetchScalarGridSpec(
            num_scalar_prefetch=2,
            grid=(keys // step,),
            in_specs=[pl.BlockSpec(memory_space=pl.ANY)] * 2
            + [whole] * (1 + len(pieces))
            + [
                pl.BlockSpec((rows, cut), lambda i, c, s: (0, s[2 * i])),
                pl.BlockSpec((rows, cut), lambda i, c, s: (0, s[2 * i + 1])),
            ],
            out_specs=pl.BlockSpec((rows, step), lambda i, c, s: (0, i)),
            scratch_shapes=[
                pltpu.VMEM((keys, groups * wide), BF16),
                pltpu.VMEM(half.shape, F32),
                pltpu.VMEM((rows, TILE), BF16),
                *row_scratch(rows, groups, wide),
            ],
        ),
        out_shape=jax.ShapeDtypeStruct((rows, keys), BF16),
        compiler_params=pltpu.CompilerParams(vmem_limit_bytes=50 << 20),
        cost_estimate=pl.CostEstimate(flops=1, bytes_accessed=1, transcendentals=0),
        name="final_scores",
    )(codes, slots, samples, gid, half, *pieces, total, total)


def per_device(samples, coarse_label, fine_label, live_rows, old_centroids):
    groups = lax.axis_size("coarse")
    members = lax.axis_size("member")
    z = lax.axis_index("coarse")
    me = lax.axis_index("member")
    core = me & 1
    rows, width = samples.shape
    keys = old_centroids.shape[1]
    share = keys // members
    columns = streams_of(width)
    streams = range(len(columns))
    half_keys = groups * keys // 2
    blocks = half_keys // share
    outer_bits = groups.bit_length() - 1
    turned = orders_of(groups, members)
    stages = len(turned[0, 0])
    base = 256 // (groups * members // 2) + 1
    digits = 1
    while base**digits <= 2 * rows:
        digits += 1

    live = jnp.arange(rows, dtype=jnp.int32) < live_rows[0]
    label = jnp.where(live, coarse_label[:, 0] * keys + fine_label, -1)
    sibling = lambda a: exchange(a, lambda gz, m: (gz, m ^ 1), groups, members)
    other_samples = sibling(samples)
    label_all = jnp.concatenate([label, sibling(label)])

    group_of = label_all // keys
    fine = label_all % keys
    owner = fine // share
    mine = (label_all >= 0) & ((owner & 1) == core)

    def of_core(make):
        return jnp.where(core == 0, make(0), make(1))

    def pairing(stage, stream):
        def partner(gz, m):
            group_mask, member_mask = turned[m & 1, stream][stage]
            return gz ^ group_mask, m ^ member_mask

        return partner

    tail = pad_rows(blocks)
    token = start_token = jnp.zeros((8, 128), F32)
    rows_of, tiles = [], []
    for stream, (start, wide) in enumerate(columns):
        place = of_core(
            lambda c: block_position(group_of ^ z, owner ^ me, turned[c, stream], outer_bits)
        )
        rows_of.append(jnp.where(mine, place * share + fine % share, -1)[None, :])
        tile = None
        if stream == 0:
            in_block = (jnp.where(mine, place, -1)[:, None] == jnp.arange(tail)[None, :]).astype(BF16)
            in_lane = ((fine % share)[:, None] == jnp.arange(share)[None, :]).astype(BF16)
            counted = lax.dot_general(
                in_block, in_lane, (((0,), (0,)), ((), ())), preferred_element_type=F32
            ).astype(jnp.int32)
            tile = [(counted // base**digit) % base for digit in range(digits)]
            tile = jnp.concatenate(tile, axis=1).astype(BF16)
            tile = jnp.pad(tile, ((0, 0), (0, wide - digits * share)))
        tiles.append(tile)

    half_keys //= 2
    send, keep = [None] * 2, [None] * 2
    for part, found in enumerate((send, keep)):
        for stream, (start, wide) in enumerate(columns):
            found[stream], token = key_sums(
                token, rows_of[stream], samples, other_samples, tiles[stream], part * half_keys, half_keys, start, wide
            )

    tokens = [start_token] * 2
    own_turn = (2, 3, 4)

    def step_token(step, stream):
        return tokens[stream if stream == 0 and step in own_turn else 1 - stream]

    old_share = lax.dynamic_slice(old_centroids[0], (me * share, 0), (share, width))

    def bf(count, stream, tailed):
        rows_out = count * share + (tail if stream == tailed else 0)
        return jax.ShapeDtypeStruct((rows_out, columns[stream][1]), BF16)

    share_f32 = [jax.ShapeDtypeStruct((share, wide), F32) for _, wide in columns]
    held, fresh, near = [None] * 2, [None] * 2, [None] * 2
    count = blocks // 2
    for stage in range(stages - 1):
        for stream, (start, wide) in enumerate(columns):
            got = exchange(send[stream], pairing(stage, stream), groups, members)
            if stage < stages - 2:
                send[stream], keep[stream], tokens[stream] = small_call(
                    functools.partial(fold_kernel, count // 2 * share, count),
                    "fold",
                    [bf(count // 2, stream, 0)] * 2,
                    step_token(stage, stream),
                    got,
                    keep[stream],
                )
            else:
                send[stream], near[stream], tokens[stream] = small_call(
                    functools.partial(seed_kernel, share, count),
                    "seed",
                    [bf(2, stream, 0), share_f32[stream]],
                    step_token(stage, stream),
                    got,
                    keep[stream],
                    old_share[:, start : start + wide],
                )
        count //= 2
    column = jax.ShapeDtypeStruct((2 * share, 1), F32)
    for stream in streams:
        got = exchange(send[stream], pairing(stages - 1, stream), groups, members)
        if stream == 0:
            fresh[0], held[0], scale, norm, tokens[stream] = small_call(
                functools.partial(first_kernel, share, base, digits),
                "first_centroids",
                [share_f32[0], bf(2, 0, 1), column, column],
                step_token(stages - 1, stream),
                got,
                send[0],
                near[0],
            )
        else:
            fresh[1], held[1], tokens[stream] = small_call(
                functools.partial(last_kernel, share, tail),
                "last_centroids",
                [jax.ShapeDtypeStruct((share, width), F32), bf(2, 1, 1)],
                step_token(stages - 1, stream),
                got,
                send[1],
                near[1],
                scale,
                norm,
                fresh[0],
            )
    half_blocks = blocks // 2
    quarter = half_blocks // groups
    inner_of = [[dim for dim in turned[c, 0] if dim[1]] for c in range(2)]

    def part_codes(part):
        codes = []
        for flip in range(2):
            for block in range(half_blocks):
                code = []
                for c in range(2):
                    group_rel, member_rel = relative_of(part * half_blocks + block, turned[c, 0])
                    spot = block_position(0, member_rel, inner_of[c], outer_bits) % quarter
                    code.append((spot + flip * quarter) * groups + (z ^ group_rel))
                codes.append(jnp.where(core ^ flip == 0, *code))
        return jnp.stack(codes).astype(jnp.int32)

    gid = jnp.where(live, coarse_label[:, 0], -1)[None, :]
    count = 2
    arrived = [None] * 2
    for stage in reversed(range(stages - 1)):
        for stream in streams:
            got = exchange(held[stream], pairing(stage, stream), groups, members)
            if stage:
                held[stream], tokens[stream] = small_call(
                    functools.partial(join_kernel, count * share, count),
                    "join",
                    [bf(2 * count, stream, 1)],
                    step_token(2 * stages - 2 - stage, stream),
                    got,
                    held[stream],
                )
            else:
                arrived[stream] = got
            if (stage, stream) == (1, 0):
                total, tokens[0] = part_scores(
                    tokens[0], samples, gid, part_codes(1), [held[0], sibling(held[0])], None, groups, keys, share, 0
                )
        count *= 2

    def codes_of(stream, part, flip):
        codes = []
        for block in range(half_blocks):
            rel = [relative_of(part * half_blocks + block, turned[c, stream]) for c in range(2)]
            holder = core ^ flip
            group_rel = jnp.where(holder == 0, rel[0][0], rel[1][0])
            member_rel = jnp.where(holder == 0, rel[0][1], rel[1][1])
            codes.append((z ^ group_rel) * members + (me ^ flip ^ member_rel))
        return jnp.stack(codes).astype(jnp.int32)

    total, token = part_scores(
        tokens[1], samples, gid, part_codes(0), [arrived[0], sibling(arrived[0])], total, groups, keys, share, 0
    )
    last = behind(arrived[1], token)
    every = jnp.arange(members, dtype=jnp.int32)
    flip_of = (every ^ me) & 1
    spot = jnp.where(
        (core ^ flip_of) == 0,
        *(block_position(0, every ^ me, inner_of[c], outer_bits) for c in range(2)),
    )
    slots = jnp.where(spot >= quarter, spot - quarter, spot + 2 * quarter) + flip_of * quarter
    flat = [piece for got in (last, held[1]) for piece in (got, sibling(got))]
    codes = jnp.concatenate([codes_of(1, part, flip) for part in range(2) for flip in range(2)])
    half = jnp.zeros((TILE, keys), F32)
    if share < 128:
        norm_rows = []
        for piece in flat:
            norm_rows.append(piece[half_blocks * share + tail - half_blocks :].astype(F32))
        norm_rows = jnp.concatenate(norm_rows)
        spread = (codes[None, :] == jnp.arange(groups * members, dtype=jnp.int32)[:, None]).astype(F32)
        for term in range(PARTS):
            found = jnp.dot(
                spread, norm_rows[:, term * share : (term + 1) * share], precision=lax.Precision.HIGHEST
            )
            half = half.at[term * groups : (term + 1) * groups].set(found.reshape(groups, keys))
        lane = jnp.arange(keys, dtype=jnp.int32)
        source = jnp.repeat(slots, share) * share + lane % share
        move = (lane[:, None] == source[None, :]).astype(F32)
        total = jnp.dot(total, move.astype(BF16))
        slots = jnp.arange(keys // 128, dtype=jnp.int32)
    scores = final_scores(samples, gid, codes, slots, flat, total, half, groups, keys, share, columns[1][0])
    return scores, fresh[1][None]


def solution(mesh):
    return jax.shard_map(
        per_device,
        mesh=mesh,
        in_specs=(
            P(AXES, None),
            P(AXES, None),
            P(AXES),
            P(AXES),
            P("coarse", None, None),
        ),
        out_specs=(P(AXES, None), P("coarse", "member", None)),
        check_vma=False,
    )
```
